32 devices in a mesh: groups: 2 (over x), expert: 16 (over z, y, core).
Axes of the slice: x: 2, y: 2, z: 4, core: 2. Of those that a mesh axis runs over, the one named last changes fastest.
Arguments:
- tokens: bfloat16 [2048, 4096], P(('groups', 'expert')), parts along dimension 0, may hold values from -6 to 6
- routes: int32 [2048, 8], P(('groups', 'expert')), parts along dimension 0, may hold values from 0 to 15, all different within a row; in each aligned block of 64 rows (0 to 63, 64 to 127, ...) at most 64 rows name the same one
- gate_num: int32 [2048, 8], P(('groups', 'expert')), parts along dimension 0, may hold values from 1 to 32767
- gate_up_q: bfloat16 [16, 4096, 1536], P('expert'), may hold values from -127 to 127
- gate_up_scale: float32 [16, 1536], P('expert'), may hold values from 5e-05 to 0.0005
- down_q: bfloat16 [16, 768, 4096], P('expert'), may hold values from -127 to 127
- down_scale: float32 [16, 4096], P('expert'), may hold values from 0.0003 to 0.003
Outputs:
- mixed: bfloat16 [2048, 4096], P(('groups', 'expert')), parts along dimension 0
The draws below stay inside these ranges and needn't reach their ends.
There are 2 independent parts, one for each index of `groups`. The reference program is written for one: setup_inputs(seed, part) draws one part's arguments, and reference() takes and returns one part's arrays. A program takes and returns all parts, laid end to end along the dimension named above; an argument that names none is the same for every part. Nothing has to cross between parts.
Inputs may be any that keep to these rules, and one draw needn't show every extreme that they name: `routes`: each row names 8 different experts; among the 64 rows of one device no expert is named more than 64 times, a bound that some block reaches.
All inputs are finite; a program needn't handle non-finite values.
Results may differ from the reference program's by a relative error of at most 0.0057.
Values may be sent and summed in bfloat16 or wider, within the bound.
No kernel may reach another device: no remote copies, remote signals or barrier semaphores. Data moves between devices by JAX's collectives and lax.ppermute only.
A program may use at most 128 MiB of HBM per device.

```python
import math
import jax
import jax.numpy as jnp
import numpy as np
from jax import lax

D = 4096
FF = 768
TOP = 8
TOK_DEV = 64
EXPERTS = 16
TOKENS = 1024
CAP = 64
N_EXPERT = 16


def draw_gate_up_q(key, part):
    key = jax.random.fold_in(key, 11)
    values = jax.random.randint(key, (EXPERTS, D, 2 * FF), -127, 128, dtype=jnp.int32)
    return values.astype(jnp.float32).astype(jnp.bfloat16)


def draw_down_q(key, part):
    key = jax.random.fold_in(key, 23)
    values = jax.random.randint(key, (EXPERTS, FF, D), -127, 128, dtype=jnp.int32)
    return values.astype(jnp.float32).astype(jnp.bfloat16)


def touch_ends(entries, own_key, least, top_value):
    longest = entries.shape.index(max(entries.shape))
    spots = []
    for shift in (0, 1):
        where = [jax.random.randint(jax.random.fold_in(own_key, axis), (), 0, length) for axis, length in enumerate(entries.shape)]
        where[longest] = (where[longest] + shift) % entries.shape[longest]
        spots.append(tuple(where))
    return entries.at[spots[0]].set(least).at[spots[1]].set(top_value)


def block_levels(rng, extent, cuts, least, largest):
    loudness, own = 1.0, jax.random.fold_in(rng, 6)
    for axis_at, parts in cuts:
        steps = jnp.exp(jax.random.uniform(jax.random.fold_in(own, axis_at), (parts,), jnp.float32, least / len(cuts), largest / len(cuts)))
        loudness = loudness * jnp.repeat(steps, extent[axis_at] // parts).reshape([-1 if axis == axis_at else 1 for axis in range(len(extent))])
    return loudness


def routed_block(stream_key, own, number, rows, number_of, top, limit, slope):
    order = jax.random.permutation(stream_key, number_of)
    crowded, ordinary = load_shares(number_of, rows * top, limit, slope, True), load_shares(number_of, rows * top, limit, slope, False)
    places = jnp.arange(number_of)

    def named(lengths, offset_by):
        used = int((lengths > 0).sum())
        fixed = max(1, used // 4)
        passed = fixed + (places - fixed + offset_by * (used - fixed)) % max(1, number_of - fixed)
        return jnp.zeros((number_of,), jnp.int32).at[order[jnp.where(places < fixed, places, passed)]].set(jnp.asarray(lengths, jnp.int32))

    lengths = jnp.where(number % 4 == 0, named(crowded, number // 4), named(ordinary, number - number // 4 - 1))
    mixed = jax.random.permutation(jax.random.fold_in(own, 3), number_of)
    donor, taker = mixed[0:number_of // 2 * 2:2], mixed[1:number_of // 2 * 2:2]
    slack = jnp.minimum(lengths[donor] - 1, limit - lengths[taker]) // 2
    slack = jnp.where((donor == order[0]) | (taker == order[0]) | (lengths[taker] == 0), 0, jnp.maximum(slack, 0))
    passed = jax.random.randint(jax.random.fold_in(own, 4), (number_of // 2,), 0, 1 << 20) % (slack + 1)
    lengths = lengths.at[donor].add(-passed).at[taker].add(passed)
    labels = jnp.searchsorted(jnp.cumsum(lengths), jnp.arange(rows * top), side="right").astype(jnp.int32)
    table = labels.reshape(top, rows).T
    table = table[jax.random.permutation(jax.random.fold_in(own, 1), rows)]
    offset_by = jax.random.randint(jax.random.fold_in(own, 2), (rows, 1), 0, top)
    return jnp.take_along_axis(table, (jnp.arange(top)[None, :] + offset_by) % top, axis=1)


def load_shares(count, total, reach, slope, full):
    portions = [(1 << 20) // math.isqrt(grade ** slope) + 1 for grade in range(1, count + 1)]
    largest = reach if full else min(reach, max(-(-total // count), total * portions[0] // sum(portions)))
    least = 1 if total - largest >= count - 1 else 0
    holding, spare = [largest] + [least] * (count - 1), total - largest - least * (count - 1)
    while spare > 0:
        free = [i for i in range(1, count) if holding[i] < largest] or [i for i in range(1, count) if holding[i] < reach]
        mass, budget = sum([portions[i] for i in free]), spare
        for i in free:
            extra = min(reach - holding[i], max(1, budget * portions[i] // mass), spare)
            holding[i] = holding[i] + extra
            spare = spare - extra
    return np.array(holding)


def scatter_about(stream_key, shape, width, most, cuts=(), kind=jnp.bfloat16):
    drawn = jax.random.normal(stream_key, shape, jnp.float32) * width
    if len(cuts) > 0:
        drawn = block_levels(stream_key, shape, cuts, -0.22, 0.18) * drawn
    return jnp.clip(drawn, min=-most, max=most).astype(kind)


def setup_inputs(seed: int = 0, part: int = 0) -> dict:
    arg_keys = jax.random.split(jax.random.key(seed), 8)
    part_keys = jax.random.split(jax.random.fold_in(arg_keys[7], part), 8)
    tokens = scatter_about(part_keys[0], (TOKENS, D), 1.0, 6.0, ((0, 16),))
    routes_keys = jax.random.split(jax.random.fold_in(part_keys[1], 1), TOKENS // TOK_DEV)
    routes_turns = jax.random.permutation(jax.random.fold_in(part_keys[1], 3), TOKENS // TOK_DEV)
    routes = jax.vmap(lambda own, number: routed_block(jax.random.fold_in(part_keys[1], 2), own, number, TOK_DEV, EXPERTS, TOP, CAP, 2))(routes_keys, routes_turns).reshape((TOKENS, TOP))
    gate_num = touch_ends(jax.random.randint(part_keys[2], (TOKENS, TOP), 1, 32768), jax.random.fold_in(part_keys[2], 1), 1, 32767).astype(jnp.int32)
    gate_up_q = draw_gate_up_q(jax.random.fold_in(arg_keys[7], 71), part)
    gate_up_scale = jnp.clip(jnp.exp(math.log(0.0005) - 2.3025852 * jax.random.uniform(arg_keys[4], (EXPERTS, 2 * FF), jnp.float32) ** block_levels(arg_keys[4], (EXPERTS, 2 * FF), ((0, 16),), -0.2, 0.2)), 4.999999873689376e-05, 0.0005)
    down_q = draw_down_q(jax.random.fold_in(arg_keys[7], 71), part)
    down_scale = jnp.clip(jnp.exp(math.log(0.003) - 2.3025851 * jax.random.uniform(arg_keys[6], (EXPERTS, D), jnp.float32) ** block_levels(arg_keys[6], (EXPERTS, D), ((0, 16),), -0.2, 0.2)), 0.0003, 0.003)
    return {"tokens": tokens, "routes": routes, "gate_num": gate_num, "gate_up_q": gate_up_q, "gate_up_scale": gate_up_scale, "down_q": down_q, "down_scale": down_scale}


denominator = 32768.0


def expert_ffn(inputs, gate_up_w, gate_up_s, down_w, down_s):
    gate_up = jnp.dot(inputs, gate_up_w, preferred_element_type=jnp.float32) * gate_up_s
    gate_part = gate_up[:, :FF]
    up_part = gate_up[:, FF:]
    hidden = (jax.nn.silu(gate_part) * up_part).astype(jnp.bfloat16)
    return (jnp.dot(hidden, down_w, preferred_element_type=jnp.float32) * down_s).astype(jnp.bfloat16)


def reference(tokens, routes, gate_num, gate_up_q, gate_up_scale, down_q, down_scale):
    pair_count = TOKENS * TOP
    rows_cap = N_EXPERT * CAP
    flat_routes = routes.reshape(-1).astype(jnp.int32)
    weights = gate_num.reshape(-1).astype(jnp.float32) / denominator
    positions = jnp.arange(pair_count, dtype=jnp.int32)

    def one_expert(running, expert_id):
        owned = (flat_routes == expert_id).astype(jnp.int32)
        ranked = (jnp.cumsum(owned) - 1).astype(jnp.int32)
        target = jnp.where(owned == 1, ranked, rows_cap).astype(jnp.int32)
        source = jnp.zeros((rows_cap,), jnp.int32).at[target].set(positions, mode="drop")
        filled = jnp.zeros((rows_cap,), jnp.float32).at[target].set(1.0, mode="drop")
        token_ids = (source // TOP).astype(jnp.int32)
        inputs = tokens[token_ids]
        outputs = expert_ffn(inputs, gate_up_q[expert_id], gate_up_scale[expert_id], down_q[expert_id], down_scale[expert_id])
        scaled = outputs.astype(jnp.float32) * (weights[source] * filled)[:, None]
        return running.at[token_ids].add(scaled), None

    start = jnp.zeros((TOKENS, D), jnp.float32)
    mixed, unused = lax.scan(one_expert, start, jnp.arange(EXPERTS, dtype=jnp.int32))
    return mixed.astype(jnp.bfloat16)
```

```python
import jax
import jax.numpy as jnp
from jax import lax
from jax.sharding import PartitionSpec as P

DENOMINATOR = 32768.0
LANES = 128


def pack(tokens, routes, gate_num, experts):
    ids = jnp.arange(experts, dtype=jnp.int32)
    named = routes[:, :, None] == ids[None, None, :]
    dense = jnp.sum(jnp.where(named, gate_num[:, :, None], 0), axis=1)
    high = (dense >> 8).astype(jnp.bfloat16)
    low = (dense & 255).astype(jnp.bfloat16)
    spare = -(2 * experts) % LANES
    blank = jnp.zeros((tokens.shape[0], spare), jnp.bfloat16)
    return jnp.concatenate([tokens, high, low, blank], axis=1)


def gate_of(packed, width, experts, expert):
    mine = (jnp.arange(experts, dtype=jnp.int32) == expert)[None, :]
    high = packed[:, width : width + experts].astype(jnp.float32)
    low = packed[:, width + experts : width + 2 * experts].astype(jnp.float32)
    number = jnp.sum(jnp.where(mine, high * 256.0 + low, 0.0), axis=1, keepdims=True)
    return number / DENOMINATOR


def expert_part(packed, width, experts, expert, gate_up_w, gate_up_s, down_w, down_s):
    hidden_units = down_w.shape[0]
    gate_up = jnp.dot(packed[:, :width], gate_up_w, preferred_element_type=jnp.float32) * gate_up_s
    hidden = jax.nn.silu(gate_up[:, :hidden_units]) * gate_up[:, hidden_units:]
    out = jnp.dot(hidden.astype(jnp.bfloat16), down_w, preferred_element_type=jnp.float32) * down_s
    return (out * gate_of(packed, width, experts, expert)).astype(jnp.bfloat16)


def body(tokens, routes, gate_num, gate_up_q, gate_up_scale, down_q, down_scale):
    devices = lax.axis_size("expert")
    expert = lax.axis_index("expert")
    chips = devices // 2
    rows, width = tokens.shape
    same_core = [[2 * chip + core for chip in range(chips)] for core in range(2)]
    swap = [(i, i ^ 1) for i in range(devices)]
    weights = (gate_up_q[0], gate_up_scale[0], down_q[0], down_scale[0])

    packed = pack(tokens, routes, gate_num, devices)
    ours = lax.all_gather(packed, "expert", axis=0, tiled=True, axis_index_groups=same_core)
    theirs = lax.ppermute(ours, "expert", swap)
    for_them = expert_part(theirs, width, devices, expert, *weights)
    from_them = lax.ppermute(for_them, "expert", swap)
    for_us = expert_part(ours, width, devices, expert, *weights)
    total = (for_us.astype(jnp.float32) + from_them.astype(jnp.float32)).astype(jnp.bfloat16)
    return lax.psum_scatter(
        total.reshape(chips, rows, width),
        "expert",
        scatter_dimension=0,
        axis_index_groups=same_core,
        tiled=False,
    )


def solution(mesh):
    in_specs = (
        P(("groups", "expert"), None),
        P(("groups", "expert"), None),
        P(("groups", "expert"), None),
        P("expert", None, None),
        P("expert", None),
        P("expert", None, None),
        P("expert", None),
    )
    out_specs = P(("groups", "expert"), None)
    return jax.shard_map(body, mesh=mesh, in_specs=in_specs, out_specs=out_specs, check_vma=False)
```

```python
import functools

import jax
import jax.numpy as jnp
from jax import lax
from jax.experimental import pallas as pl
from jax.experimental.pallas import tpu as pltpu
from jax.sharding import PartitionSpec as P

DENOMINATOR = 32768.0
LANES = 128
DEPTH_STEPS = 8
WIDTH_STEPS = 8


def ring_of(chips):
    if chips == 8:
        return [0, 2, 4, 6, 7, 5, 3, 1]
    return list(range(chips))


def pack(tokens, routes, gate_num, experts):
    ids = jnp.arange(experts, dtype=jnp.int32)
    named = routes[:, :, None] == ids[None, None, :]
    dense = jnp.sum(jnp.where(named, gate_num[:, :, None], 0), axis=1)
    high = (dense >> 8).astype(jnp.bfloat16)
    low = (dense & 255).astype(jnp.bfloat16)
    spare = -(2 * experts) % LANES
    blank = jnp.zeros((tokens.shape[0], spare), jnp.bfloat16)
    return jnp.concatenate([tokens, high, low, blank], axis=1)


def expert_kernel(count, *refs):
    xs, gates = refs[:count], refs[count : 2 * count]
    pick, gate_up, gate_up_s, down, down_s = refs[2 * count : 2 * count + 5]
    outs = refs[2 * count + 5 : -3]
    total, hidden, weight = refs[-3:]
    step = pl.program_id(0)
    units = down.shape[0]

    @pl.when(step < DEPTH_STEPS)
    def _():
        x = jnp.concatenate([ref[...] for ref in xs], axis=0)
        part = jnp.dot(x, gate_up[...], preferred_element_type=jnp.float32)

        @pl.when(step == 0)
        def _():
            total[...] = part

        @pl.when(step > 0)
        def _():
            total[...] += part

    @pl.when(step == DEPTH_STEPS)
    def _():
        scaled = total[...] * gate_up_s[...]
        hidden[...] = (jax.nn.silu(scaled[:, :units]) * scaled[:, units:]).astype(jnp.bfloat16)
        digits = jnp.concatenate([ref[...] for ref in gates], axis=0).astype(jnp.float32)
        number = jnp.sum(digits * pick[...], axis=1, keepdims=True)
        weight[...] = jnp.broadcast_to(number / DENOMINATOR, weight.shape)

    @pl.when(step >= DEPTH_STEPS)
    def _():
        out = jnp.dot(hidden[...], down[...], preferred_element_type=jnp.float32)
        out = (out * down_s[...] * weight[:, :1]).astype(jnp.bfloat16)
        at = 0
        for ref in outs:
            ref[...] = out[at : at + ref.shape[0]]
            at += ref.shape[0]


def expert_part(blocks, split, pick, gate_up_w, gate_up_s, down_w, down_s):
    width, units2 = gate_up_w.shape
    units = down_w.shape[0]
    sizes = [block.shape[0] for block in blocks]
    rows = sum(sizes)
    deep, wide = width // DEPTH_STEPS, width // WIDTH_STEPS
    phase1 = lambda i: jnp.minimum(i, DEPTH_STEPS - 1)
    phase2 = lambda i: jnp.maximum(i - DEPTH_STEPS, 0)
    x_specs = [pl.BlockSpec((size, deep), lambda i: (0, phase1(i))) for size in sizes]
    gate_specs = [pl.BlockSpec((size, LANES), lambda i: (0, width // LANES)) for size in sizes]
    weight_specs = [
        pl.BlockSpec((1, LANES), lambda i: (0, 0)),
        pl.BlockSpec((deep, units2), lambda i: (phase1(i), 0)),
        pl.BlockSpec((1, units2), lambda i: (0, 0)),
        pl.BlockSpec((units, wide), lambda i: (0, phase2(i))),
        pl.BlockSpec((1, wide), lambda i: (0, phase2(i))),
    ]
    out_rows = [sum(sizes[:split]), sum(sizes[split:])]
    flops = 2 * rows * width * (units2 + units)
    moved = 2 * width * (units2 + units) + 4 * rows * width
    return pl.pallas_call(
        functools.partial(expert_kernel, len(sizes)),
        grid=(DEPTH_STEPS + WIDTH_STEPS,),
        in_specs=x_specs + gate_specs + weight_specs,
        out_specs=[pl.BlockSpec((size, wide), lambda i: (0, phase2(i))) for size in out_rows],
        out_shape=[jax.ShapeDtypeStruct((size, width), jnp.bfloat16) for size in out_rows],
        scratch_shapes=[
            pltpu.VMEM((rows, units2), jnp.float32),
            pltpu.VMEM((rows, units), jnp.bfloat16),
            pltpu.VMEM((rows, LANES), jnp.float32),
        ],
        compiler_params=pltpu.CompilerParams(vmem_limit_bytes=24 << 20),
        cost_estimate=pl.CostEstimate(flops=flops, bytes_accessed=moved, transcendentals=rows * units),
        name="expert",
    )(*blocks, *blocks, pick, gate_up_w, gate_up_s, down_w, down_s)


def add(*terms):
    total = terms[0].astype(jnp.float32)
    for term in terms[1:]:
        total = total + term.astype(jnp.float32)
    return total.astype(jnp.bfloat16)


def body(tokens, routes, gate_num, gate_up_q, gate_up_scale, down_q, down_scale):
    devices = lax.axis_size("expert")
    expert = lax.axis_index("expert")
    chips = devices // 2
    reach = chips // 2
    rows, width = tokens.shape
    half = rows // 2
    ring = ring_of(chips)

    def hop(way):
        pairs = []
        for place in range(chips):
            for core in range(2):
                pairs.append((2 * ring[place] + core, 2 * ring[(place + way) % chips] + core))
        return pairs

    upward, downward = hop(1), hop(-1)
    swap = [(i, i ^ 1) for i in range(devices)]
    send = functools.partial(lax.ppermute, axis_name="expert")

    lane = jnp.arange(LANES, dtype=jnp.int32)
    pick = jnp.where(lane == expert, 256.0, jnp.where(lane == devices + expert, 1.0, 0.0))
    pick = pick.astype(jnp.float32)[None, :]
    weights = (pick, gate_up_q[0], gate_up_scale, down_q[0], down_scale)

    packed = pack(tokens, routes, gate_num, devices)
    mine, theirs = {}, {}

    def run(distance, blocks):
        others = [send(block, perm=swap) for block in blocks]
        kept, given = expert_part(blocks + others, len(blocks), *weights)
        mine[distance] = kept
        theirs[distance] = send(given, perm=swap)

    from_below, from_above = packed, packed
    run(0, [packed])
    for distance in range(1, reach):
        from_below = send(from_below, perm=upward)
        from_above = send(from_above, perm=downward)
        run(distance, [from_below, from_above])
    last_below = send(from_below[:half], perm=upward)
    last_above = send(from_above[half:], perm=downward)
    run(reach, [last_below, last_above])

    to_above = send(add(mine[reach][:half], theirs[reach][:half]), perm=upward)
    to_below = send(add(mine[reach][half:], theirs[reach][half:]), perm=downward)
    for distance in range(reach - 1, 0, -1):
        if distance == reach - 1:
            to_above = jnp.pad(to_above, ((0, half), (0, 0)))
            to_below = jnp.pad(to_below, ((half, 0), (0, 0)))
        above = add(mine[distance][rows:], theirs[distance][rows:], to_above)
        below = add(mine[distance][:rows], theirs[distance][:rows], to_below)
        to_above = send(above, perm=upward)
        to_below = send(below, perm=downward)
    return add(mine[0], theirs[0], to_above, to_below)


def solution(mesh):
    in_specs = (
        P(("groups", "expert"), None),
        P(("groups", "expert"), None),
        P(("groups", "expert"), None),
        P("expert", None, None),
        P("expert", None),
        P("expert", None, None),
        P("expert", None),
    )
    out_specs = P(("groups", "expert"), None)
    return jax.shard_map(body, mesh=mesh, in_specs=in_specs, out_specs=out_specs, check_vma=False)
```

```python
import functools

import jax
import jax.numpy as jnp
from jax import lax
from jax.experimental import pallas as pl
from jax.experimental.pallas import tpu as pltpu
from jax.sharding import PartitionSpec as P

DENOMINATOR = 32768.0
LANES = 128
UNIT_CHUNK = 256
WIDTH_CHUNK = 512


def ring_of(chips):
    if chips == 8:
        return [0, 2, 4, 6, 7, 5, 3, 1]
    return list(range(chips))


def pack(tokens, routes, gate_num, experts):
    ids = jnp.arange(experts, dtype=jnp.int32)
    named = routes[:, :, None] == ids[None, None, :]
    dense = jnp.sum(jnp.where(named, gate_num[:, :, None], 0), axis=1)
    high = (dense >> 8).astype(jnp.bfloat16)
    low = (dense & 255).astype(jnp.bfloat16)
    spare = -(2 * experts) % LANES
    blank = jnp.zeros((tokens.shape[0], spare), jnp.bfloat16)
    return jnp.concatenate([tokens, high, low, blank], axis=1)


def expert_kernel(sizes, *refs):
    count = len(sizes)
    xs = refs[:count]
    pick, gate_up_s, down_s, gate_up, down = refs[count : count + 5]
    outs = refs[count + 5 : count + 7]
    x, gate_up_here, down_here, hidden, out, x_sem, gate_up_sem, down_sem, out_sem = refs[count + 7 :]
    units, width = down.shape

    starts = [sum(sizes[:i]) for i in range(count)]
    x_copies = [
        pltpu.make_async_copy(ref, x.at[pl.ds(start, size)], x_sem.at[i])
        for i, (ref, start, size) in enumerate(zip(xs, starts, sizes))
    ]

    def gate_up_copy(chunk, side):
        columns = pl.ds(pl.multiple_of(side * units + chunk * UNIT_CHUNK, UNIT_CHUNK), UNIT_CHUNK)
        return pltpu.make_async_copy(
            gate_up.at[:, columns], gate_up_here.at[:, columns], gate_up_sem.at[chunk, side]
        )

    def down_copy(chunk):
        columns = pl.ds(pl.multiple_of(chunk * WIDTH_CHUNK, WIDTH_CHUNK), WIDTH_CHUNK)
        return pltpu.make_async_copy(down.at[:, columns], down_here.at[:, columns], down_sem.at[chunk])

    def out_copies(chunk):
        columns = pl.ds(pl.multiple_of(chunk * WIDTH_CHUNK, WIDTH_CHUNK), WIDTH_CHUNK)
        copies, start = [], 0
        for i, ref in enumerate(outs):
            size = ref.shape[0]
            copies.append(
                pltpu.make_async_copy(
                    out.at[pl.ds(start, size), columns], ref.at[:, columns], out_sem.at[chunk, i]
                )
            )
            start += size
        return copies

    for copy in x_copies:
        copy.start()
    for chunk in range(units // UNIT_CHUNK):
        gate_up_copy(chunk, 0).start()
        gate_up_copy(chunk, 1).start()
    for chunk in range(width // WIDTH_CHUNK):
        down_copy(chunk).start()
    for copy in x_copies:
        copy.wait()

    digits = x[:, width:].astype(jnp.float32)
    weight = jnp.sum(digits * pick[...], axis=1, keepdims=True) / DENOMINATOR

    def unit_step(chunk, carry):
        sides = []
        for side in range(2):
            gate_up_copy(chunk, side).wait()
            columns = pl.ds(pl.multiple_of(side * units + chunk * UNIT_CHUNK, UNIT_CHUNK), UNIT_CHUNK)
            part = jnp.dot(x[:, :width], gate_up_here[:, columns], preferred_element_type=jnp.float32)
            sides.append(part * gate_up_s[:, columns])
        here = pl.ds(pl.multiple_of(chunk * UNIT_CHUNK, UNIT_CHUNK), UNIT_CHUNK)
        hidden[:, here] = (jax.nn.silu(sides[0]) * sides[1]).astype(jnp.bfloat16)
        return carry

    lax.fori_loop(0, units // UNIT_CHUNK, unit_step, 0)

    def width_step(chunk, carry):
        down_copy(chunk).wait()
        columns = pl.ds(pl.multiple_of(chunk * WIDTH_CHUNK, WIDTH_CHUNK), WIDTH_CHUNK)
        part = jnp.dot(hidden[...], down_here[:, columns], preferred_element_type=jnp.float32)
        out[:, columns] = (part * down_s[:, columns] * weight).astype(jnp.bfloat16)
        for copy in out_copies(chunk):
            copy.start()
        return carry

    lax.fori_loop(0, width // WIDTH_CHUNK, width_step, 0)
    for chunk in range(width // WIDTH_CHUNK):
        for copy in out_copies(chunk):
            copy.wait()


def expert_part(blocks, split, pick, gate_up_w, gate_up_s, down_w, down_s):
    width, units2 = gate_up_w.shape
    units = down_w.shape[0]
    sizes = [block.shape[0] for block in blocks]
    rows, packed_width = sum(sizes), blocks[0].shape[1]
    out_rows = [sum(sizes[:split]), sum(sizes[split:])]
    anywhere, vmem = pl.BlockSpec(memory_space=pl.ANY), pl.BlockSpec(memory_space=pltpu.VMEM)
    flops = 2 * rows * width * (units2 + units)
    moved = 2 * width * (units2 + units) + 4 * rows * width
    return pl.pallas_call(
        functools.partial(expert_kernel, sizes),
        in_specs=[anywhere] * len(blocks) + [vmem] * 3 + [anywhere] * 2,
        out_specs=[anywhere] * 2,
        out_shape=[jax.ShapeDtypeStruct((size, width), jnp.bfloat16) for size in out_rows],
        scratch_shapes=[
            pltpu.VMEM((rows, packed_width), jnp.bfloat16),
            pltpu.VMEM((width, units2), jnp.bfloat16),
            pltpu.VMEM((units, width), jnp.bfloat16),
            pltpu.VMEM((rows, units), jnp.bfloat16),
            pltpu.VMEM((rows, width), jnp.bfloat16),
            pltpu.SemaphoreType.DMA((len(blocks),)),
            pltpu.SemaphoreType.DMA((units // UNIT_CHUNK, 2)),
            pltpu.SemaphoreType.DMA((width // WIDTH_CHUNK,)),
            pltpu.SemaphoreType.DMA((width // WIDTH_CHUNK, 2)),
        ],
        compiler_params=pltpu.CompilerParams(vmem_limit_bytes=52 << 20),
        cost_estimate=pl.CostEstimate(flops=flops, bytes_accessed=moved, transcendentals=rows * units),
        name="expert",
    )(*blocks, pick, gate_up_s, down_s, gate_up_w, down_w)


def add(*terms):
    total = terms[0].astype(jnp.float32)
    for term in terms[1:]:
        total = total + term.astype(jnp.float32)
    return total.astype(jnp.bfloat16)


def body(tokens, routes, gate_num, gate_up_q, gate_up_scale, down_q, down_scale):
    devices = lax.axis_size("expert")
    expert = lax.axis_index("expert")
    chips = devices // 2
    reach = chips // 2
    rows, width = tokens.shape
    half = rows // 2
    ring = ring_of(chips)

    def hop(way):
        pairs = []
        for place in range(chips):
            for core in range(2):
                pairs.append((2 * ring[place] + core, 2 * ring[(place + way) % chips] + core))
        return pairs

    upward, downward = hop(1), hop(-1)
    swap = [(i, i ^ 1) for i in range(devices)]
    send = functools.partial(lax.ppermute, axis_name="expert")

    lane = jnp.arange(LANES, dtype=jnp.int32)
    pick = jnp.where(lane == expert, 256.0, jnp.where(lane == devices + expert, 1.0, 0.0))
    pick = pick.astype(jnp.float32)[None, :]
    weights = (pick, gate_up_q[0], gate_up_scale, down_q[0], down_scale)

    packed = pack(tokens, routes, gate_num, devices)
    mine, theirs = {}, {}

    def run(distance, blocks):
        others = [send(block, perm=swap) for block in blocks]
        kept, given = expert_part(blocks + others, len(blocks), *weights)
        mine[distance] = kept
        theirs[distance] = send(given, perm=swap)

    from_below, from_above = packed, packed
    run(0, [packed])
    for distance in range(1, reach):
        from_below = send(from_below, perm=upward)
        from_above = send(from_above, perm=downward)
        run(distance, [from_below, from_above])
    last_below = send(from_below[:half], perm=upward)
    last_above = send(from_above[half:], perm=downward)
    run(reach, [last_below, last_above])

    to_above = send(add(mine[reach][:half], theirs[reach][:half]), perm=upward)
    to_below = send(add(mine[reach][half:], theirs[reach][half:]), perm=downward)
    for distance in range(reach - 1, 0, -1):
        if distance == reach - 1:
            to_above = jnp.pad(to_above, ((0, half), (0, 0)))
            to_below = jnp.pad(to_below, ((half, 0), (0, 0)))
        above = add(mine[distance][rows:], theirs[distance][rows:], to_above)
        below = add(mine[distance][:rows], theirs[distance][:rows], to_below)
        to_above = send(above, perm=upward)
        to_below = send(below, perm=downward)
    return add(mine[0], theirs[0], to_above, to_below)


def solution(mesh):
    in_specs = (
        P(("groups", "expert"), None),
        P(("groups", "expert"), None),
        P(("groups", "expert"), None),
        P("expert", None, None),
        P("expert", None),
        P("expert", None, None),
        P("expert", None),
    )
    out_specs = P(("groups", "expert"), None)
    return jax.shard_map(body, mesh=mesh, in_specs=in_specs, out_specs=out_specs, check_vma=False)
```

```python
import functools

import jax
import jax.numpy as jnp
from jax import lax
from jax.experimental import pallas as pl
from jax.experimental.pallas import tpu as pltpu
from jax.sharding import PartitionSpec as P

DENOMINATOR = 32768.0
LANES = 128
UNIT_CHUNK = 256
WIDTH_CHUNK = 512


def ring_of(chips):
    if chips == 8:
        return [0, 2, 4, 6, 7, 5, 3, 1]
    return list(range(chips))


def pack(tokens, routes, gate_num, experts):
    ids = jnp.arange(experts, dtype=jnp.int32)
    named = routes[:, :, None] == ids[None, None, :]
    dense = jnp.sum(jnp.where(named, gate_num[:, :, None], 0), axis=1)
    high = (dense >> 8).astype(jnp.bfloat16)
    low = (dense & 255).astype(jnp.bfloat16)
    spare = -(2 * experts) % LANES
    blank = jnp.zeros((tokens.shape[0], spare), jnp.bfloat16)
    return jnp.concatenate([tokens, high, low, blank], axis=1)


def keep_kernel(gate_up, down, gate_up_here, down_here, sem):
    copies = [
        pltpu.make_async_copy(gate_up, gate_up_here, sem.at[0]),
        pltpu.make_async_copy(down, down_here, sem.at[1]),
    ]
    for copy in copies:
        copy.start()
    for copy in copies:
        copy.wait()


def keep(gate_up_w, down_w):
    anywhere, vmem = pl.BlockSpec(memory_space=pl.ANY), pl.BlockSpec(memory_space=pltpu.VMEM)
    kept = pl.pallas_call(
        keep_kernel,
        in_specs=[anywhere] * 2,
        out_specs=[vmem] * 2,
        out_shape=[pltpu.VMEM(w.shape, w.dtype) for w in (gate_up_w, down_w)],
        scratch_shapes=[pltpu.SemaphoreType.DMA((2,))],
        compiler_params=pltpu.CompilerParams(vmem_limit_bytes=1 << 20),
        cost_estimate=pl.CostEstimate(
            flops=0, bytes_accessed=2 * (gate_up_w.size + down_w.size), transcendentals=0
        ),
        name="keep",
    )(*(pltpu.with_memory_space_constraint(w, pltpu.HBM) for w in (gate_up_w, down_w)))
    return kept


def expert_kernel(sizes, *refs):
    count = len(sizes)
    xs = refs[:count]
    pick, gate_up_s, down_s, gate_up, down = refs[count : count + 5]
    outs = refs[count + 5 : count + 7]
    x, hidden, out, x_sem, out_sem = refs[count + 7 :]
    units, width = down.shape

    starts = [sum(sizes[:i]) for i in range(count)]
    x_copies = [
        pltpu.make_async_copy(ref, x.at[pl.ds(start, size)], x_sem.at[i])
        for i, (ref, start, size) in enumerate(zip(xs, starts, sizes))
    ]

    def out_copies(chunk):
        columns = pl.ds(pl.multiple_of(chunk * WIDTH_CHUNK, WIDTH_CHUNK), WIDTH_CHUNK)
        copies, start = [], 0
        for i, ref in enumerate(outs):
            size = ref.shape[0]
            copies.append(
                pltpu.make_async_copy(
                    out.at[pl.ds(start, size), columns], ref.at[:, columns], out_sem.at[chunk, i]
                )
            )
            start += size
        return copies

    for copy in x_copies:
        copy.start()
    for copy in x_copies:
        copy.wait()

    digits = x[:, width:].astype(jnp.float32)
    weight = jnp.sum(digits * pick[...], axis=1, keepdims=True) / DENOMINATOR

    def unit_step(chunk, carry):
        sides = []
        for side in range(2):
            columns = pl.ds(pl.multiple_of(side * units + chunk * UNIT_CHUNK, UNIT_CHUNK), UNIT_CHUNK)
            part = jnp.dot(x[:, :width], gate_up[:, columns], preferred_element_type=jnp.float32)
            sides.append(part * gate_up_s[:, columns])
        here = pl.ds(pl.multiple_of(chunk * UNIT_CHUNK, UNIT_CHUNK), UNIT_CHUNK)
        hidden[:, here] = (jax.nn.silu(sides[0]) * sides[1]).astype(jnp.bfloat16)
        return carry

    lax.fori_loop(0, units // UNIT_CHUNK, unit_step, 0)

    def width_step(chunk, carry):
        columns = pl.ds(pl.multiple_of(chunk * WIDTH_CHUNK, WIDTH_CHUNK), WIDTH_CHUNK)
        part = jnp.dot(hidden[...], down[:, columns], preferred_element_type=jnp.float32)
        out[:, columns] = (part * down_s[:, columns] * weight).astype(jnp.bfloat16)
        for copy in out_copies(chunk):
            copy.start()
        return carry

    lax.fori_loop(0, width // WIDTH_CHUNK, width_step, 0)
    for chunk in range(width // WIDTH_CHUNK):
        for copy in out_copies(chunk):
            copy.wait()


def expert_part(blocks, split, pick, gate_up_w, gate_up_s, down_w, down_s):
    width, units2 = gate_up_w.shape
    units = down_w.shape[0]
    sizes = [block.shape[0] for block in blocks]
    rows, packed_width = sum(sizes), blocks[0].shape[1]
    out_rows = [sum(sizes[:split]), sum(sizes[split:])]
    anywhere, vmem = pl.BlockSpec(memory_space=pl.ANY), pl.BlockSpec(memory_space=pltpu.VMEM)
    flops = 2 * rows * width * (units2 + units)
    return pl.pallas_call(
        functools.partial(expert_kernel, sizes),
        in_specs=[anywhere] * len(blocks) + [vmem] * 5,
        out_specs=[anywhere] * 2,
        out_shape=[jax.ShapeDtypeStruct((size, width), jnp.bfloat16) for size in out_rows],
        scratch_shapes=[
            pltpu.VMEM((rows, packed_width), jnp.bfloat16),
            pltpu.VMEM((rows, units), jnp.bfloat16),
            pltpu.VMEM((rows, width), jnp.bfloat16),
            pltpu.SemaphoreType.DMA((len(blocks),)),
            pltpu.SemaphoreType.DMA((width // WIDTH_CHUNK, 2)),
        ],
        compiler_params=pltpu.CompilerParams(vmem_limit_bytes=16 << 20),
        cost_estimate=pl.CostEstimate(
            flops=2 * flops, bytes_accessed=4 * rows * width, transcendentals=rows * units
        ),
        name="expert",
    )(
        *blocks,
        pick,
        gate_up_s,
        down_s,
        pltpu.with_memory_space_constraint(gate_up_w, pltpu.VMEM),
        pltpu.with_memory_space_constraint(down_w, pltpu.VMEM),
    )


def add(*terms):
    total = terms[0].astype(jnp.float32)
    for term in terms[1:]:
        total = total + term.astype(jnp.float32)
    return total.astype(jnp.bfloat16)


def after(value, *others):
    return lax.optimization_barrier((value, *others))[0]


def body(tokens, routes, gate_num, gate_up_q, gate_up_scale, down_q, down_scale):
    devices = lax.axis_size("expert")
    expert = lax.axis_index("expert")
    chips = devices // 2
    reach = chips // 2
    rows, width = tokens.shape
    half = rows // 2
    ring = ring_of(chips)

    def hop(way):
        pairs = []
        for place in range(chips):
            for core in range(2):
                pairs.append((2 * ring[place] + core, 2 * ring[(place + way) % chips] + core))
        return pairs

    upward, downward = hop(1), hop(-1)
    swap = [(i, i ^ 1) for i in range(devices)]
    send = functools.partial(lax.ppermute, axis_name="expert")

    lane = jnp.arange(LANES, dtype=jnp.int32)
    pick = jnp.where(lane == expert, 256.0, jnp.where(lane == devices + expert, 1.0, 0.0))
    pick = pick.astype(jnp.float32)[None, :]
    gate_up_w, down_w = keep(gate_up_q[0], down_q[0])
    weights = (pick, gate_up_w, gate_up_scale, down_w, down_scale)

    packed = pack(tokens, routes, gate_num, devices)
    mine, theirs = {}, {}

    def run(distance, blocks):
        others = [send(block, perm=swap) for block in blocks]
        kept, given = expert_part(blocks + others, len(blocks), *weights)
        mine[distance] = kept
        theirs[distance] = send(given, perm=swap)

    from_below, from_above = packed, packed
    run(0, [packed])
    for distance in range(1, reach):
        if distance > 1:
            from_below = after(from_below, mine[distance - 2])
            from_above = after(from_above, mine[distance - 2])
        from_below = send(from_below, perm=upward)
        from_above = send(from_above, perm=downward)
        run(distance, [from_below, from_above])
    from_below = after(from_below, mine[reach - 2])
    from_above = after(from_above, mine[reach - 2])
    last_below = send(from_below[:half], perm=upward)
    last_above = send(from_above[half:], perm=downward)
    last_below = after(last_below, mine[reach - 1])
    last_above = after(last_above, mine[reach - 1])
    run(reach, [last_below, last_above])

    to_above = send(add(mine[reach][:half], theirs[reach][:half]), perm=upward)
    to_below = send(add(mine[reach][half:], theirs[reach][half:]), perm=downward)
    for distance in range(reach - 1, 0, -1):
        if distance == reach - 1:
            to_above = jnp.pad(to_above, ((0, half), (0, 0)))
            to_below = jnp.pad(to_below, ((half, 0), (0, 0)))
        above = add(mine[distance][rows:], theirs[distance][rows:], to_above)
        below = add(mine[distance][:rows], theirs[distance][:rows], to_below)
        to_above = send(above, perm=upward)
        to_below = send(below, perm=downward)
    return add(mine[0], theirs[0], to_above, to_below)


def solution(mesh):
    in_specs = (
        P(("groups", "expert"), None),
        P(("groups", "expert"), None),
        P(("groups", "expert"), None),
        P("expert", None, None),
        P("expert", None),
        P("expert", None, None),
        P("expert", None),
    )
    out_specs = P(("groups", "expert"), None)
    return jax.shard_map(body, mesh=mesh, in_specs=in_specs, out_specs=out_specs, check_vma=False)
```

```python
import functools

import jax
import jax.numpy as jnp
from jax import lax
from jax.experimental import pallas as pl
from jax.experimental.pallas import tpu as pltpu
from jax.sharding import PartitionSpec as P

DENOMINATOR = 32768.0
LANES = 128
UNIT_CHUNK = 256
WIDTH_CHUNK = 512


def ring_of(chips):
    if chips == 8:
        return [0, 2, 4, 6, 7, 5, 3, 1]
    return list(range(chips))


def pack(tokens, routes, gate_num, experts):
    ids = jnp.arange(experts, dtype=jnp.int32)
    named = routes[:, :, None] == ids[None, None, :]
    dense = jnp.sum(jnp.where(named, gate_num[:, :, None], 0), axis=1)
    high = (dense >> 8).astype(jnp.bfloat16)
    low = (dense & 255).astype(jnp.bfloat16)
    spare = -(2 * experts) % LANES
    blank = jnp.zeros((tokens.shape[0], spare), jnp.bfloat16)
    return jnp.concatenate([tokens, high, low, blank], axis=1)


def keep_kernel(gate_up, down, gate_up_here, down_here, sem):
    copies = [
        pltpu.make_async_copy(gate_up, gate_up_here, sem.at[0]),
        pltpu.make_async_copy(down, down_here, sem.at[1]),
    ]
    for copy in copies:
        copy.start()
    for copy in copies:
        copy.wait()


def keep(gate_up_w, down_w):
    anywhere, vmem = pl.BlockSpec(memory_space=pl.ANY), pl.BlockSpec(memory_space=pltpu.VMEM)
    kept = pl.pallas_call(
        keep_kernel,
        in_specs=[anywhere] * 2,
        out_specs=[vmem] * 2,
        out_shape=[pltpu.VMEM(w.shape, w.dtype) for w in (gate_up_w, down_w)],
        scratch_shapes=[pltpu.SemaphoreType.DMA((2,))],
        compiler_params=pltpu.CompilerParams(vmem_limit_bytes=1 << 20),
        cost_estimate=pl.CostEstimate(
            flops=0, bytes_accessed=2 * (gate_up_w.size + down_w.size), transcendentals=0
        ),
        name="keep",
    )(*(pltpu.with_memory_space_constraint(w, pltpu.HBM) for w in (gate_up_w, down_w)))
    return kept


def expert_kernel(sizes, *refs):
    count = len(sizes)
    xs = refs[:count]
    pick, gate_up_s, down_s, gate_up, down = refs[count : count + 5]
    outs = refs[count + 5 : -5]
    x, hidden, out, x_sem, out_sem = refs[-5:]
    units, width = down.shape

    starts = [sum(sizes[:i]) for i in range(count)]
    x_copies = [
        pltpu.make_async_copy(ref, x.at[pl.ds(start, size)], x_sem.at[i])
        for i, (ref, start, size) in enumerate(zip(xs, starts, sizes))
    ]

    def out_copies(chunk):
        columns = pl.ds(pl.multiple_of(chunk * WIDTH_CHUNK, WIDTH_CHUNK), WIDTH_CHUNK)
        copies, start = [], 0
        for i, ref in enumerate(outs):
            size = ref.shape[0]
            copies.append(
                pltpu.make_async_copy(
                    out.at[pl.ds(start, size), columns], ref.at[:, columns], out_sem.at[chunk, i]
                )
            )
            start += size
        return copies

    for copy in x_copies:
        copy.start()
    for copy in x_copies:
        copy.wait()

    digits = x[:, width:].astype(jnp.float32)
    weight = jnp.sum(digits * pick[...], axis=1, keepdims=True) / DENOMINATOR

    def unit_step(chunk, carry):
        sides = []
        for side in range(2):
            columns = pl.ds(pl.multiple_of(side * units + chunk * UNIT_CHUNK, UNIT_CHUNK), UNIT_CHUNK)
            part = jnp.dot(x[:, :width], gate_up[:, columns], preferred_element_type=jnp.float32)
            sides.append(part * gate_up_s[:, columns])
        here = pl.ds(pl.multiple_of(chunk * UNIT_CHUNK, UNIT_CHUNK), UNIT_CHUNK)
        hidden[:, here] = (jax.nn.silu(sides[0]) * sides[1]).astype(jnp.bfloat16)
        return carry

    lax.fori_loop(0, units // UNIT_CHUNK, unit_step, 0)

    def width_step(chunk, carry):
        columns = pl.ds(pl.multiple_of(chunk * WIDTH_CHUNK, WIDTH_CHUNK), WIDTH_CHUNK)
        part = jnp.dot(hidden[...], down[:, columns], preferred_element_type=jnp.float32)
        out[:, columns] = (part * down_s[:, columns] * weight).astype(jnp.bfloat16)
        for copy in out_copies(chunk):
            copy.start()
        return carry

    lax.fori_loop(0, width // WIDTH_CHUNK, width_step, 0)
    for chunk in range(width // WIDTH_CHUNK):
        for copy in out_copies(chunk):
            copy.wait()


def expert_part(blocks, out_rows, hint, pick, gate_up_w, gate_up_s, down_w, down_s):
    width, units2 = gate_up_w.shape
    units = down_w.shape[0]
    sizes = [block.shape[0] for block in blocks]
    rows, packed_width = sum(sizes), blocks[0].shape[1]
    anywhere, vmem = pl.BlockSpec(memory_space=pl.ANY), pl.BlockSpec(memory_space=pltpu.VMEM)
    flops = int(hint * 2 * rows * width * (units2 + units))
    return pl.pallas_call(
        functools.partial(expert_kernel, sizes),
        in_specs=[anywhere] * len(blocks) + [vmem] * 5,
        out_specs=[anywhere] * len(out_rows),
        out_shape=[jax.ShapeDtypeStruct((size, width), jnp.bfloat16) for size in out_rows],
        scratch_shapes=[
            pltpu.VMEM((rows, packed_width), jnp.bfloat16),
            pltpu.VMEM((rows, units), jnp.bfloat16),
            pltpu.VMEM((rows, width), jnp.bfloat16),
            pltpu.SemaphoreType.DMA((len(blocks),)),
            pltpu.SemaphoreType.DMA((width // WIDTH_CHUNK, len(out_rows))),
        ],
        compiler_params=pltpu.CompilerParams(vmem_limit_bytes=16 << 20),
        cost_estimate=pl.CostEstimate(
            flops=flops, bytes_accessed=int(hint * 4 * rows * width), transcendentals=0
        ),
        name="expert",
    )(
        *blocks,
        pick,
        gate_up_s,
        down_s,
        pltpu.with_memory_space_constraint(gate_up_w, pltpu.VMEM),
        pltpu.with_memory_space_constraint(down_w, pltpu.VMEM),
    )


def add(*terms):
    total = terms[0].astype(jnp.float32)
    for term in terms[1:]:
        total = total + term.astype(jnp.float32)
    return total.astype(jnp.bfloat16)


def together(*values):
    return lax.optimization_barrier(values)


def after(value, *others):
    return together(value, *others)[0]


def body(tokens, routes, gate_num, gate_up_q, gate_up_scale, down_q, down_scale):
    devices = lax.axis_size("expert")
    expert = lax.axis_index("expert")
    chips = devices // 2
    reach = chips // 2
    rows, width = tokens.shape
    half = rows // 2
    ring = ring_of(chips)

    def hop(way):
        pairs = []
        for place in range(chips):
            for core in range(2):
                pairs.append((2 * ring[place] + core, 2 * ring[(place + way) % chips] + core))
        return pairs

    upward, downward = hop(1), hop(-1)
    swap = [(i, i ^ 1) for i in range(devices)]
    send = functools.partial(lax.ppermute, axis_name="expert")

    lane = jnp.arange(LANES, dtype=jnp.int32)
    pick = jnp.where(lane == expert, 256.0, jnp.where(lane == devices + expert, 1.0, 0.0))
    pick = pick.astype(jnp.float32)[None, :]
    gate_up_w, down_w = keep(gate_up_q[0], down_q[0])
    weights = (pick, gate_up_w, gate_up_scale, down_w, down_scale)

    packed = pack(tokens, routes, gate_num, devices)
    mine, theirs = {}, {}

    def run(distance, blocks, cuts=()):
        others = [send(after(block, *mine.get(distance - 1, ())), perm=swap) for block in blocks]
        count = sum(block.shape[0] for block in blocks)
        kept, *given = expert_part(blocks + others, (count, *(cuts or (count,))), 2, *weights)
        mine[distance] = (kept,)
        theirs[distance] = [send(piece, perm=swap) for piece in given]

    from_below, from_above = packed, packed
    run(0, [packed])
    for distance in range(1, reach):
        if distance > 1:
            from_below = after(from_below, *mine[distance - 2])
            from_above = after(from_above, *mine[distance - 2])
        from_below = send(from_below, perm=upward)
        from_above = send(from_above, perm=downward)
        run(distance, [from_below, from_above], (half, rows, half) if distance == reach - 1 else ())
    from_below = after(from_below, *mine[reach - 2])
    from_above = after(from_above, *mine[reach - 2])
    last_below = send(from_below[:half], perm=upward)
    last_above = send(from_above[half:], perm=downward)

    def part(distance, start):
        found = []
        for arrays in (mine[distance], theirs[distance]):
            at = start
            for array in arrays:
                if 0 <= at < array.shape[0]:
                    found.append(array[at : at + half])
                at -= array.shape[0]
        return found

    def forward(distance, is_long, carried):
        up_start = rows + (0 if is_long else half)
        down_start = half if is_long else 0
        up = add(*part(distance, 0 if distance == reach else up_start), *carried[:1])
        down = add(*part(distance, down_start), *carried[1:])
        return (up, down), (send(up, perm=upward), send(down, perm=downward))

    sent, short = forward(reach - 1, False, ())
    run(reach, [last_below, last_above])
    sent, long = forward(reach, True, ())
    for distance in range(reach - 2, -1, -1):
        if distance > 0:
            sent, short = forward(distance, False, together(*short, *sent)[:2])
        sent, long = forward(distance + 1, True, together(*long, *sent)[:2])
    top = add(*part(0, 0), long[0], short[1])
    bottom = add(*part(0, half), short[0], long[1])
    return jnp.concatenate([top, bottom], axis=0)


def solution(mesh):
    in_specs = (
        P(("groups", "expert"), None),
        P(("groups", "expert"), None),
        P(("groups", "expert"), None),
        P("expert", None, None),
        P("expert", None),
        P("expert", None, None),
        P("expert", None),
    )
    out_specs = P(("groups", "expert"), None)
    return jax.shard_map(body, mesh=mesh, in_specs=in_specs, out_specs=out_specs, check_vma=False)
```

```python
import functools

import jax
import jax.numpy as jnp
from jax import lax
from jax.experimental import pallas as pl
from jax.experimental.pallas import tpu as pltpu
from jax.sharding import PartitionSpec as P

DENOMINATOR = 32768.0
LANES = 128
UNIT_CHUNK = 256
WIDTH_CHUNK = 1024
ANYWHERE = pl.BlockSpec(memory_space=pl.ANY)
VMEM = pl.BlockSpec(memory_space=pltpu.VMEM)
SMEM = pl.BlockSpec(memory_space=pltpu.SMEM)


def ring_of(chips):
    if chips == 8:
        return [0, 2, 4, 6, 7, 5, 3, 1]
    return list(range(chips))


def limits(mebibytes):
    return pltpu.CompilerParams(vmem_limit_bytes=mebibytes << 20)


def pack_kernel(experts, core, tokens, routes, gate_num, first, second, digits):
    rows, width = tokens.shape
    half = rows // 2
    lane = lax.broadcasted_iota(jnp.int32, (rows, LANES), 1)
    expert = jnp.where(lane < experts, lane, lane - experts)
    dense = jnp.zeros((rows, LANES), jnp.int32)
    for pick in range(routes.shape[1]):
        column = slice(pick, pick + 1)
        dense += jnp.where(routes[:, column] == expert, gate_num[:, column], 0)
    digit = jnp.where(lane < experts, dense >> 8, dense & 255)
    digit = jnp.where(lane < 2 * experts, digit, 0)
    digits[...] = digit.astype(jnp.float32).astype(jnp.bfloat16)
    for packed, place in ((first, core[0]), (second, 1 - core[0])):
        here = pl.ds(pl.multiple_of(place * half, half), half)
        packed[:, :width] = tokens[here]
        packed[:, width:] = digits[here]


def pack(core, tokens, routes, gate_num, experts):
    rows, width = tokens.shape
    return pl.pallas_call(
        functools.partial(pack_kernel, experts),
        in_specs=[SMEM] + [VMEM] * 3,
        out_specs=[VMEM] * 2,
        out_shape=[jax.ShapeDtypeStruct((rows // 2, width + LANES), jnp.bfloat16)] * 2,
        scratch_shapes=[pltpu.VMEM((rows, LANES), jnp.bfloat16)],
        compiler_params=limits(4),
        name="pack",
    )(core, tokens, routes, gate_num)


def keep_kernel(gate_up, down, gate_up_here, down_here, sem):
    copies = [
        pltpu.make_async_copy(gate_up, gate_up_here, sem.at[0]),
        pltpu.make_async_copy(down, down_here, sem.at[1]),
    ]
    for copy in copies:
        copy.start()
    for copy in copies:
        copy.wait()


def keep(gate_up_w, down_w):
    return pl.pallas_call(
        keep_kernel,
        in_specs=[ANYWHERE] * 2,
        out_specs=[VMEM] * 2,
        out_shape=[pltpu.VMEM(w.shape, w.dtype) for w in (gate_up_w, down_w)],
        scratch_shapes=[pltpu.SemaphoreType.DMA((2,))],
        compiler_params=limits(1),
        cost_estimate=pl.CostEstimate(
            flops=0, bytes_accessed=2 * (gate_up_w.size + down_w.size), transcendentals=0
        ),
        name="keep",
    )(*(pltpu.with_memory_space_constraint(w, pltpu.HBM) for w in (gate_up_w, down_w)))


def expert_kernel(count, *refs):
    xs = refs[:count]
    pick, gate_up_s, down_s, gate_up, down = refs[count : count + 5]
    outs = refs[count + 5 : -2]
    x, hidden = refs[-2:]
    units, width = down.shape

    at = 0
    for ref in xs:
        x[at : at + ref.shape[0]] = ref[...]
        at += ref.shape[0]
    digits = x[:, width:].astype(jnp.float32)
    weight = jnp.sum(digits * pick[...], axis=1, keepdims=True) / DENOMINATOR

    def unit_step(chunk, carry):
        sides = []
        for side in range(2):
            columns = pl.ds(pl.multiple_of(side * units + chunk * UNIT_CHUNK, UNIT_CHUNK), UNIT_CHUNK)
            part = jnp.dot(x[:, :width], gate_up[:, columns], preferred_element_type=jnp.float32)
            sides.append(part * gate_up_s[:, columns])
        here = pl.ds(pl.multiple_of(chunk * UNIT_CHUNK, UNIT_CHUNK), UNIT_CHUNK)
        hidden[:, here] = (jax.nn.silu(sides[0]) * sides[1]).astype(jnp.bfloat16)
        return carry

    lax.fori_loop(0, units // UNIT_CHUNK, unit_step, 0)

    def width_step(chunk, carry):
        columns = pl.ds(pl.multiple_of(chunk * WIDTH_CHUNK, WIDTH_CHUNK), WIDTH_CHUNK)
        part = jnp.dot(hidden[...], down[:, columns], preferred_element_type=jnp.float32)
        part = (part * down_s[:, columns] * weight).astype(jnp.bfloat16)
        at = 0
        for ref in outs:
            ref[:, columns] = part[at : at + ref.shape[0]]
            at += ref.shape[0]
        return carry

    lax.fori_loop(0, width // WIDTH_CHUNK, width_step, 0)


def expert_part(blocks, out_rows, hint, pick, gate_up_w, gate_up_s, down_w, down_s):
    width, units2 = gate_up_w.shape
    units = down_w.shape[0]
    rows, packed_width = sum(block.shape[0] for block in blocks), blocks[0].shape[1]
    flops = int(hint * 2 * rows * width * (units2 + units))
    return pl.pallas_call(
        functools.partial(expert_kernel, len(blocks)),
        in_specs=[VMEM] * (len(blocks) + 5),
        out_specs=[VMEM] * len(out_rows),
        out_shape=[jax.ShapeDtypeStruct((size, width), jnp.bfloat16) for size in out_rows],
        scratch_shapes=[
            pltpu.VMEM((rows, packed_width), jnp.bfloat16),
            pltpu.VMEM((rows, units), jnp.bfloat16),
        ],
        compiler_params=limits(14),
        cost_estimate=pl.CostEstimate(flops=flops, bytes_accessed=0, transcendentals=0),
        name="expert",
    )(
        *blocks,
        pick,
        gate_up_s,
        down_s,
        pltpu.with_memory_space_constraint(gate_up_w, pltpu.VMEM),
        pltpu.with_memory_space_constraint(down_w, pltpu.VMEM),
    )


def step_kernel(starts, rows, *refs):
    *terms, out = refs
    for column in range(0, out.shape[1], WIDTH_CHUNK):
        columns = slice(column, column + WIDTH_CHUNK)
        total = 0.0
        for ref, start in zip(terms, starts):
            total += ref[start : start + rows, columns].astype(jnp.float32)
        out[:, columns] = total.astype(jnp.bfloat16)


def step_sum(terms, rows):
    arrays, starts = zip(*terms)
    return pl.pallas_call(
        functools.partial(step_kernel, starts, rows),
        in_specs=[VMEM] * len(arrays),
        out_specs=VMEM,
        out_shape=jax.ShapeDtypeStruct((rows, arrays[0].shape[1]), jnp.bfloat16),
        compiler_params=limits(4),
        name="step_sum",
    )(*arrays)


def last_kernel(core, mine, theirs, *refs):
    *arrived, out = refs
    half = out.shape[0] // 2
    for which, place in ((0, core[0]), (1, 1 - core[0])):
        there = pl.ds(pl.multiple_of(place * half, half), half)
        here = slice(which * half, (which + 1) * half)
        for column in range(0, out.shape[1], WIDTH_CHUNK):
            columns = slice(column, column + WIDTH_CHUNK)
            total = mine[here, columns].astype(jnp.float32) + theirs[here, columns].astype(jnp.float32)
            for ref in arrived[2 * which : 2 * which + 2]:
                total += ref[:, columns].astype(jnp.float32)
            out[there, columns] = total.astype(jnp.bfloat16)


def last_sum(core, mine, theirs, *arrived):
    return pl.pallas_call(
        last_kernel,
        in_specs=[SMEM] + [VMEM] * (2 + len(arrived)),
        out_specs=VMEM,
        out_shape=jax.ShapeDtypeStruct(mine.shape, jnp.bfloat16),
        compiler_params=limits(4),
        name="last_sum",
    )(core, mine, theirs, *arrived)


def together(*values):
    return lax.optimization_barrier(values)


def after(value, *others):
    return together(value, *others)[0] if others else value


def body(tokens, routes, gate_num, gate_up_q, gate_up_scale, down_q, down_scale):
    devices = lax.axis_size("expert")
    expert = lax.axis_index("expert")
    chips = devices // 2
    reach = chips // 2
    rows, width = tokens.shape
    half = rows // 2
    ring = ring_of(chips)

    def hop(shift, cross):
        pairs = []
        for place in range(chips):
            for core, way in ((0, shift), (1, -shift)):
                to = ring[(place + way) % chips]
                pairs.append((2 * ring[place] + core, 2 * to + (core ^ cross)))
        return pairs

    on, to_other, back_to_other = hop(1, 0), hop(-1, 1), hop(1, 1)
    swap = [(i, i ^ 1) for i in range(devices)]
    send = functools.partial(lax.ppermute, axis_name="expert")

    lane = jnp.arange(LANES, dtype=jnp.int32)
    pick = jnp.where(lane == expert, 256.0, jnp.where(lane == devices + expert, 1.0, 0.0))
    pick = pick.astype(jnp.float32)[None, :]
    core = (expert & 1).astype(jnp.int32)[None]
    gate_up_w, down_w = keep(gate_up_q[0], down_q[0])
    weights = (pick, gate_up_w, gate_up_scale, down_w, down_scale)

    kept, given = {}, {}

    def run(distance, blocks, hint):
        tie = kept.get(distance - 1)
        others = [send(after(block, tie), perm=swap) for block in blocks]
        heights = [block.shape[0] for block in blocks]
        kept[distance], *cuts = expert_part(others + blocks, (sum(heights), *heights), hint, *weights)
        given[distance] = [send(cut, perm=swap) for cut in cuts]

    first, second = pack(core, tokens, routes, gate_num, devices)
    others = [send(block, perm=swap) for block in (first, second)]
    kept[0], cut = expert_part([first, second] + others, (rows, rows), 2, *weights)
    given[0] = send(cut, perm=swap)
    long = jnp.concatenate([send(first, perm=on), send(second, perm=to_other)], axis=0)
    short = jnp.concatenate([send(second, perm=on), send(first, perm=to_other)], axis=0)
    run(1, [long, short], 2)
    for distance in range(2, reach):
        tie = kept[distance - 2]
        long, short = send(after(long, tie), perm=on), send(after(short, tie), perm=on)
        run(distance, [long, short], 2)
    long = send(after(long, kept[reach - 2]), perm=on)
    run(reach, [long], 2)

    def terms(distance, number):
        return [(kept[distance], number * rows), (given[distance][number], 0)]

    short = send(step_sum(terms(reach - 1, 1), rows), perm=on)
    long = send(step_sum(terms(reach, 0), rows), perm=on)
    for distance in range(reach - 1, 1, -1):
        if distance < reach - 1:
            short = send(step_sum(terms(distance, 1) + [(short, 0)], rows), perm=on)
        long = send(step_sum(terms(distance, 0) + [(long, 0)], rows), perm=on)

    def arrive(carried, number):
        pieces = []
        for start, perm in ((0, back_to_other), (half, on)):
            (kept_1, at), (given_1, _) = terms(1, number)
            pieces.append(send(step_sum([(kept_1, at + start), (given_1, start), (carried, start)], half), perm=perm))
        return pieces

    short_cross, short_same = arrive(short, 1)
    long_cross, long_same = arrive(long, 0)
    return last_sum(core, kept[0], given[0], short_same, long_cross, long_same, short_cross)


def solution(mesh):
    in_specs = (
        P(("groups", "expert"), None),
        P(("groups", "expert"), None),
        P(("groups", "expert"), None),
        P("expert", None, None),
        P("expert", None),
        P("expert", None, None),
        P("expert", None),
    )
    out_specs = P(("groups", "expert"), None)
    return jax.shard_map(body, mesh=mesh, in_specs=in_specs, out_specs=out_specs, check_vma=False)
```

```python
import functools

import jax
import jax.numpy as jnp
from jax import lax
from jax.experimental import pallas as pl
from jax.experimental.pallas import tpu as pltpu
from jax.sharding import PartitionSpec as P

DENOMINATOR = 32768.0
LANES = 128
UNIT_CHUNK = 256
WIDTH_CHUNK = 1024
ANYWHERE = pl.BlockSpec(memory_space=pl.ANY)
VMEM = pl.BlockSpec(memory_space=pltpu.VMEM)
SMEM = pl.BlockSpec(memory_space=pltpu.SMEM)


def ring_of(chips):
    if chips == 8:
        return [0, 2, 4, 6, 7, 5, 3, 1]
    return list(range(chips))


def limits(mebibytes):
    return pltpu.CompilerParams(vmem_limit_bytes=mebibytes << 20)


def pack_kernel(experts, core, tokens, routes, gate_num, own, other, digits):
    rows, width = tokens.shape
    half = rows // 2
    lane = lax.broadcasted_iota(jnp.int32, (rows, LANES), 1)
    expert = jnp.where(lane < experts, lane, lane - experts)
    dense = jnp.zeros((rows, LANES), jnp.int32)
    for pick in range(routes.shape[1]):
        column = slice(pick, pick + 1)
        dense += jnp.where(routes[:, column] == expert, gate_num[:, column], 0)
    digit = jnp.where(lane < experts, dense >> 8, dense & 255)
    digit = jnp.where(lane < 2 * experts, digit, 0)
    digits[...] = digit.astype(jnp.float32).astype(jnp.bfloat16)
    for packed, place in ((own, core[0]), (other, 1 - core[0])):
        for there, place_here in ((0, place), (half, 1 - place)):
            here = pl.ds(pl.multiple_of(place_here * half, half), half)
            packed[there : there + half, :width] = tokens[here]
            packed[there : there + half, width:] = digits[here]


def pack(core, tokens, routes, gate_num, experts):
    rows, width = tokens.shape
    return pl.pallas_call(
        functools.partial(pack_kernel, experts),
        in_specs=[SMEM] + [VMEM] * 3,
        out_specs=[VMEM] * 2,
        out_shape=[jax.ShapeDtypeStruct((rows, width + LANES), jnp.bfloat16)] * 2,
        scratch_shapes=[pltpu.VMEM((rows, LANES), jnp.bfloat16)],
        compiler_params=limits(4),
        name="pack",
    )(core, tokens, routes, gate_num)


def keep_kernel(gate_up, down, gate_up_here, down_here, sem):
    copies = [
        pltpu.make_async_copy(gate_up, gate_up_here, sem.at[0]),
        pltpu.make_async_copy(down, down_here, sem.at[1]),
    ]
    for copy in copies:
        copy.start()
    for copy in copies:
        copy.wait()


def keep(gate_up_w, down_w):
    return pl.pallas_call(
        keep_kernel,
        in_specs=[ANYWHERE] * 2,
        out_specs=[VMEM] * 2,
        out_shape=[pltpu.VMEM(w.shape, w.dtype) for w in (gate_up_w, down_w)],
        scratch_shapes=[pltpu.SemaphoreType.DMA((2,))],
        compiler_params=limits(1),
        cost_estimate=pl.CostEstimate(
            flops=0, bytes_accessed=2 * (gate_up_w.size + down_w.size), transcendentals=0
        ),
        name="keep",
    )(*(pltpu.with_memory_space_constraint(w, pltpu.HBM) for w in (gate_up_w, down_w)))


def expert_kernel(count, *refs):
    xs = refs[:count]
    pick, gate_up_s, down_s, gate_up, down = refs[count : count + 5]
    outs = refs[count + 5 : -2]
    x, hidden = refs[-2:]
    units, width = down.shape

    at = 0
    for ref in xs:
        x[at : at + ref.shape[0]] = ref[...]
        at += ref.shape[0]
    digits = x[:, width:].astype(jnp.float32)
    weight = jnp.sum(digits * pick[...], axis=1, keepdims=True) / DENOMINATOR

    def unit_step(chunk, carry):
        sides = []
        for side in range(2):
            columns = pl.ds(pl.multiple_of(side * units + chunk * UNIT_CHUNK, UNIT_CHUNK), UNIT_CHUNK)
            part = jnp.dot(x[:, :width], gate_up[:, columns], preferred_element_type=jnp.float32)
            sides.append(part * gate_up_s[:, columns])
        here = pl.ds(pl.multiple_of(chunk * UNIT_CHUNK, UNIT_CHUNK), UNIT_CHUNK)
        hidden[:, here] = (jax.nn.silu(sides[0]) * sides[1]).astype(jnp.bfloat16)
        return carry

    lax.fori_loop(0, units // UNIT_CHUNK, unit_step, 0)

    def width_step(chunk, carry):
        columns = pl.ds(pl.multiple_of(chunk * WIDTH_CHUNK, WIDTH_CHUNK), WIDTH_CHUNK)
        part = jnp.dot(hidden[...], down[:, columns], preferred_element_type=jnp.float32)
        part = (part * down_s[:, columns] * weight).astype(jnp.bfloat16)
        at = 0
        for ref in outs:
            ref[:, columns] = part[at : at + ref.shape[0]]
            at += ref.shape[0]
        return carry

    lax.fori_loop(0, width // WIDTH_CHUNK, width_step, 0)


def expert_part(blocks, out_rows, hint, pick, gate_up_w, gate_up_s, down_w, down_s):
    width, units2 = gate_up_w.shape
    units = down_w.shape[0]
    rows, packed_width = sum(block.shape[0] for block in blocks), blocks[0].shape[1]
    flops = int(hint * 2 * rows * width * (units2 + units))
    return pl.pallas_call(
        functools.partial(expert_kernel, len(blocks)),
        in_specs=[VMEM] * (len(blocks) + 5),
        out_specs=[VMEM] * len(out_rows),
        out_shape=[jax.ShapeDtypeStruct((size, width), jnp.bfloat16) for size in out_rows],
        scratch_shapes=[
            pltpu.VMEM((rows, packed_width), jnp.bfloat16),
            pltpu.VMEM((rows, units), jnp.bfloat16),
        ],
        compiler_params=limits(14),
        cost_estimate=pl.CostEstimate(flops=flops, bytes_accessed=0, transcendentals=0),
        name="expert",
    )(
        *blocks,
        pick,
        gate_up_s,
        down_s,
        pltpu.with_memory_space_constraint(gate_up_w, pltpu.VMEM),
        pltpu.with_memory_space_constraint(down_w, pltpu.VMEM),
    )


def step_kernel(plan, *refs):
    *terms, out = refs
    for first, rows, places in plan:
        for column in range(0, out.shape[1], WIDTH_CHUNK):
            columns = slice(column, column + WIDTH_CHUNK)
            total = 0.0
            for number, start in places:
                total += terms[number][start : start + rows, columns].astype(jnp.float32)
            out[first : first + rows, columns] = total.astype(jnp.bfloat16)


def step_sum(*segments):
    arrays, plan, height = [], [], 0
    for rows, terms in segments:
        places = []
        for array, start in terms:
            number = next((i for i, known in enumerate(arrays) if known is array), len(arrays))
            if number == len(arrays):
                arrays.append(array)
            places.append((number, start))
        plan.append((height, rows, tuple(places)))
        height += rows
    return pl.pallas_call(
        functools.partial(step_kernel, tuple(plan)),
        in_specs=[VMEM] * len(arrays),
        out_specs=VMEM,
        out_shape=jax.ShapeDtypeStruct((height, arrays[0].shape[1]), jnp.bfloat16),
        compiler_params=limits(4),
        name="step_sum",
    )(*arrays)


def join_kernel(same, cross, block):
    half = same.shape[0] // 2
    for number in range(4):
        place = slice((number // 2) * half, (number // 2 + 1) * half)
        block[number * half : (number + 1) * half] = (same, cross)[number % 2][place]


def join(same, cross):
    return pl.pallas_call(
        join_kernel,
        in_specs=[VMEM] * 2,
        out_specs=VMEM,
        out_shape=jax.ShapeDtypeStruct((2 * same.shape[0], same.shape[1]), same.dtype),
        compiler_params=limits(4),
        name="join",
    )(same, cross)


def last_kernel(core, mine, theirs, *refs):
    *arrived, out = refs
    half = out.shape[0] // 2
    for which, place in ((0, core[0]), (1, 1 - core[0])):
        there = pl.ds(pl.multiple_of(place * half, half), half)
        here = slice(which * half, (which + 1) * half)
        for column in range(0, out.shape[1], WIDTH_CHUNK):
            columns = slice(column, column + WIDTH_CHUNK)
            total = mine[here, columns].astype(jnp.float32) + theirs[here, columns].astype(jnp.float32)
            for ref in arrived[2 * which : 2 * which + 2]:
                total += ref[:, columns].astype(jnp.float32)
            out[there, columns] = total.astype(jnp.bfloat16)


def last_sum(core, mine, theirs, *arrived):
    return pl.pallas_call(
        last_kernel,
        in_specs=[SMEM] + [VMEM] * (2 + len(arrived)),
        out_specs=VMEM,
        out_shape=jax.ShapeDtypeStruct(mine.shape, jnp.bfloat16),
        compiler_params=limits(4),
        name="last_sum",
    )(core, mine, theirs, *arrived)


def together(*values):
    return lax.optimization_barrier(values)


def after(value, *others):
    return together(value, *others)[0] if others else value


def body(tokens, routes, gate_num, gate_up_q, gate_up_scale, down_q, down_scale):
    devices = lax.axis_size("expert")
    expert = lax.axis_index("expert")
    chips = devices // 2
    reach = chips // 2
    rows, width = tokens.shape
    half = rows // 2
    ring = ring_of(chips)

    def hop(shift, cross):
        pairs = []
        for place in range(chips):
            for core, way in ((0, shift), (1, -shift)):
                to = ring[(place + way) % chips]
                pairs.append((2 * ring[place] + core, 2 * to + (core ^ cross)))
        return pairs

    on, to_other, back_to_other = hop(1, 0), hop(-1, 1), hop(1, 1)
    swap = [(i, i ^ 1) for i in range(devices)]

    def send(x, perm, name):
        with jax.named_scope(name):
            return lax.ppermute(x, "expert", perm)

    lane = jnp.arange(LANES, dtype=jnp.int32)
    pick = jnp.where(lane == expert, 256.0, jnp.where(lane == devices + expert, 1.0, 0.0))
    pick = pick.astype(jnp.float32)[None, :]
    core = (expert & 1).astype(jnp.int32)[None]
    gate_up_w, down_w = keep(gate_up_q[0], down_q[0])
    weights = (pick, gate_up_w, gate_up_scale, down_w, down_scale)

    kept, given = {}, {}

    def run(distance, block, cuts, hint):
        other = send(after(block, kept[distance - 1]), swap, f"swap_in_{distance}")
        kept[distance], *given_here = expert_part([other, block], (block.shape[0], *cuts), hint, *weights)
        given[distance] = [send(cut, swap, f"swap_out_{distance}") for cut in given_here]

    own, own_for_other = pack(core, tokens, routes, gate_num, devices)
    other = send(own, swap, "swap_in_0")
    kept[0], cut = expert_part([own, other], (rows, rows), 2, *weights)
    given[0] = send(cut, swap, "swap_out_0")
    same, cross = send(own, on, "gather_1"), send(own_for_other, to_other, "gather_1")
    block = join(after(same, kept[0]), cross)
    run(1, block, (rows, rows), 2)
    for distance in range(2, reach):
        block = send(after(block, kept[distance - 2]), on, f"gather_{distance}")
        run(distance, block, (rows, rows), 2)
    block = send(after(block[:rows], kept[reach - 2]), on, f"gather_{reach}")

    def terms(distance, number):
        return [(kept[distance], number * rows), (given[distance][number], 0)]

    total = step_sum((rows, terms(reach - 1, 1)))
    short = send(total, on, f"return_short_{reach - 1}")
    block = after(block, total)
    run(reach, block, (rows,), 2)

    def arrive(carried, number, name):
        pieces, totals = [], []
        for start, perm in ((0, back_to_other), (half, on)):
            (kept_1, at), (given_1, _) = terms(1, number)
            total = step_sum((half, [(kept_1, at + start), (given_1, start), (carried, start)]))
            pieces.append(send(total, perm, name))
            totals.append(total)
        return pieces, totals

    pieces, height = [], rows // len(given[reach])
    for number, piece in enumerate(given[reach]):
        pieces.append((height, [(kept[reach], number * height), (after(piece, short), 0)]))
    long = send(step_sum(*pieces), on, f"return_long_{reach}")
    for distance in range(reach - 1, 1, -1):
        if distance > 2:
            total = step_sum((rows, terms(distance - 1, 1) + [(short, 0)]))
            short_next = send(total, on, f"return_short_{distance - 1}")
            totals = [total]
        else:
            short_next, totals = arrive(short, 1, "return_short_1")
        total = step_sum((rows, terms(distance, 0) + [(after(long, *totals), 0)]))
        long = send(total, on, f"return_long_{distance}")
        short = short_next

    short_cross, short_same = short
    long_cross, long_same = arrive(long, 0, "return_long_1")[0]
    return last_sum(core, kept[0], given[0], short_same, long_cross, long_same, short_cross)


def solution(mesh):
    in_specs = (
        P(("groups", "expert"), None),
        P(("groups", "expert"), None),
        P(("groups", "expert"), None),
        P("expert", None, None),
        P("expert", None),
        P("expert", None, None),
        P("expert", None),
    )
    out_specs = P(("groups", "expert"), None)
    return jax.shard_map(body, mesh=mesh, in_specs=in_specs, out_specs=out_specs, check_vma=False)
```

```python
import functools

import jax
import jax.numpy as jnp
from jax import lax
from jax.experimental import pallas as pl
from jax.experimental.pallas import tpu as pltpu
from jax.sharding import PartitionSpec as P

DENOMINATOR = 32768.0
LANES = 128
UNIT_CHUNK = 256
WIDTH_CHUNK = 1024
ANYWHERE = pl.BlockSpec(memory_space=pl.ANY)
VMEM = pl.BlockSpec(memory_space=pltpu.VMEM)
SMEM = pl.BlockSpec(memory_space=pltpu.SMEM)


def ring_of(chips):
    if chips == 8:
        return [0, 2, 4, 6, 7, 5, 3, 1]
    return list(range(chips))


def limits(mebibytes):
    return pltpu.CompilerParams(vmem_limit_bytes=mebibytes << 20)


def pack_kernel(experts, core, tokens, routes, gate_num, own, for_other, digits):
    rows, width = tokens.shape
    half = rows // 2
    lane = lax.broadcasted_iota(jnp.int32, (rows, LANES), 1)
    expert = jnp.where(lane < experts, lane, lane - experts)
    dense = jnp.zeros((rows, LANES), jnp.int32)
    for pick in range(routes.shape[1]):
        column = slice(pick, pick + 1)
        dense += jnp.where(routes[:, column] == expert, gate_num[:, column], 0)
    digit = jnp.where(lane < experts, dense >> 8, dense & 255)
    digit = jnp.where(lane < 2 * experts, digit, 0)
    digits[...] = digit.astype(jnp.float32).astype(jnp.bfloat16)
    for packed, place in ((own, core[0]), (for_other, 1 - core[0])):
        for there, place_here in ((0, place), (half, 1 - place)):
            here = pl.ds(pl.multiple_of(place_here * half, half), half)
            packed[there : there + half, :width] = tokens[here]
            packed[there : there + half, width:] = digits[here]


def pack(core, tokens, routes, gate_num, experts):
    rows, width = tokens.shape
    return pl.pallas_call(
        functools.partial(pack_kernel, experts),
        in_specs=[SMEM] + [VMEM] * 3,
        out_specs=[VMEM] * 2,
        out_shape=[jax.ShapeDtypeStruct((rows, width + LANES), jnp.bfloat16)] * 2,
        scratch_shapes=[pltpu.VMEM((rows, LANES), jnp.bfloat16)],
        compiler_params=limits(2),
        name="pack",
    )(core, tokens, routes, gate_num)


def expert_kernel(count, experts, has_before, fetch, *refs):
    refs = list(refs)
    take = lambda number: [refs.pop(0) for _ in range(number)]
    xs, sets = take(count), [take(5) for _ in range(experts)]
    before = take(count) if has_before else []
    outs, here = take(count), take(2) if fetch else []
    (x,), hiddens, sems = take(1), take(experts), refs
    units, width = sets[0][4].shape

    def unit_columns(chunk, side):
        return pl.ds(pl.multiple_of(side * units + chunk * UNIT_CHUNK, UNIT_CHUNK), UNIT_CHUNK)

    def width_columns(chunk):
        return pl.ds(pl.multiple_of(chunk * WIDTH_CHUNK, WIDTH_CHUNK), WIDTH_CHUNK)

    def unit_copy(chunk, side):
        columns = unit_columns(chunk, side)
        return pltpu.make_async_copy(there[0].at[:, columns], here[0].at[:, columns], sems[0].at[chunk, side])

    def width_copy(chunk):
        columns = width_columns(chunk)
        return pltpu.make_async_copy(there[1].at[:, columns], here[1].at[:, columns], sems[1].at[chunk])

    if fetch:
        there = sets[0][3:]
        sets[0][3:] = here
        for chunk in range(units // UNIT_CHUNK):
            for side in range(2):
                unit_copy(chunk, side).start()
        for chunk in range(width // WIDTH_CHUNK):
            width_copy(chunk).start()

    at = 0
    for ref in xs:
        x[at : at + ref.shape[0]] = ref[...]
        at += ref.shape[0]
    digits = x[:, width:].astype(jnp.float32)
    gates = [jnp.sum(digits * pick[...], axis=1, keepdims=True) / DENOMINATOR for pick, *_ in sets]

    for (_, gate_up_s, _, gate_up, _), hidden in zip(sets, hiddens):

        def unit_step(chunk, carry, gate_up_s=gate_up_s, gate_up=gate_up, hidden=hidden):
            sides = []
            for side in range(2):
                columns = unit_columns(chunk, side)
                if fetch:
                    unit_copy(chunk, side).wait()
                part = jnp.dot(x[:, :width], gate_up[:, columns], preferred_element_type=jnp.float32)
                sides.append(part * gate_up_s[:, columns])
            hidden[:, unit_columns(chunk, 0)] = (jax.nn.silu(sides[0]) * sides[1]).astype(jnp.bfloat16)
            return carry

        lax.fori_loop(0, units // UNIT_CHUNK, unit_step, 0)

    def width_step(chunk, carry):
        columns = width_columns(chunk)
        if fetch:
            width_copy(chunk).wait()
        total = 0.0
        for (_, _, down_s, _, down), hidden, gate in zip(sets, hiddens, gates):
            part = jnp.dot(hidden[...], down[:, columns], preferred_element_type=jnp.float32)
            total += part * down_s[:, columns] * gate
        at = 0
        for number, ref in enumerate(outs):
            part = total[at : at + ref.shape[0]]
            if has_before:
                part += before[number][:, columns].astype(jnp.float32)
            ref[:, columns] = part.astype(jnp.bfloat16)
            at += ref.shape[0]
        return carry

    lax.fori_loop(0, width // WIDTH_CHUNK, width_step, 0)


def expert_part(blocks, sets, before=(), fetch=False):
    units, width = sets[0][4].shape
    rows, packed_width = sum(block.shape[0] for block in blocks), blocks[0].shape[1]
    space = pltpu.HBM if fetch else pltpu.VMEM
    operands, specs = list(blocks), [VMEM] * len(blocks)
    for pick, gate_up_s, down_s, gate_up_w, down_w in sets:
        operands += [pick, gate_up_s, down_s]
        operands += [pltpu.with_memory_space_constraint(w, space) for w in (gate_up_w, down_w)]
        specs += [VMEM] * 3 + [ANYWHERE if fetch else VMEM] * 2
    operands += before
    specs += [VMEM] * len(before)
    out_shape = [jax.ShapeDtypeStruct((block.shape[0], width), jnp.bfloat16) for block in blocks]
    scratch = [pltpu.VMEM((rows, packed_width), jnp.bfloat16)]
    scratch += [pltpu.VMEM((rows, units), jnp.bfloat16)] * len(sets)
    if fetch:
        out_shape += [pltpu.VMEM(w.shape, w.dtype) for w in sets[0][3:]]
        scratch.append(pltpu.SemaphoreType.DMA((units // UNIT_CHUNK, 2)))
        scratch.append(pltpu.SemaphoreType.DMA((width // WIDTH_CHUNK,)))
    return pl.pallas_call(
        functools.partial(expert_kernel, len(blocks), len(sets), bool(before), fetch),
        in_specs=specs,
        out_specs=[VMEM] * len(out_shape),
        out_shape=out_shape,
        scratch_shapes=scratch,
        compiler_params=limits(6),
        cost_estimate=pl.CostEstimate(
            flops=2 * len(sets) * 2 * rows * width * 3 * units, bytes_accessed=0, transcendentals=0
        ),
        name="expert",
    )(*operands)


def step_kernel(plan, *refs):
    *terms, out = refs
    for first, rows, places in plan:
        for column in range(0, out.shape[1], WIDTH_CHUNK):
            columns = slice(column, column + WIDTH_CHUNK)
            total = 0.0
            for number, start in places:
                total += terms[number][start : start + rows, columns].astype(jnp.float32)
            out[first : first + rows, columns] = total.astype(jnp.bfloat16)


def step_sum(*segments):
    arrays, plan, height = [], [], 0
    for rows, terms in segments:
        places = []
        for array, start in terms:
            number = next((i for i, known in enumerate(arrays) if known is array), len(arrays))
            if number == len(arrays):
                arrays.append(array)
            places.append((number, start))
        plan.append((height, rows, tuple(places)))
        height += rows
    return pl.pallas_call(
        functools.partial(step_kernel, tuple(plan)),
        in_specs=[VMEM] * len(arrays),
        out_specs=VMEM,
        out_shape=jax.ShapeDtypeStruct((height, arrays[0].shape[1]), jnp.bfloat16),
        compiler_params=limits(2),
        name="step_sum",
    )(*arrays)


def join_kernel(same, cross, long, short):
    half = same.shape[0] // 2
    for block, first in ((long, 0), (short, half)):
        block[:half] = same[first : first + half]
        block[half:] = cross[first : first + half]


def join(same, cross):
    return pl.pallas_call(
        join_kernel,
        in_specs=[VMEM] * 2,
        out_specs=[VMEM] * 2,
        out_shape=[jax.ShapeDtypeStruct(same.shape, same.dtype)] * 2,
        compiler_params=limits(2),
        name="join",
    )(same, cross)


def last_kernel(core, mine, *refs):
    *arrived, out = refs
    half = out.shape[0] // 2
    for which, place in ((0, core[0]), (1, 1 - core[0])):
        there = pl.ds(pl.multiple_of(place * half, half), half)
        for column in range(0, out.shape[1], WIDTH_CHUNK):
            columns = slice(column, column + WIDTH_CHUNK)
            total = mine[which * half : (which + 1) * half, columns].astype(jnp.float32)
            for ref in arrived[2 * which : 2 * which + 2]:
                total += ref[:, columns].astype(jnp.float32)
            out[there, columns] = total.astype(jnp.bfloat16)


def last_sum(core, mine, *arrived):
    return pl.pallas_call(
        last_kernel,
        in_specs=[SMEM] + [VMEM] * (1 + len(arrived)),
        out_specs=VMEM,
        out_shape=jax.ShapeDtypeStruct(mine.shape, jnp.bfloat16),
        compiler_params=limits(2),
        name="last_sum",
    )(core, mine, *arrived)


def together(*values):
    return lax.optimization_barrier(values)


def after(value, *others):
    return together(value, *others)[0] if others else value


def body(tokens, routes, gate_num, gate_up_q, gate_up_scale, down_q, down_scale):
    devices = lax.axis_size("expert")
    expert = lax.axis_index("expert")
    chips = devices // 2
    reach = chips // 2
    rows, width = tokens.shape
    half = rows // 2
    ring = ring_of(chips)

    def hop(shift, cross):
        pairs = []
        for place in range(chips):
            for core, way in ((0, shift), (1, -shift)):
                to = ring[(place + way) % chips]
                pairs.append((2 * ring[place] + core, 2 * to + (core ^ cross)))
        return pairs

    on, back, back_to_other = hop(1, 0), hop(-1, 0), hop(-1, 1)
    swap = [(i, i ^ 1) for i in range(devices)]

    def send(x, perm, name):
        with jax.named_scope(name):
            return lax.ppermute(x, "expert", perm)

    def pick(expert):
        lane = jnp.arange(LANES, dtype=jnp.int32)
        digits = jnp.where(lane == expert, 256.0, jnp.where(lane == devices + expert, 1.0, 0.0))
        return digits.astype(jnp.float32)[None, :]

    core = (expert & 1).astype(jnp.int32)[None]
    theirs = [send(x, swap, "weights") for x in (gate_up_q[0], down_q[0])]
    scales = send(jnp.concatenate([gate_up_scale, down_scale], axis=1), swap, "weights")
    theirs += [scales[:, : gate_up_scale.shape[1]], scales[:, gate_up_scale.shape[1] :]]
    own_set = (pick(expert), gate_up_scale, down_scale, gate_up_q[0], down_q[0])
    other_set = (pick(expert ^ 1), theirs[2], theirs[3], theirs[0], theirs[1])

    blocks, mine = {}, {}
    own, own_for_other = pack(core, tokens, routes, gate_num, devices)
    blocks[0] = [own]
    *mine[0], gate_up_w, down_w = expert_part(blocks[0], [own_set], fetch=True)
    own_set = (*own_set[:3], gate_up_w, down_w)
    same, cross = send(own, on, "gather_long_1"), send(own_for_other, back_to_other, "gather_long_1")
    long, short = join(after(same, *mine[0]), cross)
    for distance in range(1, reach):
        if distance > 1:
            tie = mine[distance - 2]
            long = send(after(long, *tie), on, f"gather_long_{distance}")
            short = send(after(short, *tie), on, f"gather_short_{distance}")
        blocks[distance] = [long, short]
        if distance < reach - 1:
            mine[distance] = expert_part(blocks[distance], [own_set])
    for start in range(0, reach - 1, 3):
        near = [(distance, number) for distance in range(start, min(start + 3, reach - 1)) for number in range(len(mine[distance]))]
        done = expert_part(
            [blocks[distance][number] for distance, number in near],
            [other_set],
            [mine[distance][number] for distance, number in near],
            fetch=start == 0,
        )
        if start == 0:
            other_set = (*other_set[:3], *done[-2:])
        for (distance, number), part in zip(near, done):
            mine[distance] = [part if i == number else x for i, x in enumerate(mine[distance])]
    farthest = send(after(long, *mine[reach - 3]), on, f"gather_long_{reach}")
    blocks[reach - 1] = [after(block, mine[0][0]) for block in blocks[reach - 1]]
    mine[reach - 1] = expert_part(blocks[reach - 1], [own_set, other_set])
    mine[reach] = expert_part([after(farthest, *mine[reach - 1])], [own_set, other_set])

    def onward(distance, number, carried):
        terms = [(mine[distance][number], 0)] + [(x, 0) for x in carried]
        name = f"return_{('long', 'short')[number]}_{distance}"
        if distance > 1:
            total = step_sum((rows, terms)) if carried else mine[distance][number]
            return [send(total, back, name)], total
        sent, totals = [], []
        for start, perm in ((0, back), (half, back_to_other)):
            totals.append(step_sum((half, [(x, start) for x, _ in terms])))
            sent.append(send(totals[-1], perm, name))
        return sent, totals[0]

    short, _ = onward(reach - 1, 1, [])
    long, total = onward(reach, 0, [])
    for distance in range(reach - 1, 0, -1):
        if distance > 1:
            short, total = onward(distance - 1, 1, [after(x, total) for x in short])
        long, total = onward(distance, 0, [after(x, total) for x in long])
    return last_sum(core, *mine[0], long[0], short[1], short[0], long[1])


def solution(mesh):
    in_specs = (
        P(("groups", "expert"), None),
        P(("groups", "expert"), None),
        P(("groups", "expert"), None),
        P("expert", None, None),
        P("expert", None),
        P("expert", None, None),
        P("expert", None),
    )
    out_specs = P(("groups", "expert"), None)
    return jax.shard_map(body, mesh=mesh, in_specs=in_specs, out_specs=out_specs, check_vma=False)
```

```python
import functools

import jax
import jax.numpy as jnp
from jax import lax
from jax.experimental import pallas as pl
from jax.experimental.pallas import tpu as pltpu
from jax.sharding import PartitionSpec as P

DENOMINATOR = 32768.0
LANES = 128
UNIT_CHUNK = 256
WIDTH_CHUNK = 1024
ANYWHERE = pl.BlockSpec(memory_space=pl.ANY)
VMEM = pl.BlockSpec(memory_space=pltpu.VMEM)
SMEM = pl.BlockSpec(memory_space=pltpu.SMEM)


def ring_of(chips):
    if chips == 8:
        return [0, 2, 4, 6, 7, 5, 3, 1]
    return list(range(chips))


def limits(mebibytes):
    return pltpu.CompilerParams(vmem_limit_bytes=mebibytes << 20)


def pack_kernel(experts, core, tokens, routes, gate_num, own, other, digits):
    rows, width = tokens.shape
    half = rows // 2
    lane = lax.broadcasted_iota(jnp.int32, (rows, LANES), 1)
    expert = jnp.where(lane < experts, lane, lane - experts)
    dense = jnp.zeros((rows, LANES), jnp.int32)
    for pick in range(routes.shape[1]):
        column = slice(pick, pick + 1)
        dense += jnp.where(routes[:, column] == expert, gate_num[:, column], 0)
    digit = jnp.where(lane < experts, dense >> 8, dense & 255)
    digit = jnp.where(lane < 2 * experts, digit, 0)
    digits[...] = digit.astype(jnp.float32).astype(jnp.bfloat16)
    for packed, place in ((own, core[0]), (other, 1 - core[0])):
        for there, place_here in ((0, place), (half, 1 - place)):
            here = pl.ds(pl.multiple_of(place_here * half, half), half)
            packed[there : there + half, :width] = tokens[here]
            packed[there : there + half, width:] = digits[here]


def pack(core, tokens, routes, gate_num, experts):
    rows, width = tokens.shape
    return pl.pallas_call(
        functools.partial(pack_kernel, experts),
        in_specs=[SMEM] + [VMEM] * 3,
        out_specs=[VMEM] * 2,
        out_shape=[jax.ShapeDtypeStruct((rows, width + LANES), jnp.bfloat16)] * 2,
        scratch_shapes=[pltpu.VMEM((rows, LANES), jnp.bfloat16)],
        compiler_params=limits(4),
        name="pack",
    )(core, tokens, routes, gate_num)


def keep_kernel(gate_up, down, gate_up_here, down_here, sem):
    copies = [
        pltpu.make_async_copy(gate_up, gate_up_here, sem.at[0]),
        pltpu.make_async_copy(down, down_here, sem.at[1]),
    ]
    for copy in copies:
        copy.start()
    for copy in copies:
        copy.wait()


def keep(gate_up_w, down_w):
    return pl.pallas_call(
        keep_kernel,
        in_specs=[ANYWHERE] * 2,
        out_specs=[VMEM] * 2,
        out_shape=[pltpu.VMEM(w.shape, w.dtype) for w in (gate_up_w, down_w)],
        scratch_shapes=[pltpu.SemaphoreType.DMA((2,))],
        compiler_params=limits(1),
        cost_estimate=pl.CostEstimate(
            flops=0, bytes_accessed=2 * (gate_up_w.size + down_w.size), transcendentals=0
        ),
        name="keep",
    )(*(pltpu.with_memory_space_constraint(w, pltpu.HBM) for w in (gate_up_w, down_w)))


def expert_kernel(count, *refs):
    xs = refs[:count]
    pick, gate_up_s, down_s, gate_up, down = refs[count : count + 5]
    outs = refs[count + 5 : -2]
    x, hidden = refs[-2:]
    units, width = down.shape

    at = 0
    for ref in xs:
        x[at : at + ref.shape[0]] = ref[...]
        at += ref.shape[0]
    digits = x[:, width:].astype(jnp.float32)
    weight = jnp.sum(digits * pick[...], axis=1, keepdims=True) / DENOMINATOR

    def unit_step(chunk, carry):
        sides = []
        for side in range(2):
            columns = pl.ds(pl.multiple_of(side * units + chunk * UNIT_CHUNK, UNIT_CHUNK), UNIT_CHUNK)
            part = jnp.dot(x[:, :width], gate_up[:, columns], preferred_element_type=jnp.float32)
            sides.append(part * gate_up_s[:, columns])
        here = pl.ds(pl.multiple_of(chunk * UNIT_CHUNK, UNIT_CHUNK), UNIT_CHUNK)
        hidden[:, here] = (jax.nn.silu(sides[0]) * sides[1]).astype(jnp.bfloat16)
        return carry

    lax.fori_loop(0, units // UNIT_CHUNK, unit_step, 0)

    def width_step(chunk, carry):
        columns = pl.ds(pl.multiple_of(chunk * WIDTH_CHUNK, WIDTH_CHUNK), WIDTH_CHUNK)
        part = jnp.dot(hidden[...], down[:, columns], preferred_element_type=jnp.float32)
        part = (part * down_s[:, columns] * weight).astype(jnp.bfloat16)
        at = 0
        for ref in outs:
            ref[:, columns] = part[at : at + ref.shape[0]]
            at += ref.shape[0]
        return carry

    lax.fori_loop(0, width // WIDTH_CHUNK, width_step, 0)


def expert_part(blocks, out_rows, hint, pick, gate_up_w, gate_up_s, down_w, down_s):
    width, units2 = gate_up_w.shape
    units = down_w.shape[0]
    rows, packed_width = sum(block.shape[0] for block in blocks), blocks[0].shape[1]
    flops = int(hint * 2 * rows * width * (units2 + units))
    return pl.pallas_call(
        functools.partial(expert_kernel, len(blocks)),
        in_specs=[VMEM] * (len(blocks) + 5),
        out_specs=[VMEM] * len(out_rows),
        out_shape=[jax.ShapeDtypeStruct((size, width), jnp.bfloat16) for size in out_rows],
        scratch_shapes=[
            pltpu.VMEM((rows, packed_width), jnp.bfloat16),
            pltpu.VMEM((rows, units), jnp.bfloat16),
        ],
        compiler_params=limits(14),
        cost_estimate=pl.CostEstimate(flops=flops, bytes_accessed=0, transcendentals=0),
        name="expert",
    )(
        *blocks,
        pick,
        gate_up_s,
        down_s,
        pltpu.with_memory_space_constraint(gate_up_w, pltpu.VMEM),
        pltpu.with_memory_space_constraint(down_w, pltpu.VMEM),
    )


def step_kernel(plan, *refs):
    *terms, out = refs
    for first, rows, places in plan:
        for column in range(0, out.shape[1], WIDTH_CHUNK):
            columns = slice(column, column + WIDTH_CHUNK)
            total = 0.0
            for number, start in places:
                total += terms[number][start : start + rows, columns].astype(jnp.float32)
            out[first : first + rows, columns] = total.astype(jnp.bfloat16)


def step_sum(*segments):
    arrays, plan, height = [], [], 0
    for rows, terms in segments:
        places = []
        for array, start in terms:
            number = next((i for i, known in enumerate(arrays) if known is array), len(arrays))
            if number == len(arrays):
                arrays.append(array)
            places.append((number, start))
        plan.append((height, rows, tuple(places)))
        height += rows
    return pl.pallas_call(
        functools.partial(step_kernel, tuple(plan)),
        in_specs=[VMEM] * len(arrays),
        out_specs=VMEM,
        out_shape=jax.ShapeDtypeStruct((height, arrays[0].shape[1]), jnp.bfloat16),
        compiler_params=limits(4),
        name="step_sum",
    )(*arrays)


def join_kernel(same, cross, long, short):
    half = same.shape[0] // 2
    for block, first in ((long, 0), (short, half)):
        block[:half] = same[first : first + half]
        block[half:] = cross[first : first + half]


def join(same, cross):
    return pl.pallas_call(
        join_kernel,
        in_specs=[VMEM] * 2,
        out_specs=[VMEM] * 2,
        out_shape=[jax.ShapeDtypeStruct(same.shape, same.dtype)] * 2,
        compiler_params=limits(2),
        name="join",
    )(same, cross)


def last_kernel(core, mine, theirs, *refs):
    *arrived, out = refs
    half = out.shape[0] // 2
    for which, place in ((0, core[0]), (1, 1 - core[0])):
        there = pl.ds(pl.multiple_of(place * half, half), half)
        here = slice(which * half, (which + 1) * half)
        for column in range(0, out.shape[1], WIDTH_CHUNK):
            columns = slice(column, column + WIDTH_CHUNK)
            total = mine[here, columns].astype(jnp.float32) + theirs[here, columns].astype(jnp.float32)
            for ref in arrived[2 * which : 2 * which + 2]:
                total += ref[:, columns].astype(jnp.float32)
            out[there, columns] = total.astype(jnp.bfloat16)


def last_sum(core, mine, theirs, *arrived):
    return pl.pallas_call(
        last_kernel,
        in_specs=[SMEM] + [VMEM] * (2 + len(arrived)),
        out_specs=VMEM,
        out_shape=jax.ShapeDtypeStruct(mine.shape, jnp.bfloat16),
        compiler_params=limits(4),
        name="last_sum",
    )(core, mine, theirs, *arrived)


def together(*values):
    return lax.optimization_barrier(values)


def after(value, *others):
    return together(value, *others)[0] if others else value


def body(tokens, routes, gate_num, gate_up_q, gate_up_scale, down_q, down_scale):
    devices = lax.axis_size("expert")
    expert = lax.axis_index("expert")
    chips = devices // 2
    reach = chips // 2
    rows, width = tokens.shape
    half = rows // 2
    ring = ring_of(chips)

    def hop(shift, cross):
        pairs = []
        for place in range(chips):
            for core, way in ((0, shift), (1, -shift)):
                to = ring[(place + way) % chips]
                pairs.append((2 * ring[place] + core, 2 * to + (core ^ cross)))
        return pairs

    on, to_other, back_to_other = hop(1, 0), hop(-1, 1), hop(1, 1)
    swap = [(i, i ^ 1) for i in range(devices)]

    def send(x, perm, name):
        with jax.named_scope(name):
            return lax.ppermute(x, "expert", perm)

    lane = jnp.arange(LANES, dtype=jnp.int32)
    pick = jnp.where(lane == expert, 256.0, jnp.where(lane == devices + expert, 1.0, 0.0))
    pick = pick.astype(jnp.float32)[None, :]
    core = (expert & 1).astype(jnp.int32)[None]
    gate_up_w, down_w = keep(gate_up_q[0], down_q[0])
    weights = (pick, gate_up_w, gate_up_scale, down_w, down_scale)

    kept, given = {}, {}

    def run(items, tie, hint=2):
        halves = [after(blocks[item], *tie) for item in items]
        others = [send(x, swap, f"swap_in_{item[0]}") for x, item in zip(halves, items)]
        outs = expert_part([*others, *halves], [x.shape[0] for x in halves] * 2, hint, *weights)
        for number, (distance, name) in enumerate(items):
            kept[distance, name] = outs[number]
            given[distance, name] = send(outs[len(items) + number], swap, f"swap_out_{distance}")
        return outs[:1]

    own, own_for_other = pack(core, tokens, routes, gate_num, devices)
    other = send(own, swap, "swap_in_0")
    kept[0], cut = expert_part([own, other], (rows, rows), 2, *weights)
    given[0] = send(cut, swap, "swap_out_0")
    same, cross = send(own, on, "gather_long_1"), send(own_for_other, to_other, "gather_long_1")
    long, short = join(after(same, kept[0]), cross)
    blocks = {(1, "long"): long, (1, "short"): short}
    last = run([(1, "long"), (1, "short")], [kept[0]])
    for distance in range(2, reach):
        tie = last if distance > 2 else []
        long = send(after(long, *tie), on, f"gather_long_{distance}")
        short = send(after(short, *tie), on, f"gather_short_{distance}")
        blocks[distance, "long"], blocks[distance, "short"] = long, short
    blocks[reach, "long"] = send(long, on, f"gather_long_{reach}")

    def step(distance, name, carried):
        terms = [(x, 0) for x in (kept[distance, name], given[distance, name], *carried)]
        total = step_sum((rows, terms))
        return [send(total, on, f"return_{name}_{distance}")], [total]

    def arrive(name, carried):
        sent, totals = [], []
        for start, perm in ((0, back_to_other), (half, on)):
            terms = [(x, start) for x in (kept[1, name], given[1, name], *carried)]
            totals.append(step_sum((half, terms)))
            sent.append(send(totals[-1], perm, f"return_{name}_1"))
        return sent, totals

    run([(distance, "short") for distance in (reach - 1, reach - 2) if distance > 1], [])
    short, totals = step(reach - 1, "short", ())
    run([(reach, "long")], totals, 2)
    given[reach, "long"] = after(given[reach, "long"], *short)
    long, totals = step(reach, "long", ())
    for distance in range(reach - 1, 0, -1):
        if distance > 1:
            run([(distance, "long")] + [(distance - 2, "short")] * (distance > 3), [], 2)
        if distance > 2:
            short, totals = step(distance - 1, "short", [after(x, *totals) for x in short])
        elif distance == 2:
            short, totals = arrive("short", [after(x, *totals) for x in short])
        if distance > 1:
            long, totals = step(distance, "long", [after(x, *totals) for x in long])
        else:
            long, totals = arrive("long", long)
    short_cross, short_same = short
    long_cross, long_same = long
    return last_sum(core, kept[0], given[0], short_same, long_cross, long_same, short_cross)


def solution(mesh):
    in_specs = (
        P(("groups", "expert"), None),
        P(("groups", "expert"), None),
        P(("groups", "expert"), None),
        P("expert", None, None),
        P("expert", None),
        P("expert", None, None),
        P("expert", None),
    )
    out_specs = P(("groups", "expert"), None)
    return jax.shard_map(body, mesh=mesh, in_specs=in_specs, out_specs=out_specs, check_vma=False)
```

```python
import functools

import jax
import jax.numpy as jnp
from jax import lax
from jax.experimental import pallas as pl
from jax.experimental.pallas import tpu as pltpu
from jax.sharding import PartitionSpec as P

DENOMINATOR = 32768.0
LANES = 128
UNIT_CHUNK = 256
WIDTH_CHUNK = 1024
ANYWHERE = pl.BlockSpec(memory_space=pl.ANY)
VMEM = pl.BlockSpec(memory_space=pltpu.VMEM)
SMEM = pl.BlockSpec(memory_space=pltpu.SMEM)


def ring_of(chips):
    if chips == 8:
        return [0, 2, 4, 6, 7, 5, 3, 1]
    return list(range(chips))


def limits(mebibytes):
    return pltpu.CompilerParams(vmem_limit_bytes=mebibytes << 20)


def pack_kernel(experts, tokens, routes, gate_num, packed):
    rows, width = tokens.shape
    lane = lax.broadcasted_iota(jnp.int32, (rows, LANES), 1)
    expert = jnp.where(lane < experts, lane, lane - experts)
    dense = jnp.zeros((rows, LANES), jnp.int32)
    for pick in range(routes.shape[1]):
        column = slice(pick, pick + 1)
        dense += jnp.where(routes[:, column] == expert, gate_num[:, column], 0)
    digit = jnp.where(lane < experts, dense >> 8, dense & 255)
    digit = jnp.where(lane < 2 * experts, digit, 0)
    packed[:, :width] = tokens[...]
    packed[:, width:] = digit.astype(jnp.float32).astype(jnp.bfloat16)


def pack(tokens, routes, gate_num, experts):
    rows, width = tokens.shape
    return pl.pallas_call(
        functools.partial(pack_kernel, experts),
        in_specs=[VMEM] * 3,
        out_specs=VMEM,
        out_shape=jax.ShapeDtypeStruct((rows, width + LANES), jnp.bfloat16),
        compiler_params=limits(4),
        name="pack",
    )(tokens, routes, gate_num)


def keep_kernel(gate_up, down, gate_up_here, down_here, sem):
    copies = [
        pltpu.make_async_copy(gate_up, gate_up_here, sem.at[0]),
        pltpu.make_async_copy(down, down_here, sem.at[1]),
    ]
    for copy in copies:
        copy.start()
    for copy in copies:
        copy.wait()


def keep(gate_up_w, down_w):
    return pl.pallas_call(
        keep_kernel,
        in_specs=[ANYWHERE] * 2,
        out_specs=[VMEM] * 2,
        out_shape=[pltpu.VMEM(w.shape, w.dtype) for w in (gate_up_w, down_w)],
        scratch_shapes=[pltpu.SemaphoreType.DMA((2,))],
        compiler_params=limits(1),
        cost_estimate=pl.CostEstimate(
            flops=0, bytes_accessed=2 * (gate_up_w.size + down_w.size), transcendentals=0
        ),
        name="keep",
    )(*(pltpu.with_memory_space_constraint(w, pltpu.HBM) for w in (gate_up_w, down_w)))


def expert_kernel(count, *refs):
    xs = refs[:count]
    pick, gate_up_s, down_s, gate_up, down = refs[count : count + 5]
    outs = refs[count + 5 : -2]
    x, hidden = refs[-2:]
    units, width = down.shape

    at = 0
    for ref in xs:
        x[at : at + ref.shape[0]] = ref[...]
        at += ref.shape[0]
    digits = x[:, width:].astype(jnp.float32)
    weight = jnp.sum(digits * pick[...], axis=1, keepdims=True) / DENOMINATOR

    def unit_step(chunk, carry):
        sides = []
        for side in range(2):
            columns = pl.ds(pl.multiple_of(side * units + chunk * UNIT_CHUNK, UNIT_CHUNK), UNIT_CHUNK)
            part = jnp.dot(x[:, :width], gate_up[:, columns], preferred_element_type=jnp.float32)
            sides.append(part * gate_up_s[:, columns])
        here = pl.ds(pl.multiple_of(chunk * UNIT_CHUNK, UNIT_CHUNK), UNIT_CHUNK)
        hidden[:, here] = (jax.nn.silu(sides[0]) * sides[1]).astype(jnp.bfloat16)
        return carry

    lax.fori_loop(0, units // UNIT_CHUNK, unit_step, 0)

    def width_step(chunk, carry):
        columns = pl.ds(pl.multiple_of(chunk * WIDTH_CHUNK, WIDTH_CHUNK), WIDTH_CHUNK)
        part = jnp.dot(hidden[...], down[:, columns], preferred_element_type=jnp.float32)
        part = (part * down_s[:, columns] * weight).astype(jnp.bfloat16)
        at = 0
        for ref in outs:
            ref[:, columns] = part[at : at + ref.shape[0]]
            at += ref.shape[0]
        return carry

    lax.fori_loop(0, width // WIDTH_CHUNK, width_step, 0)


def expert_part(blocks, out_rows, hint, pick, gate_up_w, gate_up_s, down_w, down_s):
    width, units2 = gate_up_w.shape
    units = down_w.shape[0]
    rows, packed_width = sum(block.shape[0] for block in blocks), blocks[0].shape[1]
    flops = int(hint * 2 * rows * width * (units2 + units))
    return pl.pallas_call(
        functools.partial(expert_kernel, len(blocks)),
        in_specs=[VMEM] * (len(blocks) + 5),
        out_specs=[VMEM] * len(out_rows),
        out_shape=[jax.ShapeDtypeStruct((size, width), jnp.bfloat16) for size in out_rows],
        scratch_shapes=[
            pltpu.VMEM((rows, packed_width), jnp.bfloat16),
            pltpu.VMEM((rows, units), jnp.bfloat16),
        ],
        compiler_params=limits(14),
        cost_estimate=pl.CostEstimate(flops=flops, bytes_accessed=0, transcendentals=0),
        name="expert",
    )(
        *blocks,
        pick,
        gate_up_s,
        down_s,
        pltpu.with_memory_space_constraint(gate_up_w, pltpu.VMEM),
        pltpu.with_memory_space_constraint(down_w, pltpu.VMEM),
    )


def sums_kernel(plan, *refs):
    outs = refs[-1 - max(out for _, out, _, _ in plan) :]
    for terms, out, first, rows in plan:
        for column in range(0, outs[out].shape[1], WIDTH_CHUNK):
            columns = slice(column, column + WIDTH_CHUNK)
            total = 0.0
            for number, start in terms:
                total += refs[number][start : start + rows, columns].astype(jnp.float32)
            outs[out][first : first + rows, columns] = total.astype(jnp.bfloat16)


def sums(wanted, shapes, name):
    arrays, plan = [], []
    for terms, *place in wanted:
        numbers = []
        for array, start in terms:
            number = next((i for i, known in enumerate(arrays) if known is array), len(arrays))
            if number == len(arrays):
                arrays.append(array)
            numbers.append((number, start))
        plan.append((tuple(numbers), *place))
    return pl.pallas_call(
        functools.partial(sums_kernel, tuple(plan)),
        in_specs=[VMEM] * len(arrays),
        out_specs=[VMEM] * len(shapes),
        out_shape=[jax.ShapeDtypeStruct(shape, jnp.bfloat16) for shape in shapes],
        compiler_params=limits(4),
        name=name,
    )(*arrays)


def together(*values):
    return lax.optimization_barrier(values)


def after(value, *others):
    return together(value, *others)[0] if others else value


def body(tokens, routes, gate_num, gate_up_q, gate_up_scale, down_q, down_scale):
    devices = lax.axis_size("expert")
    expert = lax.axis_index("expert")
    chips = devices // 2
    reach = chips // 2
    rows, width = tokens.shape
    half = rows // 2
    ring = ring_of(chips)

    def hop(way):
        pairs = []
        for place in range(chips):
            for core in range(2):
                pairs.append((2 * ring[place] + core, 2 * ring[(place + way) % chips] + core))
        return pairs

    ways = (hop(1), hop(-1))
    swap = [(i, i ^ 1) for i in range(devices)]

    def send(x, perm, name):
        with jax.named_scope(name):
            return lax.ppermute(x, "expert", perm)

    def send_both(pair, name):
        return [send(x, way, name) for x, way in zip(pair, ways)]

    lane = jnp.arange(LANES, dtype=jnp.int32)
    pick = jnp.where(lane == expert, 256.0, jnp.where(lane == devices + expert, 1.0, 0.0))
    pick = pick.astype(jnp.float32)[None, :]
    gate_up_w, down_w = keep(gate_up_q[0], down_q[0])
    weights = (pick, gate_up_w, gate_up_scale, down_w, down_scale)

    kept, given = {}, {}

    def run(arrays, items, tie, hint=2):
        arrays = together(*arrays, *tie)[: len(arrays)]
        name = items[0][0]
        others = together(*[send(x, swap, f"swap_in_{name}") for x in arrays])
        outs = expert_part([*arrays, *others], [half] * (2 * len(items)), hint, *weights)
        for number, item in enumerate(items):
            kept[item] = outs[number]
            given[item] = send(outs[len(items) + number], swap, f"swap_out_{name}")
        return outs[:1]

    def run_late(keys, tie, hint=2):
        return run([x for key in keys for x in blocks[key]], [(*key, way) for key in keys for way in range(2)], tie, hint)

    own = pack(tokens, routes, gate_num, devices)
    start = run([own], [(0, "own", 0), (0, "own", 1)], [])
    below, above = send_both((own, own), "gather_long_1")
    below, above = together(below, above, *start)[:2]
    items = [(1, "long", 0), (1, "short", 0), (1, "short", 1), (1, "long", 1)]
    last = run([below, above], items, start)
    long, short = (below[:half], above[half:]), (below[half:], above[:half])
    blocks = {}
    for distance in range(2, reach):
        tie = last if distance > 2 else []
        long = send_both(together(*long, *tie)[:2], f"gather_long_{distance}")
        short = send_both(together(*short, *tie)[:2], f"gather_short_{distance}")
        blocks[distance, "long"], blocks[distance, "short"] = long, short
    blocks[reach, "long"] = send_both(together(*long), f"gather_long_{reach}")

    def step(distance, name, carried):
        wanted = []
        for way in range(2):
            item = (distance, name, 1 - way)
            terms = [(x, 0) for x in (kept[item], given[item], *carried[way : way + 1])]
            wanted.append((terms, way, 0, half))
        totals = sums(wanted, [(half, width)] * 2, "step_sums")
        return send_both(totals, f"return_{name}_{distance}"), totals

    run_late([(distance, "short") for distance in (reach - 1, reach - 2) if distance > 1], [])
    short, totals = step(reach - 1, "short", ())
    run_late([(reach, "long")], totals)
    for way in range(2):
        item = (reach, "long", way)
        given[item] = after(given[item], *short)
    long, totals = step(reach, "long", ())
    for distance in range(reach - 1, 0, -1):
        if distance > 1:
            late = [(d, "long") for d in (distance, distance - 1) if d > 1 and (d, "long", 0) not in kept]
            late += [(d, "short") for d in (distance - 2,) if d > 1]
            if late:
                run_late(late, totals)
            short, totals = step(distance - 1, "short", together(*short, *totals)[:2])
        tie = short if distance == 1 else totals
        long, totals = step(distance, "long", together(*long, *tie)[:2])
    wanted = []
    for which, arrived in enumerate(((short[0], long[1]), (long[0], short[1]))):
        item = (0, "own", which)
        wanted.append(([(x, 0) for x in (kept[item], given[item], *arrived)], 0, which * half, half))
    return sums(wanted, [(rows, width)], "last_sums")[0]


def solution(mesh):
    in_specs = (
        P(("groups", "expert"), None),
        P(("groups", "expert"), None),
        P(("groups", "expert"), None),
        P("expert", None, None),
        P("expert", None),
        P("expert", None, None),
        P("expert", None),
    )
    out_specs = P(("groups", "expert"), None)
    return jax.shard_map(body, mesh=mesh, in_specs=in_specs, out_specs=out_specs, check_vma=False)
```

```python
import functools

import jax
import jax.numpy as jnp
from jax import lax
from jax.experimental import pallas as pl
from jax.experimental.pallas import tpu as pltpu
from jax.sharding import PartitionSpec as P

DENOMINATOR = 32768.0
LANES = 128
UNIT_CHUNK = 256
WIDTH_CHUNK = 1024
ANYWHERE = pl.BlockSpec(memory_space=pl.ANY)
VMEM = pl.BlockSpec(memory_space=pltpu.VMEM)
SMEM = pl.BlockSpec(memory_space=pltpu.SMEM)


def ring_of(chips):
    if chips == 8:
        return [0, 2, 4, 6, 7, 5, 3, 1]
    return list(range(chips))


def limits(mebibytes):
    return pltpu.CompilerParams(vmem_limit_bytes=mebibytes << 20)


def pack_kernel(experts, core, tokens, routes, gate_num, own, for_other, routes_here, gate_num_here, digits, sem):
    rows, width = tokens.shape
    half = rows // 2
    halves = []
    for packed, place in ((own, core[0]), (for_other, 1 - core[0])):
        for there, from_place in ((0, place), (half, 1 - place)):
            halves.append((packed, there, pl.ds(pl.multiple_of(from_place * half, half), half)))
    copies = [pltpu.make_async_copy(routes, routes_here, sem.at[0])]
    copies.append(pltpu.make_async_copy(gate_num, gate_num_here, sem.at[1]))
    for number, (packed, there, here) in enumerate(halves):
        target = packed.at[pl.ds(there, half), pl.ds(0, width)]
        copies.append(pltpu.make_async_copy(tokens.at[here], target, sem.at[2 + number]))
    for copy in copies:
        copy.start()
    for copy in copies[:2]:
        copy.wait()

    place = lax.broadcasted_iota(jnp.int32, (LANES, rows), 0)
    expert = jnp.where(place < experts, place, place - experts)
    dense = jnp.zeros((LANES, rows), jnp.int32)
    for pick in range(routes_here.shape[0]):
        choice = slice(pick, pick + 1)
        dense += jnp.where(routes_here[choice] == expert, gate_num_here[choice], 0)
    digit = jnp.where(place < experts, dense >> 8, dense & 255)
    digit = jnp.where(place < 2 * experts, digit, 0)
    digits[...] = digit.astype(jnp.float32).T.astype(jnp.bfloat16)
    for packed, there, here in halves:
        packed[there : there + half, width:] = digits[here]
    for copy in copies[2:]:
        copy.wait()


def pack(core, tokens, routes, gate_num, experts):
    rows, width = tokens.shape
    operands = [pltpu.with_memory_space_constraint(x, pltpu.HBM) for x in (tokens, routes.T, gate_num.T)]
    return pl.pallas_call(
        functools.partial(pack_kernel, experts),
        in_specs=[SMEM] + [ANYWHERE] * 3,
        out_specs=[VMEM] * 2,
        out_shape=[jax.ShapeDtypeStruct((rows, width + LANES), jnp.bfloat16)] * 2,
        scratch_shapes=[pltpu.VMEM(routes.T.shape, jnp.int32)] * 2
        + [pltpu.VMEM((rows, LANES), jnp.bfloat16), pltpu.SemaphoreType.DMA((6,))],
        compiler_params=limits(4),
        name="pack",
    )(core, *operands)


def keep_kernel(gate_up, down, gate_up_here, down_here, sem):
    copies = [
        pltpu.make_async_copy(gate_up, gate_up_here, sem.at[0]),
        pltpu.make_async_copy(down, down_here, sem.at[1]),
    ]
    for copy in copies:
        copy.start()
    for copy in copies:
        copy.wait()


def keep(gate_up_w, down_w):
    return pl.pallas_call(
        keep_kernel,
        in_specs=[ANYWHERE] * 2,
        out_specs=[VMEM] * 2,
        out_shape=[pltpu.VMEM(w.shape, w.dtype) for w in (gate_up_w, down_w)],
        scratch_shapes=[pltpu.SemaphoreType.DMA((2,))],
        compiler_params=limits(1),
        cost_estimate=pl.CostEstimate(
            flops=0, bytes_accessed=2 * (gate_up_w.size + down_w.size), transcendentals=0
        ),
        name="keep",
    )(*(pltpu.with_memory_space_constraint(w, pltpu.HBM) for w in (gate_up_w, down_w)))


def expert_kernel(count, *refs):
    xs = refs[:count]
    pick, gate_up_s, down_s, gate_up, down = refs[count : count + 5]
    outs = refs[count + 5 : -2]
    x, hidden = refs[-2:]
    units, width = down.shape

    at = 0
    for ref in xs:
        x[at : at + ref.shape[0]] = ref[...]
        at += ref.shape[0]
    digits = x[:, width:].astype(jnp.float32)
    weight = jnp.sum(digits * pick[...], axis=1, keepdims=True) / DENOMINATOR

    def unit_step(chunk, carry):
        sides = []
        for side in range(2):
            columns = pl.ds(pl.multiple_of(side * units + chunk * UNIT_CHUNK, UNIT_CHUNK), UNIT_CHUNK)
            part = jnp.dot(x[:, :width], gate_up[:, columns], preferred_element_type=jnp.float32)
            sides.append(part * gate_up_s[:, columns])
        here = pl.ds(pl.multiple_of(chunk * UNIT_CHUNK, UNIT_CHUNK), UNIT_CHUNK)
        hidden[:, here] = (jax.nn.silu(sides[0]) * sides[1]).astype(jnp.bfloat16)
        return carry

    lax.fori_loop(0, units // UNIT_CHUNK, unit_step, 0)

    def width_step(chunk, carry):
        columns = pl.ds(pl.multiple_of(chunk * WIDTH_CHUNK, WIDTH_CHUNK), WIDTH_CHUNK)
        part = jnp.dot(hidden[...], down[:, columns], preferred_element_type=jnp.float32)
        part = (part * down_s[:, columns] * weight).astype(jnp.bfloat16)
        at = 0
        for ref in outs:
            ref[:, columns] = part[at : at + ref.shape[0]]
            at += ref.shape[0]
        return carry

    lax.fori_loop(0, width // WIDTH_CHUNK, width_step, 0)


def expert_part(blocks, out_rows, hint, pick, gate_up_w, gate_up_s, down_w, down_s):
    width, units2 = gate_up_w.shape
    units = down_w.shape[0]
    rows, packed_width = sum(block.shape[0] for block in blocks), blocks[0].shape[1]
    flops = int(hint * 2 * rows * width * (units2 + units))
    return pl.pallas_call(
        functools.partial(expert_kernel, len(blocks)),
        in_specs=[VMEM] * (len(blocks) + 5),
        out_specs=[VMEM] * len(out_rows),
        out_shape=[jax.ShapeDtypeStruct((size, width), jnp.bfloat16) for size in out_rows],
        scratch_shapes=[
            pltpu.VMEM((rows, packed_width), jnp.bfloat16),
            pltpu.VMEM((rows, units), jnp.bfloat16),
        ],
        compiler_params=limits(14),
        cost_estimate=pl.CostEstimate(flops=flops, bytes_accessed=0, transcendentals=0),
        name="expert",
    )(
        *blocks,
        pick,
        gate_up_s,
        down_s,
        pltpu.with_memory_space_constraint(gate_up_w, pltpu.VMEM),
        pltpu.with_memory_space_constraint(down_w, pltpu.VMEM),
    )


def step_kernel(plan, *refs):
    *terms, out = refs
    for first, rows, places in plan:
        for column in range(0, out.shape[1], WIDTH_CHUNK):
            columns = slice(column, column + WIDTH_CHUNK)
            total = 0.0
            for number, start in places:
                total += terms[number][start : start + rows, columns].astype(jnp.float32)
            out[first : first + rows, columns] = total.astype(jnp.bfloat16)


def step_sum(*segments):
    arrays, plan, height = [], [], 0
    for rows, terms in segments:
        places = []
        for array, start in terms:
            number = next((i for i, known in enumerate(arrays) if known is array), len(arrays))
            if number == len(arrays):
                arrays.append(array)
            places.append((number, start))
        plan.append((height, rows, tuple(places)))
        height += rows
    return pl.pallas_call(
        functools.partial(step_kernel, tuple(plan)),
        in_specs=[VMEM] * len(arrays),
        out_specs=VMEM,
        out_shape=jax.ShapeDtypeStruct((height, arrays[0].shape[1]), jnp.bfloat16),
        compiler_params=limits(4),
        name="step_sum",
    )(*arrays)


def split_kernel(*refs):
    *terms, first, second = refs
    half = first.shape[0]
    for out, start in ((first, 0), (second, half)):
        for column in range(0, out.shape[1], WIDTH_CHUNK):
            columns = slice(column, column + WIDTH_CHUNK)
            total = 0.0
            for term in terms:
                total += term[start : start + half, columns].astype(jnp.float32)
            out[:, columns] = total.astype(jnp.bfloat16)


def split_sum(*terms):
    rows, width = terms[0].shape
    return pl.pallas_call(
        split_kernel,
        in_specs=[VMEM] * len(terms),
        out_specs=[VMEM] * 2,
        out_shape=[jax.ShapeDtypeStruct((rows // 2, width), jnp.bfloat16)] * 2,
        compiler_params=limits(4),
        name="split_sum",
    )(*terms)


def join_kernel(same, cross, long, short):
    half = same.shape[0] // 2
    for block, first in ((long, 0), (short, half)):
        block[:half] = same[first : first + half]
        block[half:] = cross[first : first + half]


def join(same, cross):
    return pl.pallas_call(
        join_kernel,
        in_specs=[VMEM] * 2,
        out_specs=[VMEM] * 2,
        out_shape=[jax.ShapeDtypeStruct(same.shape, same.dtype)] * 2,
        compiler_params=limits(2),
        name="join",
    )(same, cross)


def last_kernel(core, mine, theirs, *refs):
    *arrived, out = refs
    half = out.shape[0] // 2
    for which, place in ((0, core[0]), (1, 1 - core[0])):
        there = pl.ds(pl.multiple_of(place * half, half), half)
        here = slice(which * half, (which + 1) * half)
        for column in range(0, out.shape[1], WIDTH_CHUNK):
            columns = slice(column, column + WIDTH_CHUNK)
            total = mine[here, columns].astype(jnp.float32) + theirs[here, columns].astype(jnp.float32)
            for ref in arrived[2 * which : 2 * which + 2]:
                total += ref[:, columns].astype(jnp.float32)
            out[there, columns] = total.astype(jnp.bfloat16)


def last_sum(core, mine, theirs, *arrived):
    return pl.pallas_call(
        last_kernel,
        in_specs=[SMEM] + [VMEM] * (2 + len(arrived)),
        out_specs=VMEM,
        out_shape=jax.ShapeDtypeStruct(mine.shape, jnp.bfloat16),
        compiler_params=limits(4),
        name="last_sum",
    )(core, mine, theirs, *arrived)


def together(*values):
    return lax.optimization_barrier(values)


def after(value, *others):
    return together(value, *others)[0] if others else value


def body(tokens, routes, gate_num, gate_up_q, gate_up_scale, down_q, down_scale):
    devices = lax.axis_size("expert")
    expert = lax.axis_index("expert")
    chips = devices // 2
    reach = chips // 2
    rows, width = tokens.shape
    half = rows // 2
    ring = ring_of(chips)

    def hop(shift, cross):
        pairs = []
        for place in range(chips):
            for core, way in ((0, shift), (1, -shift)):
                to = ring[(place + way) % chips]
                pairs.append((2 * ring[place] + core, 2 * to + (core ^ cross)))
        return pairs

    on, to_other, back_to_other = hop(1, 0), hop(-1, 1), hop(1, 1)
    swap = [(i, i ^ 1) for i in range(devices)]

    def send(x, perm, name):
        with jax.named_scope(name):
            return lax.ppermute(x, "expert", perm)

    lane = jnp.arange(LANES, dtype=jnp.int32)
    pick = jnp.where(lane == expert, 256.0, jnp.where(lane == devices + expert, 1.0, 0.0))
    pick = pick.astype(jnp.float32)[None, :]
    core = (expert & 1).astype(jnp.int32)[None]
    gate_up_w, down_w = keep(gate_up_q[0], down_q[0])
    weights = (pick, gate_up_w, gate_up_scale, down_w, down_scale)

    kept, given = {}, {}

    def run(items, tie, hint=2):
        halves = [after(blocks[item], *tie) for item in items]
        others = [send(x, swap, f"swap_in_{item[0]}") for x, item in zip(halves, items)]
        outs = expert_part([*others, *halves], [x.shape[0] for x in halves] * 2, hint, *weights)
        for number, (distance, name) in enumerate(items):
            kept[distance, name] = outs[number]
            given[distance, name] = send(outs[len(items) + number], swap, f"swap_out_{distance}")
        return outs[:1]

    own, own_for_other = pack(core, tokens, routes, gate_num, devices)
    other = send(own, swap, "swap_in_0")
    kept[0], cut = expert_part([own, other], (rows, rows), 2, *weights)
    given[0] = send(cut, swap, "swap_out_0")
    same, cross = send(own, on, "gather_long_1"), send(own_for_other, to_other, "gather_long_1")
    long, short = join(after(same, kept[0]), cross)
    blocks = {(1, "long"): long, (1, "short"): short}
    last = run([(1, "long"), (1, "short")], [kept[0]])
    for distance in range(2, reach):
        tie = last if distance > 2 else []
        long = send(after(long, *tie), on, f"gather_long_{distance}")
        short = send(after(short, *tie), on, f"gather_short_{distance}")
        blocks[distance, "long"], blocks[distance, "short"] = long, short
    blocks[reach, "long"] = send(long, on, f"gather_long_{reach}")

    def step(distance, name, carried):
        terms = [(x, 0) for x in (kept[distance, name], given[distance, name], *carried)]
        total = step_sum((rows, terms))
        return [send(total, on, f"return_{name}_{distance}")], [total]

    def arrive(name, carried):
        terms = (kept[1, name], given[1, name], *carried)
        totals = split_sum(*terms)
        return [send(x, perm, f"return_{name}_1") for x, perm in zip(totals, (back_to_other, on))], totals

    if reach > 3:
        last = run([(reach - 2, "short")], last)
    run([(reach - 1, "short")], last)
    short, totals = step(reach - 1, "short", ())
    run([(reach, "long")], totals, 2)
    given[reach, "long"] = after(given[reach, "long"], *short)
    long, totals = step(reach, "long", ())
    for distance in range(reach - 1, 0, -1):
        if distance > 1:
            run([(distance, "long")] + [(distance - 2, "short")] * (distance > 3), [], 2)
        if distance > 2:
            short, totals = step(distance - 1, "short", [after(x, *totals) for x in short])
        elif distance == 2:
            short, totals = arrive("short", [after(x, *totals) for x in short])
        if distance > 1:
            long, totals = step(distance, "long", [after(x, *totals) for x in long])
        else:
            long, totals = arrive("long", [after(x, *short) for x in long])
    short_cross, short_same = short
    long_cross, long_same = long
    return last_sum(core, kept[0], given[0], short_same, long_cross, long_same, short_cross)


def solution(mesh):
    in_specs = (
        P(("groups", "expert"), None),
        P(("groups", "expert"), None),
        P(("groups", "expert"), None),
        P("expert", None, None),
        P("expert", None),
        P("expert", None, None),
        P("expert", None),
    )
    out_specs = P(("groups", "expert"), None)
    return jax.shard_map(body, mesh=mesh, in_specs=in_specs, out_specs=out_specs, check_vma=False)
```

```python
import functools

import jax
import jax.numpy as jnp
from jax import lax
from jax.experimental import pallas as pl
from jax.experimental.pallas import tpu as pltpu
from jax.sharding import PartitionSpec as P

DENOMINATOR = 32768.0
LANES = 128
UNIT_CHUNK = 256
WIDTH_CHUNK = 1024
ANYWHERE = pl.BlockSpec(memory_space=pl.ANY)
VMEM = pl.BlockSpec(memory_space=pltpu.VMEM)
SMEM = pl.BlockSpec(memory_space=pltpu.SMEM)


def ring_of(chips):
    if chips == 8:
        return [0, 2, 4, 6, 7, 5, 3, 1]
    return list(range(chips))


def limits(mebibytes):
    return pltpu.CompilerParams(vmem_limit_bytes=mebibytes << 20)


def pack_kernel(experts, core, tokens, routes, gate_num, own, for_other, routes_here, gate_num_here, digits, sem):
    rows, width = tokens.shape
    half = rows // 2
    halves = []
    for packed, place in ((own, core[0]), (for_other, 1 - core[0])):
        for there, from_place in ((0, place), (half, 1 - place)):
            halves.append((packed, there, pl.ds(pl.multiple_of(from_place * half, half), half)))
    copies = [pltpu.make_async_copy(routes, routes_here, sem.at[0])]
    copies.append(pltpu.make_async_copy(gate_num, gate_num_here, sem.at[1]))
    for number, (packed, there, here) in enumerate(halves):
        target = packed.at[pl.ds(there, half), pl.ds(0, width)]
        copies.append(pltpu.make_async_copy(tokens.at[here], target, sem.at[2 + number]))
    for copy in copies:
        copy.start()
    for copy in copies[:2]:
        copy.wait()

    place = lax.broadcasted_iota(jnp.int32, (LANES, rows), 0)
    expert = jnp.where(place < experts, place, place - experts)
    dense = jnp.zeros((LANES, rows), jnp.int32)
    for pick in range(routes_here.shape[0]):
        choice = slice(pick, pick + 1)
        dense += jnp.where(routes_here[choice] == expert, gate_num_here[choice], 0)
    digit = jnp.where(place < experts, dense >> 8, dense & 255)
    digit = jnp.where(place < 2 * experts, digit, 0)
    digits[...] = digit.astype(jnp.float32).T.astype(jnp.bfloat16)
    for packed, there, here in halves:
        packed[there : there + half, width:] = digits[here]
    for copy in copies[2:]:
        copy.wait()


def pack(core, tokens, routes, gate_num, experts):
    rows, width = tokens.shape
    operands = [pltpu.with_memory_space_constraint(x, pltpu.HBM) for x in (tokens, routes.T, gate_num.T)]
    return pl.pallas_call(
        functools.partial(pack_kernel, experts),
        in_specs=[SMEM] + [ANYWHERE] * 3,
        out_specs=[VMEM] * 2,
        out_shape=[jax.ShapeDtypeStruct((rows, width + LANES), jnp.bfloat16)] * 2,
        scratch_shapes=[pltpu.VMEM(routes.T.shape, jnp.int32)] * 2
        + [pltpu.VMEM((rows, LANES), jnp.bfloat16), pltpu.SemaphoreType.DMA((6,))],
        compiler_params=limits(4),
        name="pack",
    )(core, *operands)


def keep_kernel(gate_up, down, gate_up_here, down_here, sem):
    copies = [
        pltpu.make_async_copy(gate_up, gate_up_here, sem.at[0]),
        pltpu.make_async_copy(down, down_here, sem.at[1]),
    ]
    for copy in copies:
        copy.start()
    for copy in copies:
        copy.wait()


def keep(gate_up_w, down_w):
    return pl.pallas_call(
        keep_kernel,
        in_specs=[ANYWHERE] * 2,
        out_specs=[VMEM] * 2,
        out_shape=[pltpu.VMEM(w.shape, w.dtype) for w in (gate_up_w, down_w)],
        scratch_shapes=[pltpu.SemaphoreType.DMA((2,))],
        compiler_params=limits(1),
        cost_estimate=pl.CostEstimate(
            flops=0, bytes_accessed=2 * (gate_up_w.size + down_w.size), transcendentals=0
        ),
        name="keep",
    )(*(pltpu.with_memory_space_constraint(w, pltpu.HBM) for w in (gate_up_w, down_w)))


def expert_kernel(count, *refs):
    xs = refs[:count]
    pick, gate_up_s, down_s, gate_up, down = refs[count : count + 5]
    outs = refs[count + 5 : -2]
    x, hidden = refs[-2:]
    units, width = down.shape

    at = 0
    for ref in xs:
        x[at : at + ref.shape[0]] = ref[...]
        at += ref.shape[0]
    digits = x[:, width:].astype(jnp.float32)
    weight = jnp.sum(digits * pick[...], axis=1, keepdims=True) / DENOMINATOR

    def unit_step(chunk, carry):
        sides = []
        for side in range(2):
            columns = pl.ds(pl.multiple_of(side * units + chunk * UNIT_CHUNK, UNIT_CHUNK), UNIT_CHUNK)
            part = jnp.dot(x[:, :width], gate_up[:, columns], preferred_element_type=jnp.float32)
            sides.append(part * gate_up_s[:, columns])
        here = pl.ds(pl.multiple_of(chunk * UNIT_CHUNK, UNIT_CHUNK), UNIT_CHUNK)
        hidden[:, here] = (jax.nn.silu(sides[0]) * sides[1]).astype(jnp.bfloat16)
        return carry

    lax.fori_loop(0, units // UNIT_CHUNK, unit_step, 0)

    def width_step(chunk, carry):
        columns = pl.ds(pl.multiple_of(chunk * WIDTH_CHUNK, WIDTH_CHUNK), WIDTH_CHUNK)
        part = jnp.dot(hidden[...], down[:, columns], preferred_element_type=jnp.float32)
        part = (part * down_s[:, columns] * weight).astype(jnp.bfloat16)
        at = 0
        for ref in outs:
            ref[:, columns] = part[at : at + ref.shape[0]]
            at += ref.shape[0]
        return carry

    lax.fori_loop(0, width // WIDTH_CHUNK, width_step, 0)


def expert_part(blocks, out_rows, hint, pick, gate_up_w, gate_up_s, down_w, down_s):
    width, units2 = gate_up_w.shape
    units = down_w.shape[0]
    rows, packed_width = sum(block.shape[0] for block in blocks), blocks[0].shape[1]
    flops = int(hint * 2 * rows * width * (units2 + units))
    return pl.pallas_call(
        functools.partial(expert_kernel, len(blocks)),
        in_specs=[VMEM] * (len(blocks) + 5),
        out_specs=[VMEM] * len(out_rows),
        out_shape=[jax.ShapeDtypeStruct((size, width), jnp.bfloat16) for size in out_rows],
        scratch_shapes=[
            pltpu.VMEM((rows, packed_width), jnp.bfloat16),
            pltpu.VMEM((rows, units), jnp.bfloat16),
        ],
        compiler_params=limits(14),
        cost_estimate=pl.CostEstimate(flops=flops, bytes_accessed=0, transcendentals=0),
        name="expert",
    )(
        *blocks,
        pick,
        gate_up_s,
        down_s,
        pltpu.with_memory_space_constraint(gate_up_w, pltpu.VMEM),
        pltpu.with_memory_space_constraint(down_w, pltpu.VMEM),
    )


def step_kernel(plan, *refs):
    *terms, out = refs
    for first, rows, places in plan:
        for column in range(0, out.shape[1], WIDTH_CHUNK):
            columns = slice(column, column + WIDTH_CHUNK)
            total = 0.0
            for number, start in places:
                total += terms[number][start : start + rows, columns].astype(jnp.float32)
            out[first : first + rows, columns] = total.astype(jnp.bfloat16)


def step_sum(*segments):
    arrays, plan, height = [], [], 0
    for rows, terms in segments:
        places = []
        for array, start in terms:
            number = next((i for i, known in enumerate(arrays) if known is array), len(arrays))
            if number == len(arrays):
                arrays.append(array)
            places.append((number, start))
        plan.append((height, rows, tuple(places)))
        height += rows
    return pl.pallas_call(
        functools.partial(step_kernel, tuple(plan)),
        in_specs=[VMEM] * len(arrays),
        out_specs=VMEM,
        out_shape=jax.ShapeDtypeStruct((height, arrays[0].shape[1]), jnp.bfloat16),
        compiler_params=limits(4),
        name="step_sum",
    )(*arrays)


def split_kernel(*refs):
    *terms, first, second = refs
    half = first.shape[0]
    for out, start in ((first, 0), (second, half)):
        for column in range(0, out.shape[1], WIDTH_CHUNK):
            columns = slice(column, column + WIDTH_CHUNK)
            total = 0.0
            for term in terms:
                total += term[start : start + half, columns].astype(jnp.float32)
            out[:, columns] = total.astype(jnp.bfloat16)


def split_sum(*terms):
    rows, width = terms[0].shape
    return pl.pallas_call(
        split_kernel,
        in_specs=[VMEM] * len(terms),
        out_specs=[VMEM] * 2,
        out_shape=[jax.ShapeDtypeStruct((rows // 2, width), jnp.bfloat16)] * 2,
        compiler_params=limits(4),
        name="split_sum",
    )(*terms)


def join_kernel(same, cross, long, short):
    half = same.shape[0] // 2
    for block, first in ((long, 0), (short, half)):
        block[:half] = same[first : first + half]
        block[half:] = cross[first : first + half]


def join(same, cross):
    return pl.pallas_call(
        join_kernel,
        in_specs=[VMEM] * 2,
        out_specs=[VMEM] * 2,
        out_shape=[jax.ShapeDtypeStruct(same.shape, same.dtype)] * 2,
        compiler_params=limits(2),
        name="join",
    )(same, cross)


def last_kernel(core, mine, theirs, *refs):
    *arrived, out = refs
    half = out.shape[0] // 2
    for which, place in ((0, core[0]), (1, 1 - core[0])):
        there = pl.ds(pl.multiple_of(place * half, half), half)
        here = slice(which * half, (which + 1) * half)
        for column in range(0, out.shape[1], WIDTH_CHUNK):
            columns = slice(column, column + WIDTH_CHUNK)
            total = mine[here, columns].astype(jnp.float32) + theirs[here, columns].astype(jnp.float32)
            for ref in arrived[2 * which : 2 * which + 2]:
                total += ref[:, columns].astype(jnp.float32)
            out[there, columns] = total.astype(jnp.bfloat16)


def last_sum(core, mine, theirs, *arrived):
    return pl.pallas_call(
        last_kernel,
        in_specs=[SMEM] + [VMEM] * (2 + len(arrived)),
        out_specs=VMEM,
        out_shape=jax.ShapeDtypeStruct(mine.shape, jnp.bfloat16),
        compiler_params=limits(4),
        name="last_sum",
    )(core, mine, theirs, *arrived)


def together(*values):
    return lax.optimization_barrier(values)


def after(value, *others):
    return together(value, *others)[0] if others else value


def body(tokens, routes, gate_num, gate_up_q, gate_up_scale, down_q, down_scale):
    devices = lax.axis_size("expert")
    expert = lax.axis_index("expert")
    chips = devices // 2
    reach = chips // 2
    rows, width = tokens.shape
    half = rows // 2
    ring = ring_of(chips)

    def hop(shift, cross):
        pairs = []
        for place in range(chips):
            for core, way in ((0, shift), (1, -shift)):
                to = ring[(place + way) % chips]
                pairs.append((2 * ring[place] + core, 2 * to + (core ^ cross)))
        return pairs

    on, to_other, back_to_other = hop(1, 0), hop(-1, 1), hop(1, 1)
    swap = [(i, i ^ 1) for i in range(devices)]

    def send(x, perm, name):
        with jax.named_scope(name):
            return lax.ppermute(x, "expert", perm)

    lane = jnp.arange(LANES, dtype=jnp.int32)
    pick = jnp.where(lane == expert, 256.0, jnp.where(lane == devices + expert, 1.0, 0.0))
    pick = pick.astype(jnp.float32)[None, :]
    core = (expert & 1).astype(jnp.int32)[None]
    gate_up_w, down_w = keep(gate_up_q[0], down_q[0])
    weights = (pick, gate_up_w, gate_up_scale, down_w, down_scale)

    kept, given = {}, {}

    def run(items, tie, hint=2):
        halves = [after(blocks[item], *tie) for item in items]
        others = [send(x, swap, f"swap_in_{item[0]}") for x, item in zip(halves, items)]
        outs = expert_part([*others, *halves], [x.shape[0] for x in halves] * 2, hint, *weights)
        for number, (distance, name) in enumerate(items):
            kept[distance, name] = outs[number]
            given[distance, name] = send(outs[len(items) + number], swap, f"swap_out_{distance}")
        return outs[:1]

    own, own_for_other = pack(core, tokens, routes, gate_num, devices)
    other = send(own, swap, "swap_in_0")
    kept[0], cut = expert_part([own, other], (rows, rows), 2, *weights)
    given[0] = send(cut, swap, "swap_out_0")
    same, cross = send(own, on, "gather_long_1"), send(own_for_other, to_other, "gather_long_1")
    long, short = join(after(same, kept[0]), cross)
    blocks = {(1, "long"): long, (1, "short"): short}
    last = run([(1, "long"), (1, "short")], [kept[0]])
    for distance in range(2, reach):
        tie = last if distance > 2 else []
        long = send(after(long, *tie), on, f"gather_long_{distance}")
        short = send(after(short, *tie), on, f"gather_short_{distance}")
        blocks[distance, "long"], blocks[distance, "short"] = long, short
    blocks[reach, "long"] = send(long, on, f"gather_long_{reach}")

    def step(distance, name, carried):
        terms = [(x, 0) for x in (kept[distance, name], given[distance, name], *carried)]
        total = step_sum((rows, terms))
        return [send(total, on, f"return_{name}_{distance}")], [total]

    def arrive(name, carried):
        terms = (kept[1, name], given[1, name], *carried)
        totals = split_sum(*terms)
        return [send(x, perm, f"return_{name}_1") for x, perm in zip(totals, (back_to_other, on))], totals

    for distance in range(2, reach - 1):
        last = run([(distance, "short")], last)
    run([(reach - 1, "short"), (reach - 1, "long")], last)
    short, totals = step(reach - 1, "short", ())
    run([(reach, "long")], totals, 2)
    given[reach, "long"] = after(given[reach, "long"], *short)
    long, totals = step(reach, "long", ())
    for distance in range(reach - 1, 0, -1):
        if 1 < distance < reach - 1:
            run([(distance, "long")], [])
        if distance > 2:
            short, totals = step(distance - 1, "short", [after(x, *totals) for x in short])
        elif distance == 2:
            short, totals = arrive("short", [after(x, *totals) for x in short])
        if distance > 1:
            long, totals = step(distance, "long", [after(x, *totals) for x in long])
        else:
            long, totals = arrive("long", long)
    short_cross, short_same = short
    long_cross, long_same = long
    return last_sum(core, kept[0], given[0], short_same, long_cross, long_same, short_cross)


def solution(mesh):
    in_specs = (
        P(("groups", "expert"), None),
        P(("groups", "expert"), None),
        P(("groups", "expert"), None),
        P("expert", None, None),
        P("expert", None),
        P("expert", None, None),
        P("expert", None),
    )
    out_specs = P(("groups", "expert"), None)
    return jax.shard_map(body, mesh=mesh, in_specs=in_specs, out_specs=out_specs, check_vma=False)
```

```python
import functools

import jax
import jax.numpy as jnp
from jax import lax
from jax.experimental import pallas as pl
from jax.experimental.pallas import tpu as pltpu
from jax.sharding import PartitionSpec as P

DENOMINATOR = 32768.0
LANES = 128
UNIT_CHUNK = 256
WIDTH_CHUNK = 1024
ANYWHERE = pl.BlockSpec(memory_space=pl.ANY)
VMEM = pl.BlockSpec(memory_space=pltpu.VMEM)
SMEM = pl.BlockSpec(memory_space=pltpu.SMEM)


def ring_of(chips):
    if chips == 8:
        return [0, 2, 4, 6, 7, 5, 3, 1]
    return list(range(chips))


def limits(mebibytes):
    return pltpu.CompilerParams(vmem_limit_bytes=mebibytes << 20)


def pack_kernel(experts, core, tokens, routes, gate_num, own, for_other, routes_here, gate_num_here, digits, sem):
    rows, width = tokens.shape
    half = rows // 2
    halves = []
    for packed, place in ((own, core[0]), (for_other, 1 - core[0])):
        for there, from_place in ((0, place), (half, 1 - place)):
            halves.append((packed, there, pl.ds(pl.multiple_of(from_place * half, half), half)))
    copies = [pltpu.make_async_copy(routes, routes_here, sem.at[0])]
    copies.append(pltpu.make_async_copy(gate_num, gate_num_here, sem.at[1]))
    for number, (packed, there, here) in enumerate(halves):
        target = packed.at[pl.ds(there, half), pl.ds(0, width)]
        copies.append(pltpu.make_async_copy(tokens.at[here], target, sem.at[2 + number]))
    for copy in copies:
        copy.start()
    for copy in copies[:2]:
        copy.wait()

    place = lax.broadcasted_iota(jnp.int32, (LANES, rows), 0)
    expert = jnp.where(place < experts, place, place - experts)
    dense = jnp.zeros((LANES, rows), jnp.int32)
    for pick in range(routes_here.shape[0]):
        choice = slice(pick, pick + 1)
        dense += jnp.where(routes_here[choice] == expert, gate_num_here[choice], 0)
    digit = jnp.where(place < experts, dense >> 8, dense & 255)
    digit = jnp.where(place < 2 * experts, digit, 0)
    digits[...] = digit.astype(jnp.float32).T.astype(jnp.bfloat16)
    for packed, there, here in halves:
        packed[there : there + half, width:] = digits[here]
    for copy in copies[2:]:
        copy.wait()


def pack(core, tokens, routes, gate_num, experts):
    rows, width = tokens.shape
    operands = [pltpu.with_memory_space_constraint(x, pltpu.HBM) for x in (tokens, routes.T, gate_num.T)]
    return pl.pallas_call(
        functools.partial(pack_kernel, experts),
        in_specs=[SMEM] + [ANYWHERE] * 3,
        out_specs=[VMEM] * 2,
        out_shape=[jax.ShapeDtypeStruct((rows, width + LANES), jnp.bfloat16)] * 2,
        scratch_shapes=[pltpu.VMEM(routes.T.shape, jnp.int32)] * 2
        + [pltpu.VMEM((rows, LANES), jnp.bfloat16), pltpu.SemaphoreType.DMA((6,))],
        compiler_params=limits(4),
        name="pack",
    )(core, *operands)


def keep_kernel(gate_up, down, gate_up_here, down_here, sem):
    copies = [
        pltpu.make_async_copy(gate_up, gate_up_here, sem.at[0]),
        pltpu.make_async_copy(down, down_here, sem.at[1]),
    ]
    for copy in copies:
        copy.start()
    for copy in copies:
        copy.wait()


def keep(gate_up_w, down_w):
    return pl.pallas_call(
        keep_kernel,
        in_specs=[ANYWHERE] * 2,
        out_specs=[VMEM] * 2,
        out_shape=[pltpu.VMEM(w.shape, w.dtype) for w in (gate_up_w, down_w)],
        scratch_shapes=[pltpu.SemaphoreType.DMA((2,))],
        compiler_params=limits(1),
        cost_estimate=pl.CostEstimate(
            flops=0, bytes_accessed=2 * (gate_up_w.size + down_w.size), transcendentals=0
        ),
        name="keep",
    )(*(pltpu.with_memory_space_constraint(w, pltpu.HBM) for w in (gate_up_w, down_w)))


def expert_kernel(count, *refs):
    xs = refs[:count]
    pick, gate_up_s, down_s, gate_up, down = refs[count : count + 5]
    outs = refs[count + 5 : -2]
    x, hidden = refs[-2:]
    units, width = down.shape

    at = 0
    for ref in xs:
        x[at : at + ref.shape[0]] = ref[...]
        at += ref.shape[0]
    digits = x[:, width:].astype(jnp.float32)
    weight = jnp.sum(digits * pick[...], axis=1, keepdims=True) / DENOMINATOR

    def unit_step(chunk, carry):
        sides = []
        for side in range(2):
            columns = pl.ds(pl.multiple_of(side * units + chunk * UNIT_CHUNK, UNIT_CHUNK), UNIT_CHUNK)
            part = jnp.dot(x[:, :width], gate_up[:, columns], preferred_element_type=jnp.float32)
            sides.append(part * gate_up_s[:, columns])
        here = pl.ds(pl.multiple_of(chunk * UNIT_CHUNK, UNIT_CHUNK), UNIT_CHUNK)
        hidden[:, here] = (jax.nn.silu(sides[0]) * sides[1]).astype(jnp.bfloat16)
        return carry

    lax.fori_loop(0, units // UNIT_CHUNK, unit_step, 0)

    def width_step(chunk, carry):
        columns = pl.ds(pl.multiple_of(chunk * WIDTH_CHUNK, WIDTH_CHUNK), WIDTH_CHUNK)
        part = jnp.dot(hidden[...], down[:, columns], preferred_element_type=jnp.float32)
        part = (part * down_s[:, columns] * weight).astype(jnp.bfloat16)
        at = 0
        for ref in outs:
            ref[:, columns] = part[at : at + ref.shape[0]]
            at += ref.shape[0]
        return carry

    lax.fori_loop(0, width // WIDTH_CHUNK, width_step, 0)


def expert_part(blocks, out_rows, hint, pick, gate_up_w, gate_up_s, down_w, down_s):
    width, units2 = gate_up_w.shape
    units = down_w.shape[0]
    rows, packed_width = sum(block.shape[0] for block in blocks), blocks[0].shape[1]
    flops = int(hint * 2 * rows * width * (units2 + units))
    return pl.pallas_call(
        functools.partial(expert_kernel, len(blocks)),
        in_specs=[VMEM] * (len(blocks) + 5),
        out_specs=[VMEM] * len(out_rows),
        out_shape=[jax.ShapeDtypeStruct((size, width), jnp.bfloat16) for size in out_rows],
        scratch_shapes=[
            pltpu.VMEM((rows, packed_width), jnp.bfloat16),
            pltpu.VMEM((rows, units), jnp.bfloat16),
        ],
        compiler_params=limits(14),
        cost_estimate=pl.CostEstimate(flops=flops, bytes_accessed=0, transcendentals=0),
        name="expert",
    )(
        *blocks,
        pick,
        gate_up_s,
        down_s,
        pltpu.with_memory_space_constraint(gate_up_w, pltpu.VMEM),
        pltpu.with_memory_space_constraint(down_w, pltpu.VMEM),
    )


def step_kernel(plan, *refs):
    *terms, out = refs
    for first, rows, places in plan:
        for column in range(0, out.shape[1], WIDTH_CHUNK):
            columns = slice(column, column + WIDTH_CHUNK)
            total = 0.0
            for number, start in places:
                total += terms[number][start : start + rows, columns].astype(jnp.float32)
            out[first : first + rows, columns] = total.astype(jnp.bfloat16)


def step_sum(*segments):
    arrays, plan, height = [], [], 0
    for rows, terms in segments:
        places = []
        for array, start in terms:
            number = next((i for i, known in enumerate(arrays) if known is array), len(arrays))
            if number == len(arrays):
                arrays.append(array)
            places.append((number, start))
        plan.append((height, rows, tuple(places)))
        height += rows
    return pl.pallas_call(
        functools.partial(step_kernel, tuple(plan)),
        in_specs=[VMEM] * len(arrays),
        out_specs=VMEM,
        out_shape=jax.ShapeDtypeStruct((height, arrays[0].shape[1]), jnp.bfloat16),
        compiler_params=limits(4),
        name="step_sum",
    )(*arrays)


def split_kernel(*refs):
    *terms, first, second = refs
    half = first.shape[0]
    for out, start in ((first, 0), (second, half)):
        for column in range(0, out.shape[1], WIDTH_CHUNK):
            columns = slice(column, column + WIDTH_CHUNK)
            total = 0.0
            for term in terms:
                total += term[start : start + half, columns].astype(jnp.float32)
            out[:, columns] = total.astype(jnp.bfloat16)


def split_sum(*terms):
    rows, width = terms[0].shape
    return pl.pallas_call(
        split_kernel,
        in_specs=[VMEM] * len(terms),
        out_specs=[VMEM] * 2,
        out_shape=[jax.ShapeDtypeStruct((rows // 2, width), jnp.bfloat16)] * 2,
        compiler_params=limits(4),
        name="split_sum",
    )(*terms)


def join_kernel(same, cross, long, short):
    half = same.shape[0] // 2
    for block, first in ((long, 0), (short, half)):
        block[:half] = same[first : first + half]
        block[half:] = cross[first : first + half]


def join(same, cross):
    return pl.pallas_call(
        join_kernel,
        in_specs=[VMEM] * 2,
        out_specs=[VMEM] * 2,
        out_shape=[jax.ShapeDtypeStruct(same.shape, same.dtype)] * 2,
        compiler_params=limits(2),
        name="join",
    )(same, cross)


def near_kernel(mine, theirs, short_same, short_cross, out):
    half = out.shape[0] // 2
    for which, arrived in enumerate((short_same, short_cross)):
        here = slice(which * half, (which + 1) * half)
        for column in range(0, out.shape[1], WIDTH_CHUNK):
            columns = slice(column, column + WIDTH_CHUNK)
            total = mine[here, columns].astype(jnp.float32) + theirs[here, columns].astype(jnp.float32)
            out[here, columns] = total + arrived[:, columns].astype(jnp.float32)


def near_sum(*terms):
    return pl.pallas_call(
        near_kernel,
        in_specs=[VMEM] * 4,
        out_specs=VMEM,
        out_shape=jax.ShapeDtypeStruct(terms[0].shape, jnp.float32),
        compiler_params=limits(4),
        cost_estimate=pl.CostEstimate(flops=10_000_000_000, bytes_accessed=0, transcendentals=0),
        name="near_sum",
    )(*terms)


def last_kernel(core, near, long_cross, long_same, out, here, sem):
    half = out.shape[0] // 2
    copies = []
    for which, arrived in enumerate((long_cross, long_same)):
        place = core[0] if which == 0 else 1 - core[0]
        there = pl.ds(pl.multiple_of(place * half, half), half)
        from_rows = slice(which * half, (which + 1) * half)
        for chunk in range(0, out.shape[1] // WIDTH_CHUNK):
            columns = slice(chunk * WIDTH_CHUNK, (chunk + 1) * WIDTH_CHUNK)
            total = near[from_rows, columns] + arrived[:, columns].astype(jnp.float32)
            here[from_rows, columns] = total.astype(jnp.bfloat16)
            source = here.at[pl.ds(which * half, half), pl.ds(chunk * WIDTH_CHUNK, WIDTH_CHUNK)]
            target = out.at[there, pl.ds(chunk * WIDTH_CHUNK, WIDTH_CHUNK)]
            copies.append(pltpu.make_async_copy(source, target, sem.at[which, chunk]))
            copies[-1].start()
    for copy in copies:
        copy.wait()


def last_sum(core, near, *arrived):
    rows, width = near.shape
    return pl.pallas_call(
        last_kernel,
        in_specs=[SMEM] + [VMEM] * 3,
        out_specs=ANYWHERE,
        out_shape=jax.ShapeDtypeStruct(near.shape, jnp.bfloat16),
        scratch_shapes=[pltpu.VMEM(near.shape, jnp.bfloat16), pltpu.SemaphoreType.DMA((2, width // WIDTH_CHUNK))],
        compiler_params=limits(4),
        name="last_sum",
    )(core, near, *arrived)


def together(*values):
    return lax.optimization_barrier(values)


def after(value, *others):
    return together(value, *others)[0] if others else value


def body(tokens, routes, gate_num, gate_up_q, gate_up_scale, down_q, down_scale):
    devices = lax.axis_size("expert")
    expert = lax.axis_index("expert")
    chips = devices // 2
    reach = chips // 2
    rows, width = tokens.shape
    half = rows // 2
    ring = ring_of(chips)

    def hop(shift, cross):
        pairs = []
        for place in range(chips):
            for core, way in ((0, shift), (1, -shift)):
                to = ring[(place + way) % chips]
                pairs.append((2 * ring[place] + core, 2 * to + (core ^ cross)))
        return pairs

    on, to_other, back_to_other = hop(1, 0), hop(-1, 1), hop(1, 1)
    swap = [(i, i ^ 1) for i in range(devices)]

    def send(x, perm, name):
        with jax.named_scope(name):
            return lax.ppermute(x, "expert", perm)

    lane = jnp.arange(LANES, dtype=jnp.int32)
    pick = jnp.where(lane == expert, 256.0, jnp.where(lane == devices + expert, 1.0, 0.0))
    pick = pick.astype(jnp.float32)[None, :]
    core = (expert & 1).astype(jnp.int32)[None]
    gate_up_w, down_w = keep(gate_up_q[0], down_q[0])
    weights = (pick, gate_up_w, gate_up_scale, down_w, down_scale)

    kept, given = {}, {}

    def run(items, tie, hint=2):
        halves = [after(blocks[item], *tie) for item in items]
        others = [send(x, swap, f"swap_in_{item[0]}") for x, item in zip(halves, items)]
        outs = expert_part([*others, *halves], [x.shape[0] for x in halves] * 2, hint, *weights)
        for number, (distance, name) in enumerate(items):
            kept[distance, name] = outs[number]
            given[distance, name] = send(outs[len(items) + number], swap, f"swap_out_{distance}")
        return outs[:1]

    own, own_for_other = pack(core, tokens, routes, gate_num, devices)
    other = send(own, swap, "swap_in_0")
    kept[0], cut = expert_part([own, other], (rows, rows), 2, *weights)
    given[0] = send(cut, swap, "swap_out_0")
    same, cross = send(own, on, "gather_long_1"), send(own_for_other, to_other, "gather_long_1")
    long, short = join(after(same, kept[0]), cross)
    blocks = {(1, "long"): long, (1, "short"): short}
    last = run([(1, "long"), (1, "short")], [kept[0]])
    for distance in range(2, reach):
        tie = last if distance > 2 else []
        long = send(after(long, *tie), on, f"gather_long_{distance}")
        short = send(after(short, *tie), on, f"gather_short_{distance}")
        blocks[distance, "long"], blocks[distance, "short"] = long, short
    blocks[reach, "long"] = send(long, on, f"gather_long_{reach}")

    def step(distance, name, carried):
        terms = [(x, 0) for x in (kept[distance, name], given[distance, name], *carried)]
        total = step_sum((rows, terms))
        return [send(total, on, f"return_{name}_{distance}")], [total]

    def arrive(name, carried):
        terms = (kept[1, name], given[1, name], *carried)
        totals = split_sum(*terms)
        return [send(x, perm, f"return_{name}_1") for x, perm in zip(totals, (back_to_other, on))], totals

    for distance in range(2, reach - 1):
        last = run([(distance, "short")], last)
    run([(reach - 1, "short")], last)
    short, totals = step(reach - 1, "short", ())
    run([(reach, "long"), (reach - 1, "long")], totals)
    given[reach, "long"] = after(given[reach, "long"], *short)
    long, totals = step(reach, "long", ())
    for distance in range(reach - 1, 0, -1):
        if 1 < distance < reach - 1:
            run([(distance, "long")], [])
        if distance > 2:
            short, totals = step(distance - 1, "short", [after(x, *totals) for x in short])
        elif distance == 2:
            short, totals = arrive("short", [after(x, *totals) for x in short])
        if distance > 1:
            long, totals = step(distance, "long", [after(x, *totals) for x in long])
        else:
            short_cross, short_same = short
            near = near_sum(kept[0], given[0], short_same, short_cross)
            long, totals = arrive("long", [after(x, near) for x in long])
    long_cross, long_same = long
    return last_sum(core, near, long_cross, long_same)


def solution(mesh):
    in_specs = (
        P(("groups", "expert"), None),
        P(("groups", "expert"), None),
        P(("groups", "expert"), None),
        P("expert", None, None),
        P("expert", None),
        P("expert", None, None),
        P("expert", None),
    )
    out_specs = P(("groups", "expert"), None)
    return jax.shard_map(body, mesh=mesh, in_specs=in_specs, out_specs=out_specs, check_vma=False)
```

```python
import functools

import jax
import jax.numpy as jnp
from jax import lax
from jax.experimental import pallas as pl
from jax.experimental.pallas import tpu as pltpu
from jax.sharding import PartitionSpec as P

DENOMINATOR = 32768.0
LANES = 128
UNIT_CHUNK = 256
WIDTH_CHUNK = 1024
ANYWHERE = pl.BlockSpec(memory_space=pl.ANY)
VMEM = pl.BlockSpec(memory_space=pltpu.VMEM)
SMEM = pl.BlockSpec(memory_space=pltpu.SMEM)


def ring_of(chips):
    if chips == 8:
        return [0, 2, 4, 6, 7, 5, 3, 1]
    return list(range(chips))


def limits(mebibytes):
    return pltpu.CompilerParams(vmem_limit_bytes=mebibytes << 20)


def pack_kernel(experts, core, tokens, routes, gate_num, own, for_other, routes_here, gate_num_here, digits, sem):
    rows, width = tokens.shape
    half = rows // 2
    halves = []
    for packed, place in ((own, core[0]), (for_other, 1 - core[0])):
        for there, from_place in ((0, place), (half, 1 - place)):
            halves.append((packed, there, pl.ds(pl.multiple_of(from_place * half, half), half)))
    copies = [pltpu.make_async_copy(routes, routes_here, sem.at[0])]
    copies.append(pltpu.make_async_copy(gate_num, gate_num_here, sem.at[1]))
    for number, (packed, there, here) in enumerate(halves):
        target = packed.at[pl.ds(there, half), pl.ds(0, width)]
        copies.append(pltpu.make_async_copy(tokens.at[here], target, sem.at[2 + number]))
    for copy in copies:
        copy.start()
    for copy in copies[:2]:
        copy.wait()

    place = lax.broadcasted_iota(jnp.int32, (LANES, rows), 0)
    expert = jnp.where(place < experts, place, place - experts)
    dense = jnp.zeros((LANES, rows), jnp.int32)
    for pick in range(routes_here.shape[0]):
        choice = slice(pick, pick + 1)
        dense += jnp.where(routes_here[choice] == expert, gate_num_here[choice], 0)
    digit = jnp.where(place < experts, dense >> 8, dense & 255)
    digit = jnp.where(place < 2 * experts, digit, 0)
    digits[...] = digit.astype(jnp.float32).T.astype(jnp.bfloat16)
    for packed, there, here in halves:
        packed[there : there + half, width:] = digits[here]
    for copy in copies[2:]:
        copy.wait()


def pack(core, tokens, routes, gate_num, experts):
    rows, width = tokens.shape
    operands = [pltpu.with_memory_space_constraint(x, pltpu.HBM) for x in (tokens, routes.T, gate_num.T)]
    return pl.pallas_call(
        functools.partial(pack_kernel, experts),
        in_specs=[SMEM] + [ANYWHERE] * 3,
        out_specs=[VMEM] * 2,
        out_shape=[jax.ShapeDtypeStruct((rows, width + LANES), jnp.bfloat16)] * 2,
        scratch_shapes=[pltpu.VMEM(routes.T.shape, jnp.int32)] * 2
        + [pltpu.VMEM((rows, LANES), jnp.bfloat16), pltpu.SemaphoreType.DMA((6,))],
        compiler_params=limits(4),
        name="pack",
    )(core, *operands)


def keep_kernel(gate_up, down, gate_up_here, down_here, sem):
    copies = [
        pltpu.make_async_copy(gate_up, gate_up_here, sem.at[0]),
        pltpu.make_async_copy(down, down_here, sem.at[1]),
    ]
    for copy in copies:
        copy.start()
    for copy in copies:
        copy.wait()


def keep(gate_up_w, down_w):
    return pl.pallas_call(
        keep_kernel,
        in_specs=[ANYWHERE] * 2,
        out_specs=[VMEM] * 2,
        out_shape=[pltpu.VMEM(w.shape, w.dtype) for w in (gate_up_w, down_w)],
        scratch_shapes=[pltpu.SemaphoreType.DMA((2,))],
        compiler_params=limits(1),
        cost_estimate=pl.CostEstimate(
            flops=0, bytes_accessed=2 * (gate_up_w.size + down_w.size), transcendentals=0
        ),
        name="keep",
    )(*(pltpu.with_memory_space_constraint(w, pltpu.HBM) for w in (gate_up_w, down_w)))


def expert_kernel(count, *refs):
    xs = refs[:count]
    pick, gate_up_s, down_s, gate_up, down = refs[count : count + 5]
    outs = refs[count + 5 : -2]
    x, hidden = refs[-2:]
    units, width = down.shape

    at = 0
    for ref in xs:
        x[at : at + ref.shape[0]] = ref[...]
        at += ref.shape[0]
    digits = x[:, width:].astype(jnp.float32)
    weight = jnp.sum(digits * pick[...], axis=1, keepdims=True) / DENOMINATOR

    def unit_step(chunk, carry):
        sides = []
        for side in range(2):
            columns = pl.ds(pl.multiple_of(side * units + chunk * UNIT_CHUNK, UNIT_CHUNK), UNIT_CHUNK)
            part = jnp.dot(x[:, :width], gate_up[:, columns], preferred_element_type=jnp.float32)
            sides.append(part * gate_up_s[:, columns])
        here = pl.ds(pl.multiple_of(chunk * UNIT_CHUNK, UNIT_CHUNK), UNIT_CHUNK)
        hidden[:, here] = (jax.nn.silu(sides[0]) * sides[1]).astype(jnp.bfloat16)
        return carry

    lax.fori_loop(0, units // UNIT_CHUNK, unit_step, 0)

    def width_step(chunk, carry):
        columns = pl.ds(pl.multiple_of(chunk * WIDTH_CHUNK, WIDTH_CHUNK), WIDTH_CHUNK)
        part = jnp.dot(hidden[...], down[:, columns], preferred_element_type=jnp.float32)
        part = (part * down_s[:, columns] * weight).astype(jnp.bfloat16)
        at = 0
        for ref in outs:
            ref[:, columns] = part[at : at + ref.shape[0]]
            at += ref.shape[0]
        return carry

    lax.fori_loop(0, width // WIDTH_CHUNK, width_step, 0)


def expert_part(blocks, out_rows, hint, pick, gate_up_w, gate_up_s, down_w, down_s):
    width, units2 = gate_up_w.shape
    units = down_w.shape[0]
    rows, packed_width = sum(block.shape[0] for block in blocks), blocks[0].shape[1]
    flops = int(hint * 2 * rows * width * (units2 + units))
    return pl.pallas_call(
        functools.partial(expert_kernel, len(blocks)),
        in_specs=[VMEM] * (len(blocks) + 5),
        out_specs=[VMEM] * len(out_rows),
        out_shape=[jax.ShapeDtypeStruct((size, width), jnp.bfloat16) for size in out_rows],
        scratch_shapes=[
            pltpu.VMEM((rows, packed_width), jnp.bfloat16),
            pltpu.VMEM((rows, units), jnp.bfloat16),
        ],
        compiler_params=limits(14),
        cost_estimate=pl.CostEstimate(flops=flops, bytes_accessed=0, transcendentals=0),
        name="expert",
    )(
        *blocks,
        pick,
        gate_up_s,
        down_s,
        pltpu.with_memory_space_constraint(gate_up_w, pltpu.VMEM),
        pltpu.with_memory_space_constraint(down_w, pltpu.VMEM),
    )


def step_kernel(plan, *refs):
    *terms, out = refs
    for first, rows, places in plan:
        for column in range(0, out.shape[1], WIDTH_CHUNK):
            columns = slice(column, column + WIDTH_CHUNK)
            total = 0.0
            for number, start in places:
                total += terms[number][start : start + rows, columns].astype(jnp.float32)
            out[first : first + rows, columns] = total.astype(jnp.bfloat16)


def step_sum(*segments):
    arrays, plan, height = [], [], 0
    for rows, terms in segments:
        places = []
        for array, start in terms:
            number = next((i for i, known in enumerate(arrays) if known is array), len(arrays))
            if number == len(arrays):
                arrays.append(array)
            places.append((number, start))
        plan.append((height, rows, tuple(places)))
        height += rows
    return pl.pallas_call(
        functools.partial(step_kernel, tuple(plan)),
        in_specs=[VMEM] * len(arrays),
        out_specs=VMEM,
        out_shape=jax.ShapeDtypeStruct((height, arrays[0].shape[1]), jnp.bfloat16),
        compiler_params=limits(4),
        name="step_sum",
    )(*arrays)


def split_kernel(*refs):
    *terms, first, second = refs
    half = first.shape[0]
    for out, start in ((first, 0), (second, half)):
        for column in range(0, out.shape[1], WIDTH_CHUNK):
            columns = slice(column, column + WIDTH_CHUNK)
            total = 0.0
            for term in terms:
                total += term[start : start + half, columns].astype(jnp.float32)
            out[:, columns] = total.astype(jnp.bfloat16)


def split_sum(*terms):
    rows, width = terms[0].shape
    return pl.pallas_call(
        split_kernel,
        in_specs=[VMEM] * len(terms),
        out_specs=[VMEM] * 2,
        out_shape=[jax.ShapeDtypeStruct((rows // 2, width), jnp.bfloat16)] * 2,
        compiler_params=limits(4),
        name="split_sum",
    )(*terms)


def join_kernel(same, cross, long, short):
    half = same.shape[0] // 2
    for block, first in ((long, 0), (short, half)):
        block[:half] = same[first : first + half]
        block[half:] = cross[first : first + half]


def join(same, cross):
    return pl.pallas_call(
        join_kernel,
        in_specs=[VMEM] * 2,
        out_specs=[VMEM] * 2,
        out_shape=[jax.ShapeDtypeStruct(same.shape, same.dtype)] * 2,
        compiler_params=limits(2),
        name="join",
    )(same, cross)


def near_kernel(mine, theirs, short_same, short_cross, out):
    half = out.shape[0] // 2
    for which, arrived in enumerate((short_same, short_cross)):
        here = slice(which * half, (which + 1) * half)
        for column in range(0, out.shape[1], WIDTH_CHUNK):
            columns = slice(column, column + WIDTH_CHUNK)
            total = mine[here, columns].astype(jnp.float32) + theirs[here, columns].astype(jnp.float32)
            out[here, columns] = total + arrived[:, columns].astype(jnp.float32)


def near_sum(*terms):
    return pl.pallas_call(
        near_kernel,
        in_specs=[VMEM] * 4,
        out_specs=VMEM,
        out_shape=jax.ShapeDtypeStruct(terms[0].shape, jnp.float32),
        compiler_params=limits(4),
        cost_estimate=pl.CostEstimate(flops=10_000_000_000, bytes_accessed=0, transcendentals=0),
        name="near_sum",
    )(*terms)


def last_kernel(core, near, long_cross, long_same, out, here, sem):
    half = out.shape[0] // 2
    copies = []
    for which, arrived in enumerate((long_cross, long_same)):
        place = core[0] if which == 0 else 1 - core[0]
        there = pl.ds(pl.multiple_of(place * half, half), half)
        from_rows = slice(which * half, (which + 1) * half)
        for chunk in range(0, out.shape[1] // WIDTH_CHUNK):
            columns = slice(chunk * WIDTH_CHUNK, (chunk + 1) * WIDTH_CHUNK)
            total = near[from_rows, columns] + arrived[:, columns].astype(jnp.float32)
            here[from_rows, columns] = total.astype(jnp.bfloat16)
            source = here.at[pl.ds(which * half, half), pl.ds(chunk * WIDTH_CHUNK, WIDTH_CHUNK)]
            target = out.at[there, pl.ds(chunk * WIDTH_CHUNK, WIDTH_CHUNK)]
            copies.append(pltpu.make_async_copy(source, target, sem.at[which, chunk]))
            copies[-1].start()
    for copy in copies:
        copy.wait()


def last_sum(core, near, *arrived):
    rows, width = near.shape
    return pl.pallas_call(
        last_kernel,
        in_specs=[SMEM] + [VMEM] * 3,
        out_specs=ANYWHERE,
        out_shape=jax.ShapeDtypeStruct(near.shape, jnp.bfloat16),
        scratch_shapes=[pltpu.VMEM(near.shape, jnp.bfloat16), pltpu.SemaphoreType.DMA((2, width // WIDTH_CHUNK))],
        compiler_params=limits(4),
        name="last_sum",
    )(core, near, *arrived)


def together(*values):
    return lax.optimization_barrier(values)


def after(value, *others):
    return together(value, *others)[0] if others else value


def body(tokens, routes, gate_num, gate_up_q, gate_up_scale, down_q, down_scale):
    devices = lax.axis_size("expert")
    expert = lax.axis_index("expert")
    chips = devices // 2
    reach = chips // 2
    rows, width = tokens.shape
    half = rows // 2
    ring = ring_of(chips)

    def hop(shift, cross):
        pairs = []
        for place in range(chips):
            for core, way in ((0, shift), (1, -shift)):
                to = ring[(place + way) % chips]
                pairs.append((2 * ring[place] + core, 2 * to + (core ^ cross)))
        return pairs

    on, to_other, back_to_other = hop(1, 0), hop(-1, 1), hop(1, 1)
    swap = [(i, i ^ 1) for i in range(devices)]

    def send(x, perm, name):
        with jax.named_scope(name):
            return lax.ppermute(x, "expert", perm)

    lane = jnp.arange(LANES, dtype=jnp.int32)
    pick = jnp.where(lane == expert, 256.0, jnp.where(lane == devices + expert, 1.0, 0.0))
    pick = pick.astype(jnp.float32)[None, :]
    core = (expert & 1).astype(jnp.int32)[None]
    gate_up_w, down_w = keep(gate_up_q[0], down_q[0])
    weights = (pick, gate_up_w, gate_up_scale, down_w, down_scale)

    kept, given = {}, {}

    def run(items, tie, hint=2):
        halves = [after(blocks[item], *tie) for item in items]
        others = [send(x, swap, f"swap_in_{item[0]}") for x, item in zip(halves, items)]
        outs = expert_part([*others, *halves], [x.shape[0] for x in halves] * 2, hint, *weights)
        for number, (distance, name) in enumerate(items):
            kept[distance, name] = outs[number]
            given[distance, name] = send(outs[len(items) + number], swap, f"swap_out_{distance}")
        return outs[:1]

    own, own_for_other = pack(core, tokens, routes, gate_num, devices)
    other = send(own, swap, "swap_in_0")
    kept[0], cut = expert_part([own, other], (rows, rows), 2, *weights)
    given[0] = send(cut, swap, "swap_out_0")
    same, cross = send(own, on, "gather_long_1"), send(own_for_other, to_other, "gather_long_1")
    long, short = join(after(same, kept[0]), cross)
    blocks = {(1, "long"): long, (1, "short"): short}
    last = run([(1, "long"), (1, "short")], [kept[0]])
    for distance in range(2, reach):
        tie = last if distance > 2 else []
        long = send(after(long, *tie), on, f"gather_long_{distance}")
        short = send(after(short, *tie), on, f"gather_short_{distance}")
        blocks[distance, "long"], blocks[distance, "short"] = long, short
    blocks[reach, "long"] = send(long, on, f"gather_long_{reach}")

    def step(distance, name, carried):
        terms = [(x, 0) for x in (kept[distance, name], given[distance, name], *carried)]
        total = step_sum((rows, terms))
        return [send(total, on, f"return_{name}_{distance}")], [total]

    def arrive(name, carried):
        terms = (kept[1, name], given[1, name], *carried)
        totals = split_sum(*terms)
        return [send(x, perm, f"return_{name}_1") for x, perm in zip(totals, (back_to_other, on))], totals

    for distance in range(2, reach - 1):
        last = run([(distance, "short")], last)
    run([(reach - 1, "short")], last, 2)
    second = run([(reach - 1, "long")], last, 2)
    short, totals = step(reach - 1, "short", ())
    run([(reach, "long")], [*totals, *second])
    given[reach, "long"] = after(given[reach, "long"], *short)
    long, totals = step(reach, "long", ())
    for distance in range(reach - 1, 0, -1):
        if 1 < distance < reach - 1:
            run([(distance, "long")], [])
        if distance > 2:
            short, totals = step(distance - 1, "short", [after(x, *totals) for x in short])
        elif distance == 2:
            short, totals = arrive("short", [after(x, *totals) for x in short])
        if distance > 1:
            long, totals = step(distance, "long", [after(x, *totals) for x in long])
        else:
            short_cross, short_same = short
            near = near_sum(kept[0], given[0], short_same, short_cross)
            long, totals = arrive("long", [after(x, near) for x in long])
    long_cross, long_same = long
    return last_sum(core, near, long_cross, long_same)


def solution(mesh):
    in_specs = (
        P(("groups", "expert"), None),
        P(("groups", "expert"), None),
        P(("groups", "expert"), None),
        P("expert", None, None),
        P("expert", None),
        P("expert", None, None),
        P("expert", None),
    )
    out_specs = P(("groups", "expert"), None)
    return jax.shard_map(body, mesh=mesh, in_specs=in_specs, out_specs=out_specs, check_vma=False)
```

```python
import functools

import jax
import jax.numpy as jnp
from jax import lax
from jax.experimental import pallas as pl
from jax.experimental.pallas import tpu as pltpu
from jax.sharding import PartitionSpec as P

DENOMINATOR = 32768.0
LANES = 128
UNIT_CHUNK = 256
WIDTH_CHUNK = 1024
ANYWHERE = pl.BlockSpec(memory_space=pl.ANY)
VMEM = pl.BlockSpec(memory_space=pltpu.VMEM)
SMEM = pl.BlockSpec(memory_space=pltpu.SMEM)


def ring_of(chips):
    if chips == 8:
        return [0, 2, 4, 6, 7, 5, 3, 1]
    return list(range(chips))


def limits(mebibytes):
    return pltpu.CompilerParams(vmem_limit_bytes=mebibytes << 20)


def pack_kernel(experts, core, tokens, routes, gate_num, own, for_other, routes_here, gate_num_here, digits, sem):
    rows, width = tokens.shape
    half = rows // 2
    halves = []
    for packed, place in ((own, core[0]), (for_other, 1 - core[0])):
        for there, from_place in ((0, place), (half, 1 - place)):
            halves.append((packed, there, pl.ds(pl.multiple_of(from_place * half, half), half)))
    copies = [pltpu.make_async_copy(routes, routes_here, sem.at[0])]
    copies.append(pltpu.make_async_copy(gate_num, gate_num_here, sem.at[1]))
    for number, (packed, there, here) in enumerate(halves):
        target = packed.at[pl.ds(there, half), pl.ds(0, width)]
        copies.append(pltpu.make_async_copy(tokens.at[here], target, sem.at[2 + number]))
    for copy in copies:
        copy.start()
    for copy in copies[:2]:
        copy.wait()

    place = lax.broadcasted_iota(jnp.int32, (LANES, rows), 0)
    expert = jnp.where(place < experts, place, place - experts)
    dense = jnp.zeros((LANES, rows), jnp.int32)
    for pick in range(routes_here.shape[0]):
        choice = slice(pick, pick + 1)
        dense += jnp.where(routes_here[choice] == expert, gate_num_here[choice], 0)
    digit = jnp.where(place < experts, dense >> 8, dense & 255)
    digit = jnp.where(place < 2 * experts, digit, 0)
    digits[...] = digit.astype(jnp.float32).T.astype(jnp.bfloat16)
    for packed, there, here in halves:
        packed[there : there + half, width:] = digits[here]
    for copy in copies[2:]:
        copy.wait()


def pack(core, tokens, routes, gate_num, experts):
    rows, width = tokens.shape
    operands = [pltpu.with_memory_space_constraint(x, pltpu.HBM) for x in (tokens, routes.T, gate_num.T)]
    return pl.pallas_call(
        functools.partial(pack_kernel, experts),
        in_specs=[SMEM] + [ANYWHERE] * 3,
        out_specs=[VMEM] * 2,
        out_shape=[jax.ShapeDtypeStruct((rows, width + LANES), jnp.bfloat16)] * 2,
        scratch_shapes=[pltpu.VMEM(routes.T.shape, jnp.int32)] * 2
        + [pltpu.VMEM((rows, LANES), jnp.bfloat16), pltpu.SemaphoreType.DMA((6,))],
        compiler_params=limits(4),
        name="pack",
    )(core, *operands)


def keep_kernel(gate_up, down, gate_up_here, down_here, sem):
    copies = [
        pltpu.make_async_copy(gate_up, gate_up_here, sem.at[0]),
        pltpu.make_async_copy(down, down_here, sem.at[1]),
    ]
    for copy in copies:
        copy.start()
    for copy in copies:
        copy.wait()


def keep(gate_up_w, down_w):
    return pl.pallas_call(
        keep_kernel,
        in_specs=[ANYWHERE] * 2,
        out_specs=[VMEM] * 2,
        out_shape=[pltpu.VMEM(w.shape, w.dtype) for w in (gate_up_w, down_w)],
        scratch_shapes=[pltpu.SemaphoreType.DMA((2,))],
        compiler_params=limits(1),
        cost_estimate=pl.CostEstimate(
            flops=0, bytes_accessed=2 * (gate_up_w.size + down_w.size), transcendentals=0
        ),
        name="keep",
    )(*(pltpu.with_memory_space_constraint(w, pltpu.HBM) for w in (gate_up_w, down_w)))


def expert_kernel(count, *refs):
    xs = refs[:count]
    pick, gate_up_s, down_s, gate_up, down = refs[count : count + 5]
    outs = refs[count + 5 : -2]
    x, hidden = refs[-2:]
    units, width = down.shape

    at = 0
    for ref in xs:
        x[at : at + ref.shape[0]] = ref[...]
        at += ref.shape[0]
    digits = x[:, width:].astype(jnp.float32)
    weight = jnp.sum(digits * pick[...], axis=1, keepdims=True) / DENOMINATOR

    def unit_step(chunk, carry):
        sides = []
        for side in range(2):
            columns = pl.ds(pl.multiple_of(side * units + chunk * UNIT_CHUNK, UNIT_CHUNK), UNIT_CHUNK)
            part = jnp.dot(x[:, :width], gate_up[:, columns], preferred_element_type=jnp.float32)
            sides.append(part * gate_up_s[:, columns])
        here = pl.ds(pl.multiple_of(chunk * UNIT_CHUNK, UNIT_CHUNK), UNIT_CHUNK)
        hidden[:, here] = (jax.nn.silu(sides[0]) * sides[1]).astype(jnp.bfloat16)
        return carry

    lax.fori_loop(0, units // UNIT_CHUNK, unit_step, 0, unroll=True)

    def width_step(chunk, carry):
        columns = pl.ds(pl.multiple_of(chunk * WIDTH_CHUNK, WIDTH_CHUNK), WIDTH_CHUNK)
        part = jnp.dot(hidden[...], down[:, columns], preferred_element_type=jnp.float32)
        part = (part * down_s[:, columns] * weight).astype(jnp.bfloat16)
        at = 0
        for ref in outs:
            ref[:, columns] = part[at : at + ref.shape[0]]
            at += ref.shape[0]
        return carry

    lax.fori_loop(0, width // WIDTH_CHUNK, width_step, 0, unroll=True)


def expert_part(blocks, out_rows, hint, pick, gate_up_w, gate_up_s, down_w, down_s):
    width, units2 = gate_up_w.shape
    units = down_w.shape[0]
    rows, packed_width = sum(block.shape[0] for block in blocks), blocks[0].shape[1]
    flops = int(hint * 2 * rows * width * (units2 + units))
    return pl.pallas_call(
        functools.partial(expert_kernel, len(blocks)),
        in_specs=[VMEM] * (len(blocks) + 5),
        out_specs=[VMEM] * len(out_rows),
        out_shape=[jax.ShapeDtypeStruct((size, width), jnp.bfloat16) for size in out_rows],
        scratch_shapes=[
            pltpu.VMEM((rows, packed_width), jnp.bfloat16),
            pltpu.VMEM((rows, units), jnp.bfloat16),
        ],
        compiler_params=limits(14),
        cost_estimate=pl.CostEstimate(flops=flops, bytes_accessed=0, transcendentals=0),
        name="expert",
    )(
        *blocks,
        pick,
        gate_up_s,
        down_s,
        pltpu.with_memory_space_constraint(gate_up_w, pltpu.VMEM),
        pltpu.with_memory_space_constraint(down_w, pltpu.VMEM),
    )


def step_kernel(plan, *refs):
    *terms, out = refs
    for first, rows, places in plan:
        for column in range(0, out.shape[1], WIDTH_CHUNK):
            columns = slice(column, column + WIDTH_CHUNK)
            total = 0.0
            for number, start in places:
                total += terms[number][start : start + rows, columns].astype(jnp.float32)
            out[first : first + rows, columns] = total.astype(jnp.bfloat16)


def step_sum(*segments):
    arrays, plan, height = [], [], 0
    for rows, terms in segments:
        places = []
        for array, start in terms:
            number = next((i for i, known in enumerate(arrays) if known is array), len(arrays))
            if number == len(arrays):
                arrays.append(array)
            places.append((number, start))
        plan.append((height, rows, tuple(places)))
        height += rows
    return pl.pallas_call(
        functools.partial(step_kernel, tuple(plan)),
        in_specs=[VMEM] * len(arrays),
        out_specs=VMEM,
        out_shape=jax.ShapeDtypeStruct((height, arrays[0].shape[1]), jnp.bfloat16),
        compiler_params=limits(4),
        name="step_sum",
    )(*arrays)


def split_kernel(*refs):
    *terms, first, second = refs
    half = first.shape[0]
    for out, start in ((first, 0), (second, half)):
        for column in range(0, out.shape[1], WIDTH_CHUNK):
            columns = slice(column, column + WIDTH_CHUNK)
            total = 0.0
            for term in terms:
                total += term[start : start + half, columns].astype(jnp.float32)
            out[:, columns] = total.astype(jnp.bfloat16)


def split_sum(*terms):
    rows, width = terms[0].shape
    return pl.pallas_call(
        split_kernel,
        in_specs=[VMEM] * len(terms),
        out_specs=[VMEM] * 2,
        out_shape=[jax.ShapeDtypeStruct((rows // 2, width), jnp.bfloat16)] * 2,
        compiler_params=limits(4),
        name="split_sum",
    )(*terms)


def join_kernel(same, cross, long, short):
    half = same.shape[0] // 2
    for block, first in ((long, 0), (short, half)):
        block[:half] = same[first : first + half]
        block[half:] = cross[first : first + half]


def join(same, cross):
    return pl.pallas_call(
        join_kernel,
        in_specs=[VMEM] * 2,
        out_specs=[VMEM] * 2,
        out_shape=[jax.ShapeDtypeStruct(same.shape, same.dtype)] * 2,
        compiler_params=limits(2),
        name="join",
    )(same, cross)


def near_kernel(mine, theirs, short_same, short_cross, out):
    half = out.shape[0] // 2
    for which, arrived in enumerate((short_same, short_cross)):
        here = slice(which * half, (which + 1) * half)
        for column in range(0, out.shape[1], WIDTH_CHUNK):
            columns = slice(column, column + WIDTH_CHUNK)
            total = mine[here, columns].astype(jnp.float32) + theirs[here, columns].astype(jnp.float32)
            out[here, columns] = total + arrived[:, columns].astype(jnp.float32)


def near_sum(*terms):
    return pl.pallas_call(
        near_kernel,
        in_specs=[VMEM] * 4,
        out_specs=VMEM,
        out_shape=jax.ShapeDtypeStruct(terms[0].shape, jnp.float32),
        compiler_params=limits(4),
        cost_estimate=pl.CostEstimate(flops=10_000_000_000, bytes_accessed=0, transcendentals=0),
        name="near_sum",
    )(*terms)


def last_kernel(core, near, long_cross, long_same, out, here, sem):
    half = out.shape[0] // 2
    copies = []
    for which, arrived in enumerate((long_cross, long_same)):
        place = core[0] if which == 0 else 1 - core[0]
        there = pl.ds(pl.multiple_of(place * half, half), half)
        from_rows = slice(which * half, (which + 1) * half)
        for chunk in range(0, out.shape[1] // WIDTH_CHUNK):
            columns = slice(chunk * WIDTH_CHUNK, (chunk + 1) * WIDTH_CHUNK)
            total = near[from_rows, columns] + arrived[:, columns].astype(jnp.float32)
            here[from_rows, columns] = total.astype(jnp.bfloat16)
            source = here.at[pl.ds(which * half, half), pl.ds(chunk * WIDTH_CHUNK, WIDTH_CHUNK)]
            target = out.at[there, pl.ds(chunk * WIDTH_CHUNK, WIDTH_CHUNK)]
            copies.append(pltpu.make_async_copy(source, target, sem.at[which, chunk]))
            copies[-1].start()
    for copy in copies:
        copy.wait()


def last_sum(core, near, *arrived):
    rows, width = near.shape
    return pl.pallas_call(
        last_kernel,
        in_specs=[SMEM] + [VMEM] * 3,
        out_specs=ANYWHERE,
        out_shape=jax.ShapeDtypeStruct(near.shape, jnp.bfloat16),
        scratch_shapes=[pltpu.VMEM(near.shape, jnp.bfloat16), pltpu.SemaphoreType.DMA((2, width // WIDTH_CHUNK))],
        compiler_params=limits(4),
        name="last_sum",
    )(core, near, *arrived)


def together(*values):
    return lax.optimization_barrier(values)


def after(value, *others):
    return together(value, *others)[0] if others else value


def body(tokens, routes, gate_num, gate_up_q, gate_up_scale, down_q, down_scale):
    devices = lax.axis_size("expert")
    expert = lax.axis_index("expert")
    chips = devices // 2
    reach = chips // 2
    rows, width = tokens.shape
    half = rows // 2
    ring = ring_of(chips)

    def hop(shift, cross):
        pairs = []
        for place in range(chips):
            for core, way in ((0, shift), (1, -shift)):
                to = ring[(place + way) % chips]
                pairs.append((2 * ring[place] + core, 2 * to + (core ^ cross)))
        return pairs

    on, to_other, back_to_other = hop(1, 0), hop(-1, 1), hop(1, 1)
    swap = [(i, i ^ 1) for i in range(devices)]

    def send(x, perm, name):
        with jax.named_scope(name):
            return lax.ppermute(x, "expert", perm)

    lane = jnp.arange(LANES, dtype=jnp.int32)
    pick = jnp.where(lane == expert, 256.0, jnp.where(lane == devices + expert, 1.0, 0.0))
    pick = pick.astype(jnp.float32)[None, :]
    core = (expert & 1).astype(jnp.int32)[None]
    gate_up_w, down_w = keep(gate_up_q[0], down_q[0])
    weights = (pick, gate_up_w, gate_up_scale, down_w, down_scale)

    kept, given = {}, {}

    def run(items, tie, hint=2):
        halves = [after(blocks[item], *tie) for item in items]
        others = [send(x, swap, f"swap_in_{item[0]}") for x, item in zip(halves, items)]
        outs = expert_part([*others, *halves], [x.shape[0] for x in halves] * 2, hint, *weights)
        for number, (distance, name) in enumerate(items):
            kept[distance, name] = outs[number]
            given[distance, name] = send(outs[len(items) + number], swap, f"swap_out_{distance}")
        return outs[:1]

    own, own_for_other = pack(core, tokens, routes, gate_num, devices)
    other = send(own, swap, "swap_in_0")
    kept[0], cut = expert_part([own, other], (rows, rows), 2, *weights)
    given[0] = send(cut, swap, "swap_out_0")
    same, cross = send(own, on, "gather_long_1"), send(own_for_other, to_other, "gather_long_1")
    long, short = join(after(same, kept[0]), cross)
    blocks = {(1, "long"): long, (1, "short"): short}
    last = run([(1, "long"), (1, "short")], [kept[0]])
    for distance in range(2, reach):
        tie = last if distance > 2 else []
        long = send(after(long, *tie), on, f"gather_long_{distance}")
        short = send(after(short, *tie), on, f"gather_short_{distance}")
        blocks[distance, "long"], blocks[distance, "short"] = long, short
    blocks[reach, "long"] = send(long, on, f"gather_long_{reach}")

    def step(distance, name, carried):
        terms = [(x, 0) for x in (kept[distance, name], given[distance, name], *carried)]
        total = step_sum((rows, terms))
        return [send(total, on, f"return_{name}_{distance}")], [total]

    def arrive(name, carried):
        terms = (kept[1, name], given[1, name], *carried)
        totals = split_sum(*terms)
        return [send(x, perm, f"return_{name}_1") for x, perm in zip(totals, (back_to_other, on))], totals

    for distance in range(2, reach - 1):
        last = run([(distance, "short")], last)
    run([(reach - 1, "short")], last, 2)
    second = run([(reach - 1, "long")], last, 2)
    short, totals = step(reach - 1, "short", ())
    run([(reach, "long")], [*totals, *second])
    given[reach, "long"] = after(given[reach, "long"], *short)
    long, totals = step(reach, "long", ())
    for distance in range(reach - 1, 0, -1):
        if 1 < distance < reach - 1:
            run([(distance, "long")], [])
        if distance > 2:
            short, totals = step(distance - 1, "short", [after(x, *totals) for x in short])
        elif distance == 2:
            short, totals = arrive("short", [after(x, *totals) for x in short])
        if distance > 1:
            long, totals = step(distance, "long", [after(x, *totals) for x in long])
        else:
            short_cross, short_same = short
            near = near_sum(kept[0], given[0], short_same, short_cross)
            long, totals = arrive("long", [after(x, near) for x in long])
    long_cross, long_same = long
    return last_sum(core, near, long_cross, long_same)


def solution(mesh):
    in_specs = (
        P(("groups", "expert"), None),
        P(("groups", "expert"), None),
        P(("groups", "expert"), None),
        P("expert", None, None),
        P("expert", None),
        P("expert", None, None),
        P("expert", None),
    )
    out_specs = P(("groups", "expert"), None)
    return jax.shard_map(body, mesh=mesh, in_specs=in_specs, out_specs=out_specs, check_vma=False)
```

```python
import functools

import jax
import jax.numpy as jnp
from jax import lax
from jax.experimental import pallas as pl
from jax.experimental.pallas import tpu as pltpu
from jax.sharding import PartitionSpec as P

DENOMINATOR = 32768.0
LANES = 128
UNIT_CHUNK = 256
WIDTH_CHUNK = 1024
ANYWHERE = pl.BlockSpec(memory_space=pl.ANY)
VMEM = pl.BlockSpec(memory_space=pltpu.VMEM)
SMEM = pl.BlockSpec(memory_space=pltpu.SMEM)


def ring_of(chips):
    if chips == 8:
        return [0, 2, 4, 6, 7, 5, 3, 1]
    return list(range(chips))


def limits(mebibytes):
    return pltpu.CompilerParams(vmem_limit_bytes=mebibytes << 20)


def pack_kernel(experts, core, tokens, routes, gate_num, own, for_other, routes_here, gate_num_here, digits, sem):
    rows, width = tokens.shape
    half = rows // 2
    halves = []
    for packed, place in ((own, core[0]), (for_other, 1 - core[0])):
        for there, from_place in ((0, place), (half, 1 - place)):
            halves.append((packed, there, pl.ds(pl.multiple_of(from_place * half, half), half)))
    copies = [pltpu.make_async_copy(routes, routes_here, sem.at[0])]
    copies.append(pltpu.make_async_copy(gate_num, gate_num_here, sem.at[1]))
    for number, (packed, there, here) in enumerate(halves):
        target = packed.at[pl.ds(there, half), pl.ds(0, width)]
        copies.append(pltpu.make_async_copy(tokens.at[here], target, sem.at[2 + number]))
    for copy in copies:
        copy.start()
    for copy in copies[:2]:
        copy.wait()

    place = lax.broadcasted_iota(jnp.int32, (LANES, rows), 0)
    expert = jnp.where(place < experts, place, place - experts)
    dense = jnp.zeros((LANES, rows), jnp.int32)
    for pick in range(routes_here.shape[0]):
        choice = slice(pick, pick + 1)
        dense += jnp.where(routes_here[choice] == expert, gate_num_here[choice], 0)
    digit = jnp.where(place < experts, dense >> 8, dense & 255)
    digit = jnp.where(place < 2 * experts, digit, 0)
    digits[...] = digit.astype(jnp.float32).T.astype(jnp.bfloat16)
    for packed, there, here in halves:
        packed[there : there + half, width:] = digits[here]
    for copy in copies[2:]:
        copy.wait()


def pack(core, tokens, routes, gate_num, experts):
    rows, width = tokens.shape
    operands = [pltpu.with_memory_space_constraint(x, pltpu.HBM) for x in (tokens, routes.T, gate_num.T)]
    return pl.pallas_call(
        functools.partial(pack_kernel, experts),
        in_specs=[SMEM] + [ANYWHERE] * 3,
        out_specs=[VMEM] * 2,
        out_shape=[jax.ShapeDtypeStruct((rows, width + LANES), jnp.bfloat16)] * 2,
        scratch_shapes=[pltpu.VMEM(routes.T.shape, jnp.int32)] * 2
        + [pltpu.VMEM((rows, LANES), jnp.bfloat16), pltpu.SemaphoreType.DMA((6,))],
        compiler_params=limits(4),
        name="pack",
    )(core, *operands)


def keep_kernel(gate_up, down, gate_up_here, down_here, sem):
    copies = [
        pltpu.make_async_copy(gate_up, gate_up_here, sem.at[0]),
        pltpu.make_async_copy(down, down_here, sem.at[1]),
    ]
    for copy in copies:
        copy.start()
    for copy in copies:
        copy.wait()


def keep(gate_up_w, down_w):
    return pl.pallas_call(
        keep_kernel,
        in_specs=[ANYWHERE] * 2,
        out_specs=[VMEM] * 2,
        out_shape=[pltpu.VMEM(w.shape, w.dtype) for w in (gate_up_w, down_w)],
        scratch_shapes=[pltpu.SemaphoreType.DMA((2,))],
        compiler_params=limits(1),
        cost_estimate=pl.CostEstimate(
            flops=0, bytes_accessed=2 * (gate_up_w.size + down_w.size), transcendentals=0
        ),
        name="keep",
    )(*(pltpu.with_memory_space_constraint(w, pltpu.HBM) for w in (gate_up_w, down_w)))


def expert_kernel(count, *refs):
    xs = refs[:count]
    pick, gate_up_s, down_s, gate_up, down = refs[count : count + 5]
    outs = refs[count + 5 : -2]
    x, hidden = refs[-2:]
    units, width = down.shape

    at = 0
    for ref in xs:
        x[at : at + ref.shape[0]] = ref[...]
        at += ref.shape[0]
    digits = x[:, width:].astype(jnp.float32)
    weight = jnp.sum(digits * pick[...], axis=1, keepdims=True) / DENOMINATOR

    def unit_step(chunk, carry):
        sides = []
        for side in range(2):
            columns = pl.ds(pl.multiple_of(side * units + chunk * UNIT_CHUNK, UNIT_CHUNK), UNIT_CHUNK)
            part = jnp.dot(x[:, :width], gate_up[:, columns], preferred_element_type=jnp.float32)
            sides.append(part * gate_up_s[:, columns])
        here = pl.ds(pl.multiple_of(chunk * UNIT_CHUNK, UNIT_CHUNK), UNIT_CHUNK)
        hidden[:, here] = (jax.nn.silu(sides[0]) * sides[1]).astype(jnp.bfloat16)
        return carry

    lax.fori_loop(0, units // UNIT_CHUNK, unit_step, 0, unroll=True)

    def width_step(chunk, carry):
        columns = pl.ds(pl.multiple_of(chunk * WIDTH_CHUNK, WIDTH_CHUNK), WIDTH_CHUNK)
        part = jnp.dot(hidden[...], down[:, columns], preferred_element_type=jnp.float32)
        part = (part * down_s[:, columns] * weight).astype(jnp.bfloat16)
        at = 0
        for ref in outs:
            ref[:, columns] = part[at : at + ref.shape[0]]
            at += ref.shape[0]
        return carry

    lax.fori_loop(0, width // WIDTH_CHUNK, width_step, 0, unroll=True)


def expert_part(blocks, out_rows, hint, pick, gate_up_w, gate_up_s, down_w, down_s):
    width, units2 = gate_up_w.shape
    units = down_w.shape[0]
    rows, packed_width = sum(block.shape[0] for block in blocks), blocks[0].shape[1]
    flops = int(hint * 2 * rows * width * (units2 + units))
    return pl.pallas_call(
        functools.partial(expert_kernel, len(blocks)),
        in_specs=[VMEM] * (len(blocks) + 5),
        out_specs=[VMEM] * len(out_rows),
        out_shape=[jax.ShapeDtypeStruct((size, width), jnp.bfloat16) for size in out_rows],
        scratch_shapes=[
            pltpu.VMEM((rows, packed_width), jnp.bfloat16),
            pltpu.VMEM((rows, units), jnp.bfloat16),
        ],
        compiler_params=limits(14),
        cost_estimate=pl.CostEstimate(flops=flops, bytes_accessed=0, transcendentals=0),
        name="expert",
    )(
        *blocks,
        pick,
        gate_up_s,
        down_s,
        pltpu.with_memory_space_constraint(gate_up_w, pltpu.VMEM),
        pltpu.with_memory_space_constraint(down_w, pltpu.VMEM),
    )


def step_kernel(plan, *refs):
    *terms, out = refs
    for first, rows, places in plan:
        for column in range(0, out.shape[1], WIDTH_CHUNK):
            columns = slice(column, column + WIDTH_CHUNK)
            total = 0.0
            for number, start in places:
                total += terms[number][start : start + rows, columns].astype(jnp.float32)
            out[first : first + rows, columns] = total.astype(jnp.bfloat16)


def step_sum(*segments):
    arrays, plan, height = [], [], 0
    for rows, terms in segments:
        places = []
        for array, start in terms:
            number = next((i for i, known in enumerate(arrays) if known is array), len(arrays))
            if number == len(arrays):
                arrays.append(array)
            places.append((number, start))
        plan.append((height, rows, tuple(places)))
        height += rows
    return pl.pallas_call(
        functools.partial(step_kernel, tuple(plan)),
        in_specs=[VMEM] * len(arrays),
        out_specs=VMEM,
        out_shape=jax.ShapeDtypeStruct((height, arrays[0].shape[1]), jnp.bfloat16),
        compiler_params=limits(4),
        name="step_sum",
    )(*arrays)


def split_kernel(*refs):
    *terms, first, second = refs
    half = first.shape[0]
    for out, start in ((first, 0), (second, half)):
        for column in range(0, out.shape[1], WIDTH_CHUNK):
            columns = slice(column, column + WIDTH_CHUNK)
            total = 0.0
            for term in terms:
                total += term[start : start + half, columns].astype(jnp.float32)
            out[:, columns] = total.astype(jnp.bfloat16)


def split_sum(*terms):
    rows, width = terms[0].shape
    return pl.pallas_call(
        split_kernel,
        in_specs=[VMEM] * len(terms),
        out_specs=[VMEM] * 2,
        out_shape=[jax.ShapeDtypeStruct((rows // 2, width), jnp.bfloat16)] * 2,
        compiler_params=limits(4),
        name="split_sum",
    )(*terms)


def join_kernel(same, cross, long, short):
    half = same.shape[0] // 2
    for block, first in ((long, 0), (short, half)):
        block[:half] = same[first : first + half]
        block[half:] = cross[first : first + half]


def join(same, cross):
    return pl.pallas_call(
        join_kernel,
        in_specs=[VMEM] * 2,
        out_specs=[VMEM] * 2,
        out_shape=[jax.ShapeDtypeStruct(same.shape, same.dtype)] * 2,
        compiler_params=limits(2),
        name="join",
    )(same, cross)


def near_kernel(mine, theirs, short_same, short_cross, out):
    half = out.shape[0] // 2
    for which, arrived in enumerate((short_same, short_cross)):
        here = slice(which * half, (which + 1) * half)
        for column in range(0, out.shape[1], WIDTH_CHUNK):
            columns = slice(column, column + WIDTH_CHUNK)
            total = mine[here, columns].astype(jnp.float32) + theirs[here, columns].astype(jnp.float32)
            out[here, columns] = total + arrived[:, columns].astype(jnp.float32)


def near_sum(*terms):
    return pl.pallas_call(
        near_kernel,
        in_specs=[VMEM] * 4,
        out_specs=VMEM,
        out_shape=jax.ShapeDtypeStruct(terms[0].shape, jnp.float32),
        compiler_params=limits(4),
        cost_estimate=pl.CostEstimate(flops=10_000_000_000, bytes_accessed=0, transcendentals=0),
        name="near_sum",
    )(*terms)


def last_kernel(core, near, long_cross, long_same, out, here, sem):
    half = out.shape[0] // 2
    copies = []
    for which, arrived in enumerate((long_cross, long_same)):
        place = core[0] if which == 0 else 1 - core[0]
        there = pl.ds(pl.multiple_of(place * half, half), half)
        from_rows = slice(which * half, (which + 1) * half)
        for chunk in range(0, out.shape[1] // WIDTH_CHUNK):
            columns = slice(chunk * WIDTH_CHUNK, (chunk + 1) * WIDTH_CHUNK)
            total = near[from_rows, columns] + arrived[:, columns].astype(jnp.float32)
            here[from_rows, columns] = total.astype(jnp.bfloat16)
            source = here.at[pl.ds(which * half, half), pl.ds(chunk * WIDTH_CHUNK, WIDTH_CHUNK)]
            target = out.at[there, pl.ds(chunk * WIDTH_CHUNK, WIDTH_CHUNK)]
            copies.append(pltpu.make_async_copy(source, target, sem.at[which, chunk]))
            copies[-1].start()
    for copy in copies:
        copy.wait()


def last_sum(core, near, *arrived):
    rows, width = near.shape
    return pl.pallas_call(
        last_kernel,
        in_specs=[SMEM] + [VMEM] * 3,
        out_specs=ANYWHERE,
        out_shape=jax.ShapeDtypeStruct(near.shape, jnp.bfloat16),
        scratch_shapes=[pltpu.VMEM(near.shape, jnp.bfloat16), pltpu.SemaphoreType.DMA((2, width // WIDTH_CHUNK))],
        compiler_params=limits(4),
        name="last_sum",
    )(core, near, *arrived)


def together(*values):
    return lax.optimization_barrier(values)


def after(value, *others):
    return together(value, *others)[0] if others else value


def body(tokens, routes, gate_num, gate_up_q, gate_up_scale, down_q, down_scale):
    devices = lax.axis_size("expert")
    expert = lax.axis_index("expert")
    chips = devices // 2
    reach = chips // 2
    rows, width = tokens.shape
    half = rows // 2
    ring = ring_of(chips)

    def hop(shift, cross):
        pairs = []
        for place in range(chips):
            for core, way in ((0, shift), (1, -shift)):
                to = ring[(place + way) % chips]
                pairs.append((2 * ring[place] + core, 2 * to + (core ^ cross)))
        return pairs

    on, to_other, back_to_other = hop(1, 0), hop(-1, 1), hop(1, 1)
    swap = [(i, i ^ 1) for i in range(devices)]

    def send(x, perm, name):
        with jax.named_scope(name):
            return lax.ppermute(x, "expert", perm)

    lane = jnp.arange(LANES, dtype=jnp.int32)
    pick = jnp.where(lane == expert, 256.0, jnp.where(lane == devices + expert, 1.0, 0.0))
    pick = pick.astype(jnp.float32)[None, :]
    core = (expert & 1).astype(jnp.int32)[None]
    gate_up_w, down_w = keep(gate_up_q[0], down_q[0])
    weights = (pick, gate_up_w, gate_up_scale, down_w, down_scale)

    kept, given = {}, {}

    def run(items, tie, hint=2):
        halves = [after(blocks[item], *tie) for item in items]
        others = [send(x, swap, f"swap_in_{item[0]}") for x, item in zip(halves, items)]
        outs = expert_part([*others, *halves], [x.shape[0] for x in halves] * 2, hint, *weights)
        for number, (distance, name) in enumerate(items):
            kept[distance, name] = outs[number]
            given[distance, name] = send(outs[len(items) + number], swap, f"swap_out_{distance}")
        return outs[:1]

    own, own_for_other = pack(core, tokens, routes, gate_num, devices)
    other = send(own, swap, "swap_in_0")
    kept[0], cut = expert_part([own, other], (rows, rows), 2, *weights)
    given[0] = send(cut, swap, "swap_out_0")
    same, cross = send(own, on, "gather_long_1"), send(own_for_other, to_other, "gather_long_1")
    long, short = join(after(same, kept[0]), cross)
    blocks = {(1, "long"): long, (1, "short"): short}
    last = run([(1, "long"), (1, "short")], [kept[0]])
    for distance in range(2, reach):
        tie = last if distance > 2 else []
        long = send(after(long, *tie), on, f"gather_long_{distance}")
        short = send(after(short, *tie), on, f"gather_short_{distance}")
        blocks[distance, "long"], blocks[distance, "short"] = long, short
    blocks[reach, "long"] = send(long, on, f"gather_long_{reach}")

    def step(distance, name, carried):
        terms = [(x, 0) for x in (kept[distance, name], given[distance, name], *carried)]
        total = step_sum((rows, terms))
        return [send(total, on, f"return_{name}_{distance}")], [total]

    def arrive(name, carried):
        terms = (kept[1, name], given[1, name], *carried)
        totals = split_sum(*terms)
        return [send(x, perm, f"return_{name}_1") for x, perm in zip(totals, (back_to_other, on))], totals

    for distance in range(2, reach - 1):
        last = run([(distance, "short")], last)
    run([(reach - 1, "short")], last, 2)
    second = run([(reach - 1, "long")], last, 2)
    short, totals = step(reach - 1, "short", ())
    run([(reach, "long")], [*totals, *second])
    long, totals = step(reach, "long", ())
    for distance in range(reach - 1, 0, -1):
        if 1 < distance < reach - 1:
            run([(distance, "long")], [])
        if distance > 2:
            short, totals = step(distance - 1, "short", [after(x, *totals) for x in short])
        elif distance == 2:
            short, totals = arrive("short", [after(x, *totals) for x in short])
        if distance > 1:
            long, totals = step(distance, "long", [after(x, *totals) for x in long])
        else:
            short_cross, short_same = short
            near = near_sum(kept[0], given[0], short_same, short_cross)
            long, totals = arrive("long", [after(x, near) for x in long])
    long_cross, long_same = long
    return last_sum(core, near, long_cross, long_same)


def solution(mesh):
    in_specs = (
        P(("groups", "expert"), None),
        P(("groups", "expert"), None),
        P(("groups", "expert"), None),
        P("expert", None, None),
        P("expert", None),
        P("expert", None, None),
        P("expert", None),
    )
    out_specs = P(("groups", "expert"), None)
    return jax.shard_map(body, mesh=mesh, in_specs=in_specs, out_specs=out_specs, check_vma=False)
```

```python
import functools

import jax
import jax.numpy as jnp
from jax import lax
from jax.experimental import pallas as pl
from jax.experimental.pallas import tpu as pltpu
from jax.sharding import PartitionSpec as P

DENOMINATOR = 32768.0
LANES = 128
UNIT_CHUNK = 256
WIDTH_CHUNK = 1024
ANYWHERE = pl.BlockSpec(memory_space=pl.ANY)
VMEM = pl.BlockSpec(memory_space=pltpu.VMEM)
SMEM = pl.BlockSpec(memory_space=pltpu.SMEM)


def ring_of(chips):
    if chips == 8:
        return [0, 2, 4, 6, 7, 5, 3, 1]
    return list(range(chips))


def limits(mebibytes):
    return pltpu.CompilerParams(vmem_limit_bytes=mebibytes << 20)


def pack_kernel(experts, core, tokens, routes, gate_num, own, for_other, routes_here, gate_num_here, digits, sem):
    rows, width = tokens.shape
    half = rows // 2
    halves = []
    for packed, place in ((own, core[0]), (for_other, 1 - core[0])):
        for there, from_place in ((0, place), (half, 1 - place)):
            halves.append((packed, there, pl.ds(pl.multiple_of(from_place * half, half), half)))
    copies = [pltpu.make_async_copy(routes, routes_here, sem.at[0])]
    copies.append(pltpu.make_async_copy(gate_num, gate_num_here, sem.at[1]))
    for number, (packed, there, here) in enumerate(halves):
        target = packed.at[pl.ds(there, half), pl.ds(0, width)]
        copies.append(pltpu.make_async_copy(tokens.at[here], target, sem.at[2 + number]))
    for copy in copies:
        copy.start()
    for copy in copies[:2]:
        copy.wait()

    place = lax.broadcasted_iota(jnp.int32, (LANES, rows), 0)
    expert = jnp.where(place < experts, place, place - experts)
    dense = jnp.zeros((LANES, rows), jnp.int32)
    for pick in range(routes_here.shape[0]):
        choice = slice(pick, pick + 1)
        dense += jnp.where(routes_here[choice] == expert, gate_num_here[choice], 0)
    digit = jnp.where(place < experts, dense >> 8, dense & 255)
    digit = jnp.where(place < 2 * experts, digit, 0)
    digits[...] = digit.astype(jnp.float32).T.astype(jnp.bfloat16)
    for packed, there, here in halves:
        packed[there : there + half, width:] = digits[here]
    for copy in copies[2:]:
        copy.wait()


def pack(core, tokens, routes, gate_num, experts):
    rows, width = tokens.shape
    operands = [pltpu.with_memory_space_constraint(x, pltpu.HBM) for x in (tokens, routes.T, gate_num.T)]
    return pl.pallas_call(
        functools.partial(pack_kernel, experts),
        in_specs=[SMEM] + [ANYWHERE] * 3,
        out_specs=[VMEM] * 2,
        out_shape=[jax.ShapeDtypeStruct((rows, width + LANES), jnp.bfloat16)] * 2,
        scratch_shapes=[pltpu.VMEM(routes.T.shape, jnp.int32)] * 2
        + [pltpu.VMEM((rows, LANES), jnp.bfloat16), pltpu.SemaphoreType.DMA((6,))],
        compiler_params=limits(4),
        name="pack",
    )(core, *operands)


def keep_kernel(gate_up, down, gate_up_here, down_here, sem):
    copies = [
        pltpu.make_async_copy(gate_up, gate_up_here, sem.at[0]),
        pltpu.make_async_copy(down, down_here, sem.at[1]),
    ]
    for copy in copies:
        copy.start()
    for copy in copies:
        copy.wait()


def keep(gate_up_w, down_w):
    return pl.pallas_call(
        keep_kernel,
        in_specs=[ANYWHERE] * 2,
        out_specs=[VMEM] * 2,
        out_shape=[pltpu.VMEM(w.shape, w.dtype) for w in (gate_up_w, down_w)],
        scratch_shapes=[pltpu.SemaphoreType.DMA((2,))],
        compiler_params=limits(1),
        cost_estimate=pl.CostEstimate(
            flops=0, bytes_accessed=2 * (gate_up_w.size + down_w.size), transcendentals=0
        ),
        name="keep",
    )(*(pltpu.with_memory_space_constraint(w, pltpu.HBM) for w in (gate_up_w, down_w)))


def expert_kernel(count, *refs):
    xs = refs[:count]
    pick, gate_up_s, down_s, gate_up, down = refs[count : count + 5]
    outs = refs[count + 5 : -2]
    x, hidden = refs[-2:]
    units, width = down.shape

    at = 0
    for ref in xs:
        x[at : at + ref.shape[0]] = ref[...]
        at += ref.shape[0]
    digits = x[:, width:].astype(jnp.float32)
    weight = jnp.sum(digits * pick[...], axis=1, keepdims=True) / DENOMINATOR

    def unit_step(chunk, carry):
        sides = []
        for side in range(2):
            columns = pl.ds(pl.multiple_of(side * units + chunk * UNIT_CHUNK, UNIT_CHUNK), UNIT_CHUNK)
            part = jnp.dot(x[:, :width], gate_up[:, columns], preferred_element_type=jnp.float32)
            sides.append(part * gate_up_s[:, columns])
        here = pl.ds(pl.multiple_of(chunk * UNIT_CHUNK, UNIT_CHUNK), UNIT_CHUNK)
        hidden[:, here] = (jax.nn.silu(sides[0]) * sides[1]).astype(jnp.bfloat16)
        return carry

    lax.fori_loop(0, units // UNIT_CHUNK, unit_step, 0, unroll=True)

    def width_step(chunk, carry):
        columns = pl.ds(pl.multiple_of(chunk * WIDTH_CHUNK, WIDTH_CHUNK), WIDTH_CHUNK)
        part = jnp.dot(hidden[...], down[:, columns], preferred_element_type=jnp.float32)
        part = (part * down_s[:, columns] * weight).astype(jnp.bfloat16)
        at = 0
        for ref in outs:
            ref[:, columns] = part[at : at + ref.shape[0]]
            at += ref.shape[0]
        return carry

    lax.fori_loop(0, width // WIDTH_CHUNK, width_step, 0, unroll=True)


def expert_part(blocks, out_rows, hint, pick, gate_up_w, gate_up_s, down_w, down_s):
    width, units2 = gate_up_w.shape
    units = down_w.shape[0]
    rows, packed_width = sum(block.shape[0] for block in blocks), blocks[0].shape[1]
    flops = int(hint * 2 * rows * width * (units2 + units))
    return pl.pallas_call(
        functools.partial(expert_kernel, len(blocks)),
        in_specs=[VMEM] * (len(blocks) + 5),
        out_specs=[VMEM] * len(out_rows),
        out_shape=[jax.ShapeDtypeStruct((size, width), jnp.bfloat16) for size in out_rows],
        scratch_shapes=[
            pltpu.VMEM((rows, packed_width), jnp.bfloat16),
            pltpu.VMEM((rows, units), jnp.bfloat16),
        ],
        compiler_params=limits(14),
        cost_estimate=pl.CostEstimate(flops=flops, bytes_accessed=0, transcendentals=0),
        name="expert",
    )(
        *blocks,
        pick,
        gate_up_s,
        down_s,
        pltpu.with_memory_space_constraint(gate_up_w, pltpu.VMEM),
        pltpu.with_memory_space_constraint(down_w, pltpu.VMEM),
    )


def step_kernel(plan, *refs):
    *terms, out = refs
    for first, rows, places in plan:
        for column in range(0, out.shape[1], WIDTH_CHUNK):
            columns = slice(column, column + WIDTH_CHUNK)
            total = 0.0
            for number, start in places:
                total += terms[number][start : start + rows, columns].astype(jnp.float32)
            out[first : first + rows, columns] = total.astype(jnp.bfloat16)


def step_sum(*segments):
    arrays, plan, height = [], [], 0
    for rows, terms in segments:
        places = []
        for array, start in terms:
            number = next((i for i, known in enumerate(arrays) if known is array), len(arrays))
            if number == len(arrays):
                arrays.append(array)
            places.append((number, start))
        plan.append((height, rows, tuple(places)))
        height += rows
    return pl.pallas_call(
        functools.partial(step_kernel, tuple(plan)),
        in_specs=[VMEM] * len(arrays),
        out_specs=VMEM,
        out_shape=jax.ShapeDtypeStruct((height, arrays[0].shape[1]), jnp.bfloat16),
        compiler_params=limits(4),
        name="step_sum",
    )(*arrays)


def split_kernel(*refs):
    *terms, first, second = refs
    half = first.shape[0]
    for out, start in ((first, 0), (second, half)):
        for column in range(0, out.shape[1], WIDTH_CHUNK):
            columns = slice(column, column + WIDTH_CHUNK)
            total = 0.0
            for term in terms:
                total += term[start : start + half, columns].astype(jnp.float32)
            out[:, columns] = total.astype(jnp.bfloat16)


def split_sum(*terms):
    rows, width = terms[0].shape
    return pl.pallas_call(
        split_kernel,
        in_specs=[VMEM] * len(terms),
        out_specs=[VMEM] * 2,
        out_shape=[jax.ShapeDtypeStruct((rows // 2, width), jnp.bfloat16)] * 2,
        compiler_params=limits(4),
        name="split_sum",
    )(*terms)


def join_kernel(same, cross, long, short):
    half = same.shape[0] // 2
    for block, first in ((long, 0), (short, half)):
        block[:half] = same[first : first + half]
        block[half:] = cross[first : first + half]


def join(same, cross):
    return pl.pallas_call(
        join_kernel,
        in_specs=[VMEM] * 2,
        out_specs=[VMEM] * 2,
        out_shape=[jax.ShapeDtypeStruct(same.shape, same.dtype)] * 2,
        compiler_params=limits(2),
        name="join",
    )(same, cross)


def near_kernel(mine, theirs, short_same, short_cross, out):
    half = out.shape[0] // 2
    for which, arrived in enumerate((short_same, short_cross)):
        here = slice(which * half, (which + 1) * half)
        for column in range(0, out.shape[1], WIDTH_CHUNK):
            columns = slice(column, column + WIDTH_CHUNK)
            total = mine[here, columns].astype(jnp.float32) + theirs[here, columns].astype(jnp.float32)
            out[here, columns] = total + arrived[:, columns].astype(jnp.float32)


def near_sum(*terms):
    return pl.pallas_call(
        near_kernel,
        in_specs=[VMEM] * 4,
        out_specs=VMEM,
        out_shape=jax.ShapeDtypeStruct(terms[0].shape, jnp.float32),
        compiler_params=limits(4),
        cost_estimate=pl.CostEstimate(flops=10_000_000_000, bytes_accessed=0, transcendentals=0),
        name="near_sum",
    )(*terms)


def last_kernel(core, near, long_cross, long_same, out, here, sem):
    half = out.shape[0] // 2
    copies = []
    for which, arrived in enumerate((long_cross, long_same)):
        place = core[0] if which == 0 else 1 - core[0]
        there = pl.ds(pl.multiple_of(place * half, half), half)
        from_rows = slice(which * half, (which + 1) * half)
        for chunk in range(0, out.shape[1] // WIDTH_CHUNK):
            columns = slice(chunk * WIDTH_CHUNK, (chunk + 1) * WIDTH_CHUNK)
            total = near[from_rows, columns] + arrived[:, columns].astype(jnp.float32)
            here[from_rows, columns] = total.astype(jnp.bfloat16)
            source = here.at[pl.ds(which * half, half), pl.ds(chunk * WIDTH_CHUNK, WIDTH_CHUNK)]
            target = out.at[there, pl.ds(chunk * WIDTH_CHUNK, WIDTH_CHUNK)]
            copies.append(pltpu.make_async_copy(source, target, sem.at[which, chunk]))
            copies[-1].start()
    for copy in copies:
        copy.wait()


def last_sum(core, near, *arrived):
    rows, width = near.shape
    return pl.pallas_call(
        last_kernel,
        in_specs=[SMEM] + [VMEM] * 3,
        out_specs=ANYWHERE,
        out_shape=jax.ShapeDtypeStruct(near.shape, jnp.bfloat16),
        scratch_shapes=[pltpu.VMEM(near.shape, jnp.bfloat16), pltpu.SemaphoreType.DMA((2, width // WIDTH_CHUNK))],
        compiler_params=limits(4),
        name="last_sum",
    )(core, near, *arrived)


def together(*values):
    return lax.optimization_barrier(values)


def after(value, *others):
    return together(value, *others)[0] if others else value


def body(tokens, routes, gate_num, gate_up_q, gate_up_scale, down_q, down_scale):
    devices = lax.axis_size("expert")
    expert = lax.axis_index("expert")
    chips = devices // 2
    reach = chips // 2
    rows, width = tokens.shape
    half = rows // 2
    ring = ring_of(chips)

    def hop(shift, cross):
        pairs = []
        for place in range(chips):
            for core, way in ((0, shift), (1, -shift)):
                to = ring[(place + way) % chips]
                pairs.append((2 * ring[place] + core, 2 * to + (core ^ cross)))
        return pairs

    on, to_other, back_to_other = hop(1, 0), hop(-1, 1), hop(1, 1)
    swap = [(i, i ^ 1) for i in range(devices)]

    def send(x, perm, name):
        with jax.named_scope(name):
            return lax.ppermute(x, "expert", perm)

    lane = jnp.arange(LANES, dtype=jnp.int32)
    pick = jnp.where(lane == expert, 256.0, jnp.where(lane == devices + expert, 1.0, 0.0))
    pick = pick.astype(jnp.float32)[None, :]
    core = (expert & 1).astype(jnp.int32)[None]
    gate_up_w, down_w = keep(gate_up_q[0], down_q[0])
    weights = (pick, gate_up_w, gate_up_scale, down_w, down_scale)

    kept, given = {}, {}

    def run(items, tie, hint=2):
        halves = [after(blocks[item], *tie) for item in items]
        others = [send(x, swap, f"swap_in_{item[0]}") for x, item in zip(halves, items)]
        outs = expert_part([*others, *halves], [x.shape[0] for x in halves] * 2, hint, *weights)
        for number, (distance, name) in enumerate(items):
            kept[distance, name] = outs[number]
            given[distance, name] = send(outs[len(items) + number], swap, f"swap_out_{distance}")
        return outs[:1]

    own, own_for_other = pack(core, tokens, routes, gate_num, devices)
    other = send(own, swap, "swap_in_0")
    kept[0], cut = expert_part([own, other], (rows, rows), 2, *weights)
    given[0] = send(cut, swap, "swap_out_0")
    same, cross = send(own, on, "gather_long_1"), send(own_for_other, to_other, "gather_long_1")
    long, short = join(after(same, kept[0]), cross)
    blocks = {(1, "long"): long, (1, "short"): short}
    last = run([(1, "long"), (1, "short")], [kept[0]])
    for distance in range(2, reach):
        tie = last if distance > 2 else []
        long = send(after(long, *tie), on, f"gather_long_{distance}")
        short = send(after(short, *tie), on, f"gather_short_{distance}")
        blocks[distance, "long"], blocks[distance, "short"] = long, short
    blocks[reach, "long"] = send(long, on, f"gather_long_{reach}")

    def step(distance, name, carried):
        terms = [(x, 0) for x in (kept[distance, name], given[distance, name], *carried)]
        total = step_sum((rows, terms))
        return [send(total, on, f"return_{name}_{distance}")], [total]

    def arrive(name, carried):
        terms = (kept[1, name], given[1, name], *carried)
        totals = split_sum(*terms)
        return [send(x, perm, f"return_{name}_1") for x, perm in zip(totals, (back_to_other, on))], totals

    for distance in range(2, reach - 1):
        last = run([(distance, "short")], last)
    run([(reach - 1, "short")], last, 2)
    second = run([(reach - 1, "long")], last, 2)
    short, totals = step(reach - 1, "short", ())
    far = after(blocks[reach, "long"], *totals, *second)
    far_other = send(far, swap, f"swap_in_{reach}")
    far_given = expert_part([far], [rows], 2, *weights)
    given[reach, "long"] = send(far_given[0], swap, f"swap_out_{reach}")
    kept[reach, "long"] = expert_part([after(far_other, *far_given)], [rows], 2, *weights)[0]
    long, totals = step(reach, "long", ())
    for distance in range(reach - 1, 0, -1):
        if 1 < distance < reach - 1:
            run([(distance, "long")], [])
        if distance > 2:
            short, totals = step(distance - 1, "short", [after(x, *totals) for x in short])
        elif distance == 2:
            short, totals = arrive("short", [after(x, *totals) for x in short])
        if distance > 1:
            long, totals = step(distance, "long", [after(x, *totals) for x in long])
        else:
            short_cross, short_same = short
            near = near_sum(kept[0], given[0], short_same, short_cross)
            long, totals = arrive("long", [after(x, near) for x in long])
    long_cross, long_same = long
    return last_sum(core, near, long_cross, long_same)


def solution(mesh):
    in_specs = (
        P(("groups", "expert"), None),
        P(("groups", "expert"), None),
        P(("groups", "expert"), None),
        P("expert", None, None),
        P("expert", None),
        P("expert", None, None),
        P("expert", None),
    )
    out_specs = P(("groups", "expert"), None)
    return jax.shard_map(body, mesh=mesh, in_specs=in_specs, out_specs=out_specs, check_vma=False)
```

```python
import functools

import jax
import jax.numpy as jnp
from jax import lax
from jax.experimental import pallas as pl
from jax.experimental.pallas import tpu as pltpu
from jax.sharding import PartitionSpec as P

DENOMINATOR = 32768.0
LANES = 128
UNIT_CHUNK = 256
WIDTH_CHUNK = 1024
ANYWHERE = pl.BlockSpec(memory_space=pl.ANY)
VMEM = pl.BlockSpec(memory_space=pltpu.VMEM)
SMEM = pl.BlockSpec(memory_space=pltpu.SMEM)


def ring_of(chips):
    if chips == 8:
        return [0, 2, 4, 6, 7, 5, 3, 1]
    return list(range(chips))


def limits(mebibytes):
    return pltpu.CompilerParams(vmem_limit_bytes=mebibytes << 20)


def pack_kernel(experts, core, tokens, routes, gate_num, own, for_other, routes_here, gate_num_here, digits, sem):
    rows, width = tokens.shape
    half = rows // 2
    halves = []
    for packed, place in ((own, core[0]), (for_other, 1 - core[0])):
        for there, from_place in ((0, place), (half, 1 - place)):
            halves.append((packed, there, pl.ds(pl.multiple_of(from_place * half, half), half)))
    copies = [pltpu.make_async_copy(routes, routes_here, sem.at[0])]
    copies.append(pltpu.make_async_copy(gate_num, gate_num_here, sem.at[1]))
    for number, (packed, there, here) in enumerate(halves):
        target = packed.at[pl.ds(there, half), pl.ds(0, width)]
        copies.append(pltpu.make_async_copy(tokens.at[here], target, sem.at[2 + number]))
    for copy in copies:
        copy.start()
    for copy in copies[:2]:
        copy.wait()

    place = lax.broadcasted_iota(jnp.int32, (LANES, rows), 0)
    expert = jnp.where(place < experts, place, place - experts)
    dense = jnp.zeros((LANES, rows), jnp.int32)
    for pick in range(routes_here.shape[0]):
        choice = slice(pick, pick + 1)
        dense += jnp.where(routes_here[choice] == expert, gate_num_here[choice], 0)
    digit = jnp.where(place < experts, dense >> 8, dense & 255)
    digit = jnp.where(place < 2 * experts, digit, 0)
    digits[...] = digit.astype(jnp.float32).T.astype(jnp.bfloat16)
    for packed, there, here in halves:
        packed[there : there + half, width:] = digits[here]
    for copy in copies[2:]:
        copy.wait()


def pack(core, tokens, routes, gate_num, experts):
    rows, width = tokens.shape
    operands = [pltpu.with_memory_space_constraint(x, pltpu.HBM) for x in (tokens, routes.T, gate_num.T)]
    return pl.pallas_call(
        functools.partial(pack_kernel, experts),
        in_specs=[SMEM] + [ANYWHERE] * 3,
        out_specs=[VMEM] * 2,
        out_shape=[jax.ShapeDtypeStruct((rows, width + LANES), jnp.bfloat16)] * 2,
        scratch_shapes=[pltpu.VMEM(routes.T.shape, jnp.int32)] * 2
        + [pltpu.VMEM((rows, LANES), jnp.bfloat16), pltpu.SemaphoreType.DMA((6,))],
        compiler_params=limits(4),
        name="pack",
    )(core, *operands)


def keep_kernel(gate_up, down, gate_up_here, down_here, sem):
    copies = [
        pltpu.make_async_copy(gate_up, gate_up_here, sem.at[0]),
        pltpu.make_async_copy(down, down_here, sem.at[1]),
    ]
    for copy in copies:
        copy.start()
    for copy in copies:
        copy.wait()


def keep(gate_up_w, down_w):
    return pl.pallas_call(
        keep_kernel,
        in_specs=[ANYWHERE] * 2,
        out_specs=[VMEM] * 2,
        out_shape=[pltpu.VMEM(w.shape, w.dtype) for w in (gate_up_w, down_w)],
        scratch_shapes=[pltpu.SemaphoreType.DMA((2,))],
        compiler_params=limits(1),
        cost_estimate=pl.CostEstimate(
            flops=0, bytes_accessed=2 * (gate_up_w.size + down_w.size), transcendentals=0
        ),
        name="keep",
    )(*(pltpu.with_memory_space_constraint(w, pltpu.HBM) for w in (gate_up_w, down_w)))


def expert_kernel(count, *refs):
    xs = refs[:count]
    pick, gate_up_s, down_s, gate_up, down = refs[count : count + 5]
    outs = refs[count + 5 : -2]
    x, hidden = refs[-2:]
    units, width = down.shape

    at = 0
    for ref in xs:
        x[at : at + ref.shape[0]] = ref[...]
        at += ref.shape[0]
    digits = x[:, width:].astype(jnp.float32)
    weight = jnp.sum(digits * pick[...], axis=1, keepdims=True) / DENOMINATOR

    def unit_step(chunk, carry):
        sides = []
        for side in range(2):
            columns = pl.ds(pl.multiple_of(side * units + chunk * UNIT_CHUNK, UNIT_CHUNK), UNIT_CHUNK)
            part = jnp.dot(x[:, :width], gate_up[:, columns], preferred_element_type=jnp.float32)
            sides.append(part * gate_up_s[:, columns])
        here = pl.ds(pl.multiple_of(chunk * UNIT_CHUNK, UNIT_CHUNK), UNIT_CHUNK)
        hidden[:, here] = (jax.nn.silu(sides[0]) * sides[1]).astype(jnp.bfloat16)
        return carry

    lax.fori_loop(0, units // UNIT_CHUNK, unit_step, 0, unroll=True)

    def width_step(chunk, carry):
        columns = pl.ds(pl.multiple_of(chunk * WIDTH_CHUNK, WIDTH_CHUNK), WIDTH_CHUNK)
        part = jnp.dot(hidden[...], down[:, columns], preferred_element_type=jnp.float32)
        part = (part * down_s[:, columns] * weight).astype(jnp.bfloat16)
        at = 0
        for ref in outs:
            ref[:, columns] = part[at : at + ref.shape[0]]
            at += ref.shape[0]
        return carry

    lax.fori_loop(0, width // WIDTH_CHUNK, width_step, 0, unroll=True)


def expert_part(blocks, out_rows, hint, pick, gate_up_w, gate_up_s, down_w, down_s):
    width, units2 = gate_up_w.shape
    units = down_w.shape[0]
    rows, packed_width = sum(block.shape[0] for block in blocks), blocks[0].shape[1]
    flops = int(hint * 2 * rows * width * (units2 + units))
    return pl.pallas_call(
        functools.partial(expert_kernel, len(blocks)),
        in_specs=[VMEM] * (len(blocks) + 5),
        out_specs=[VMEM] * len(out_rows),
        out_shape=[jax.ShapeDtypeStruct((size, width), jnp.bfloat16) for size in out_rows],
        scratch_shapes=[
            pltpu.VMEM((rows, packed_width), jnp.bfloat16),
            pltpu.VMEM((rows, units), jnp.bfloat16),
        ],
        compiler_params=limits(14),
        cost_estimate=pl.CostEstimate(flops=flops, bytes_accessed=0, transcendentals=0),
        name="expert",
    )(
        *blocks,
        pick,
        gate_up_s,
        down_s,
        pltpu.with_memory_space_constraint(gate_up_w, pltpu.VMEM),
        pltpu.with_memory_space_constraint(down_w, pltpu.VMEM),
    )


def step_kernel(plan, *refs):
    *terms, out = refs
    for first, rows, places in plan:
        for column in range(0, out.shape[1], WIDTH_CHUNK):
            columns = slice(column, column + WIDTH_CHUNK)
            total = 0.0
            for number, start in places:
                total += terms[number][start : start + rows, columns].astype(jnp.float32)
            out[first : first + rows, columns] = total.astype(jnp.bfloat16)


def step_sum(*segments):
    arrays, plan, height = [], [], 0
    for rows, terms in segments:
        places = []
        for array, start in terms:
            number = next((i for i, known in enumerate(arrays) if known is array), len(arrays))
            if number == len(arrays):
                arrays.append(array)
            places.append((number, start))
        plan.append((height, rows, tuple(places)))
        height += rows
    return pl.pallas_call(
        functools.partial(step_kernel, tuple(plan)),
        in_specs=[VMEM] * len(arrays),
        out_specs=VMEM,
        out_shape=jax.ShapeDtypeStruct((height, arrays[0].shape[1]), jnp.bfloat16),
        compiler_params=limits(4),
        name="step_sum",
    )(*arrays)


def split_kernel(*refs):
    *terms, first, second = refs
    half = first.shape[0]
    for out, start in ((first, 0), (second, half)):
        for column in range(0, out.shape[1], WIDTH_CHUNK):
            columns = slice(column, column + WIDTH_CHUNK)
            total = 0.0
            for term in terms:
                total += term[start : start + half, columns].astype(jnp.float32)
            out[:, columns] = total.astype(jnp.bfloat16)


def split_sum(*terms):
    rows, width = terms[0].shape
    return pl.pallas_call(
        split_kernel,
        in_specs=[VMEM] * len(terms),
        out_specs=[VMEM] * 2,
        out_shape=[jax.ShapeDtypeStruct((rows // 2, width), jnp.bfloat16)] * 2,
        compiler_params=limits(4),
        name="split_sum",
    )(*terms)


def join_kernel(same, cross, long, short):
    half = same.shape[0] // 2
    for block, first in ((long, 0), (short, half)):
        block[:half] = same[first : first + half]
        block[half:] = cross[first : first + half]


def join(same, cross):
    return pl.pallas_call(
        join_kernel,
        in_specs=[VMEM] * 2,
        out_specs=[VMEM] * 2,
        out_shape=[jax.ShapeDtypeStruct(same.shape, same.dtype)] * 2,
        compiler_params=limits(2),
        name="join",
    )(same, cross)


def near_kernel(mine, theirs, short_same, short_cross, out):
    half = out.shape[0] // 2
    for which, arrived in enumerate((short_same, short_cross)):
        here = slice(which * half, (which + 1) * half)
        for column in range(0, out.shape[1], WIDTH_CHUNK):
            columns = slice(column, column + WIDTH_CHUNK)
            total = mine[here, columns].astype(jnp.float32) + theirs[here, columns].astype(jnp.float32)
            out[here, columns] = total + arrived[:, columns].astype(jnp.float32)


def near_sum(*terms):
    return pl.pallas_call(
        near_kernel,
        in_specs=[VMEM] * 4,
        out_specs=VMEM,
        out_shape=jax.ShapeDtypeStruct(terms[0].shape, jnp.float32),
        compiler_params=limits(4),
        cost_estimate=pl.CostEstimate(flops=10_000_000_000, bytes_accessed=0, transcendentals=0),
        name="near_sum",
    )(*terms)


def last_kernel(core, near, long_cross, long_same, out, here, sem):
    half = out.shape[0] // 2
    copies = []
    for which, arrived in enumerate((long_cross, long_same)):
        place = core[0] if which == 0 else 1 - core[0]
        there = pl.ds(pl.multiple_of(place * half, half), half)
        from_rows = slice(which * half, (which + 1) * half)
        for chunk in range(0, out.shape[1] // WIDTH_CHUNK):
            columns = slice(chunk * WIDTH_CHUNK, (chunk + 1) * WIDTH_CHUNK)
            total = near[from_rows, columns] + arrived[:, columns].astype(jnp.float32)
            here[from_rows, columns] = total.astype(jnp.bfloat16)
            source = here.at[pl.ds(which * half, half), pl.ds(chunk * WIDTH_CHUNK, WIDTH_CHUNK)]
            target = out.at[there, pl.ds(chunk * WIDTH_CHUNK, WIDTH_CHUNK)]
            copies.append(pltpu.make_async_copy(source, target, sem.at[which, chunk]))
            copies[-1].start()
    for copy in copies:
        copy.wait()


def last_sum(core, near, *arrived):
    rows, width = near.shape
    return pl.pallas_call(
        last_kernel,
        in_specs=[SMEM] + [VMEM] * 3,
        out_specs=ANYWHERE,
        out_shape=jax.ShapeDtypeStruct(near.shape, jnp.bfloat16),
        scratch_shapes=[pltpu.VMEM(near.shape, jnp.bfloat16), pltpu.SemaphoreType.DMA((2, width // WIDTH_CHUNK))],
        compiler_params=limits(4),
        name="last_sum",
    )(core, near, *arrived)


def together(*values):
    return lax.optimization_barrier(values)


def after(value, *others):
    return together(value, *others)[0] if others else value


def body(tokens, routes, gate_num, gate_up_q, gate_up_scale, down_q, down_scale):
    devices = lax.axis_size("expert")
    expert = lax.axis_index("expert")
    chips = devices // 2
    reach = chips // 2
    rows, width = tokens.shape
    half = rows // 2
    ring = ring_of(chips)

    def hop(shift, cross):
        pairs = []
        for place in range(chips):
            for core, way in ((0, shift), (1, -shift)):
                to = ring[(place + way) % chips]
                pairs.append((2 * ring[place] + core, 2 * to + (core ^ cross)))
        return pairs

    on, to_other, back_to_other = hop(1, 0), hop(-1, 1), hop(1, 1)
    swap = [(i, i ^ 1) for i in range(devices)]

    def send(x, perm, name):
        with jax.named_scope(name):
            return lax.ppermute(x, "expert", perm)

    lane = jnp.arange(LANES, dtype=jnp.int32)
    pick = jnp.where(lane == expert, 256.0, jnp.where(lane == devices + expert, 1.0, 0.0))
    pick = pick.astype(jnp.float32)[None, :]
    core = (expert & 1).astype(jnp.int32)[None]
    gate_up_w, down_w = keep(gate_up_q[0], down_q[0])
    weights = (pick, gate_up_w, gate_up_scale, down_w, down_scale)

    kept, given = {}, {}

    def run(items, tie, hint=2):
        halves = [after(blocks[item], *tie) for item in items]
        others = [send(x, swap, f"swap_in_{item[0]}") for x, item in zip(halves, items)]
        outs = expert_part([*others, *halves], [x.shape[0] for x in halves] * 2, hint, *weights)
        for number, (distance, name) in enumerate(items):
            kept[distance, name] = outs[number]
            given[distance, name] = send(outs[len(items) + number], swap, f"swap_out_{distance}")
        return outs[:1]

    own, own_for_other = pack(core, tokens, routes, gate_num, devices)
    other = send(own, swap, "swap_in_0")
    kept[0], cut = expert_part([own, other], (rows, rows), 2, *weights)
    given[0] = send(cut, swap, "swap_out_0")
    same, cross = send(own, on, "gather_long_1"), send(own_for_other, to_other, "gather_long_1")
    long, short = join(after(same, kept[0]), cross)
    blocks = {(1, "long"): long, (1, "short"): short}
    last = run([(1, "long"), (1, "short")], [kept[0]])
    for distance in range(2, reach):
        tie = last if distance > 2 else []
        long = send(after(long, *tie), on, f"gather_long_{distance}")
        short = send(after(short, *tie), on, f"gather_short_{distance}")
        blocks[distance, "long"], blocks[distance, "short"] = long, short
    blocks[reach, "long"] = send(long, on, f"gather_long_{reach}")

    def step(distance, name, carried):
        terms = [(x, 0) for x in (kept[distance, name], given[distance, name], *carried)]
        total = step_sum((rows, terms))
        return [send(total, on, f"return_{name}_{distance}")], [total]

    def arrive(name, carried):
        terms = (kept[1, name], given[1, name], *carried)
        totals = split_sum(*terms)
        return [send(x, perm, f"return_{name}_1") for x, perm in zip(totals, (back_to_other, on))], totals

    for distance in range(2, reach - 1):
        last = run([(distance, "short")], last)
    run([(reach - 1, "short")], last, 2)
    second = run([(reach - 1, "long")], last, 2)
    short, totals = step(reach - 1, "short", ())
    far = after(blocks[reach, "long"], *totals, *second)
    far_other = send(far, swap, f"swap_in_{reach}")
    far_given = expert_part([far], [rows], 2, *weights)
    given[reach, "long"] = send(far_given[0], swap, f"swap_out_{reach}")
    kept[reach, "long"] = expert_part([after(far_other, *far_given)], [rows], 2, *weights)[0]
    given[reach, "long"] = after(given[reach, "long"], *short)
    long, totals = step(reach, "long", ())
    for distance in range(reach - 1, 0, -1):
        if 1 < distance < reach - 1:
            run([(distance, "long")], [])
        if distance > 2:
            short, totals = step(distance - 1, "short", [after(x, *totals) for x in short])
        elif distance == 2:
            short, totals = arrive("short", [after(x, *totals) for x in short])
        if distance > 1:
            long, totals = step(distance, "long", [after(x, *totals) for x in long])
        else:
            short_cross, short_same = short
            near = near_sum(kept[0], given[0], short_same, short_cross)
            long, totals = arrive("long", [after(x, near) for x in long])
    long_cross, long_same = long
    return last_sum(core, near, long_cross, long_same)


def solution(mesh):
    in_specs = (
        P(("groups", "expert"), None),
        P(("groups", "expert"), None),
        P(("groups", "expert"), None),
        P("expert", None, None),
        P("expert", None),
        P("expert", None, None),
        P("expert", None),
    )
    out_specs = P(("groups", "expert"), None)
    return jax.shard_map(body, mesh=mesh, in_specs=in_specs, out_specs=out_specs, check_vma=False)
```

```python
import functools

import jax
import jax.numpy as jnp
from jax import lax
from jax.experimental import pallas as pl
from jax.experimental.pallas import tpu as pltpu
from jax.sharding import PartitionSpec as P

DENOMINATOR = 32768.0
LANES = 128
UNIT_CHUNK = 768
WIDTH_CHUNK = 1024
ANYWHERE = pl.BlockSpec(memory_space=pl.ANY)
VMEM = pl.BlockSpec(memory_space=pltpu.VMEM)
SMEM = pl.BlockSpec(memory_space=pltpu.SMEM)


def ring_of(chips):
    if chips == 8:
        return [0, 2, 4, 6, 7, 5, 3, 1]
    return list(range(chips))


def limits(mebibytes):
    return pltpu.CompilerParams(vmem_limit_bytes=mebibytes << 20)


def pack_kernel(experts, core, tokens, routes, gate_num, own, for_other, routes_here, gate_num_here, digits, sem):
    rows, width = tokens.shape
    half = rows // 2
    halves = []
    for packed, place in ((own, core[0]), (for_other, 1 - core[0])):
        for there, from_place in ((0, place), (half, 1 - place)):
            halves.append((packed, there, pl.ds(pl.multiple_of(from_place * half, half), half)))
    copies = [pltpu.make_async_copy(routes, routes_here, sem.at[0])]
    copies.append(pltpu.make_async_copy(gate_num, gate_num_here, sem.at[1]))
    for number, (packed, there, here) in enumerate(halves):
        target = packed.at[pl.ds(there, half), pl.ds(0, width)]
        copies.append(pltpu.make_async_copy(tokens.at[here], target, sem.at[2 + number]))
    for copy in copies:
        copy.start()
    for copy in copies[:2]:
        copy.wait()

    place = lax.broadcasted_iota(jnp.int32, (LANES, rows), 0)
    expert = jnp.where(place < experts, place, place - experts)
    dense = jnp.zeros((LANES, rows), jnp.int32)
    for pick in range(routes_here.shape[0]):
        choice = slice(pick, pick + 1)
        dense += jnp.where(routes_here[choice] == expert, gate_num_here[choice], 0)
    digit = jnp.where(place < experts, dense >> 8, dense & 255)
    digit = jnp.where(place < 2 * experts, digit, 0)
    digits[...] = digit.astype(jnp.float32).T.astype(jnp.bfloat16)
    for packed, there, here in halves:
        packed[there : there + half, width:] = digits[here]
    for copy in copies[2:]:
        copy.wait()


def pack(core, tokens, routes, gate_num, experts):
    rows, width = tokens.shape
    operands = [pltpu.with_memory_space_constraint(x, pltpu.HBM) for x in (tokens, routes.T, gate_num.T)]
    return pl.pallas_call(
        functools.partial(pack_kernel, experts),
        in_specs=[SMEM] + [ANYWHERE] * 3,
        out_specs=[VMEM] * 2,
        out_shape=[jax.ShapeDtypeStruct((rows, width + LANES), jnp.bfloat16)] * 2,
        scratch_shapes=[pltpu.VMEM(routes.T.shape, jnp.int32)] * 2
        + [pltpu.VMEM((rows, LANES), jnp.bfloat16), pltpu.SemaphoreType.DMA((6,))],
        compiler_params=limits(4),
        name="pack",
    )(core, *operands)


def keep_kernel(gate_up, down, gate_up_here, down_here, sem):
    copies = [
        pltpu.make_async_copy(gate_up, gate_up_here, sem.at[0]),
        pltpu.make_async_copy(down, down_here, sem.at[1]),
    ]
    for copy in copies:
        copy.start()
    for copy in copies:
        copy.wait()


def keep(gate_up_w, down_w):
    return pl.pallas_call(
        keep_kernel,
        in_specs=[ANYWHERE] * 2,
        out_specs=[VMEM] * 2,
        out_shape=[pltpu.VMEM(w.shape, w.dtype) for w in (gate_up_w, down_w)],
        scratch_shapes=[pltpu.SemaphoreType.DMA((2,))],
        compiler_params=limits(1),
        cost_estimate=pl.CostEstimate(
            flops=0, bytes_accessed=2 * (gate_up_w.size + down_w.size), transcendentals=0
        ),
        name="keep",
    )(*(pltpu.with_memory_space_constraint(w, pltpu.HBM) for w in (gate_up_w, down_w)))


def expert_kernel(count, *refs):
    xs = refs[:count]
    pick, gate_up_s, down_s, gate_up, down = refs[count : count + 5]
    outs = refs[count + 5 : -2]
    x, hidden = refs[-2:]
    units, width = down.shape

    at = 0
    for ref in xs:
        x[at : at + ref.shape[0]] = ref[...]
        at += ref.shape[0]
    digits = x[:, width:].astype(jnp.float32)
    weight = jnp.sum(digits * pick[...], axis=1, keepdims=True) / DENOMINATOR

    def unit_step(chunk, carry):
        sides = []
        for side in range(2):
            columns = pl.ds(pl.multiple_of(side * units + chunk * UNIT_CHUNK, UNIT_CHUNK), UNIT_CHUNK)
            part = jnp.dot(x[:, :width], gate_up[:, columns], preferred_element_type=jnp.float32)
            sides.append(part * gate_up_s[:, columns])
        here = pl.ds(pl.multiple_of(chunk * UNIT_CHUNK, UNIT_CHUNK), UNIT_CHUNK)
        hidden[:, here] = (jax.nn.silu(sides[0]) * sides[1]).astype(jnp.bfloat16)
        return carry

    lax.fori_loop(0, units // UNIT_CHUNK, unit_step, 0, unroll=True)

    def width_step(chunk, carry):
        columns = pl.ds(pl.multiple_of(chunk * WIDTH_CHUNK, WIDTH_CHUNK), WIDTH_CHUNK)
        part = jnp.dot(hidden[...], down[:, columns], preferred_element_type=jnp.float32)
        part = (part * down_s[:, columns] * weight).astype(jnp.bfloat16)
        at = 0
        for ref in outs:
            ref[:, columns] = part[at : at + ref.shape[0]]
            at += ref.shape[0]
        return carry

    lax.fori_loop(0, width // WIDTH_CHUNK, width_step, 0, unroll=True)


def expert_part(blocks, out_rows, hint, pick, gate_up_w, gate_up_s, down_w, down_s):
    width, units2 = gate_up_w.shape
    units = down_w.shape[0]
    rows, packed_width = sum(block.shape[0] for block in blocks), blocks[0].shape[1]
    flops = int(hint * 2 * rows * width * (units2 + units))
    return pl.pallas_call(
        functools.partial(expert_kernel, len(blocks)),
        in_specs=[VMEM] * (len(blocks) + 5),
        out_specs=[VMEM] * len(out_rows),
        out_shape=[jax.ShapeDtypeStruct((size, width), jnp.bfloat16) for size in out_rows],
        scratch_shapes=[
            pltpu.VMEM((rows, packed_width), jnp.bfloat16),
            pltpu.VMEM((rows, units), jnp.bfloat16),
        ],
        compiler_params=limits(14),
        cost_estimate=pl.CostEstimate(flops=flops, bytes_accessed=0, transcendentals=0),
        name="expert",
    )(
        *blocks,
        pick,
        gate_up_s,
        down_s,
        pltpu.with_memory_space_constraint(gate_up_w, pltpu.VMEM),
        pltpu.with_memory_space_constraint(down_w, pltpu.VMEM),
    )


def step_kernel(plan, *refs):
    *terms, out = refs
    for first, rows, places in plan:
        for column in range(0, out.shape[1], WIDTH_CHUNK):
            columns = slice(column, column + WIDTH_CHUNK)
            total = 0.0
            for number, start in places:
                total += terms[number][start : start + rows, columns].astype(jnp.float32)
            out[first : first + rows, columns] = total.astype(jnp.bfloat16)


def step_sum(*segments):
    arrays, plan, height = [], [], 0
    for rows, terms in segments:
        places = []
        for array, start in terms:
            number = next((i for i, known in enumerate(arrays) if known is array), len(arrays))
            if number == len(arrays):
                arrays.append(array)
            places.append((number, start))
        plan.append((height, rows, tuple(places)))
        height += rows
    return pl.pallas_call(
        functools.partial(step_kernel, tuple(plan)),
        in_specs=[VMEM] * len(arrays),
        out_specs=VMEM,
        out_shape=jax.ShapeDtypeStruct((height, arrays[0].shape[1]), jnp.bfloat16),
        compiler_params=limits(4),
        name="step_sum",
    )(*arrays)


def split_kernel(*refs):
    *terms, first, second = refs
    half = first.shape[0]
    for out, start in ((first, 0), (second, half)):
        for column in range(0, out.shape[1], WIDTH_CHUNK):
            columns = slice(column, column + WIDTH_CHUNK)
            total = 0.0
            for term in terms:
                total += term[start : start + half, columns].astype(jnp.float32)
            out[:, columns] = total.astype(jnp.bfloat16)


def split_sum(*terms):
    rows, width = terms[0].shape
    return pl.pallas_call(
        split_kernel,
        in_specs=[VMEM] * len(terms),
        out_specs=[VMEM] * 2,
        out_shape=[jax.ShapeDtypeStruct((rows // 2, width), jnp.bfloat16)] * 2,
        compiler_params=limits(4),
        name="split_sum",
    )(*terms)


def join_kernel(same, cross, long, short):
    half = same.shape[0] // 2
    for block, first in ((long, 0), (short, half)):
        block[:half] = same[first : first + half]
        block[half:] = cross[first : first + half]


def join(same, cross):
    return pl.pallas_call(
        join_kernel,
        in_specs=[VMEM] * 2,
        out_specs=[VMEM] * 2,
        out_shape=[jax.ShapeDtypeStruct(same.shape, same.dtype)] * 2,
        compiler_params=limits(2),
        name="join",
    )(same, cross)


def near_kernel(mine, theirs, short_same, short_cross, out):
    half = out.shape[0] // 2
    for which, arrived in enumerate((short_same, short_cross)):
        here = slice(which * half, (which + 1) * half)
        for column in range(0, out.shape[1], WIDTH_CHUNK):
            columns = slice(column, column + WIDTH_CHUNK)
            total = mine[here, columns].astype(jnp.float32) + theirs[here, columns].astype(jnp.float32)
            out[here, columns] = total + arrived[:, columns].astype(jnp.float32)


def near_sum(*terms):
    return pl.pallas_call(
        near_kernel,
        in_specs=[VMEM] * 4,
        out_specs=VMEM,
        out_shape=jax.ShapeDtypeStruct(terms[0].shape, jnp.float32),
        compiler_params=limits(4),
        cost_estimate=pl.CostEstimate(flops=10_000_000_000, bytes_accessed=0, transcendentals=0),
        name="near_sum",
    )(*terms)


def last_kernel(core, near, long_cross, long_same, out, here, sem):
    half = out.shape[0] // 2
    copies = []
    for which, arrived in enumerate((long_cross, long_same)):
        place = core[0] if which == 0 else 1 - core[0]
        there = pl.ds(pl.multiple_of(place * half, half), half)
        from_rows = slice(which * half, (which + 1) * half)
        for chunk in range(0, out.shape[1] // WIDTH_CHUNK):
            columns = slice(chunk * WIDTH_CHUNK, (chunk + 1) * WIDTH_CHUNK)
            total = near[from_rows, columns] + arrived[:, columns].astype(jnp.float32)
            here[from_rows, columns] = total.astype(jnp.bfloat16)
            source = here.at[pl.ds(which * half, half), pl.ds(chunk * WIDTH_CHUNK, WIDTH_CHUNK)]
            target = out.at[there, pl.ds(chunk * WIDTH_CHUNK, WIDTH_CHUNK)]
            copies.append(pltpu.make_async_copy(source, target, sem.at[which, chunk]))
            copies[-1].start()
    for copy in copies:
        copy.wait()


def last_sum(core, near, *arrived):
    rows, width = near.shape
    return pl.pallas_call(
        last_kernel,
        in_specs=[SMEM] + [VMEM] * 3,
        out_specs=ANYWHERE,
        out_shape=jax.ShapeDtypeStruct(near.shape, jnp.bfloat16),
        scratch_shapes=[pltpu.VMEM(near.shape, jnp.bfloat16), pltpu.SemaphoreType.DMA((2, width // WIDTH_CHUNK))],
        compiler_params=limits(4),
        name="last_sum",
    )(core, near, *arrived)


def together(*values):
    return lax.optimization_barrier(values)


def after(value, *others):
    return together(value, *others)[0] if others else value


def body(tokens, routes, gate_num, gate_up_q, gate_up_scale, down_q, down_scale):
    devices = lax.axis_size("expert")
    expert = lax.axis_index("expert")
    chips = devices // 2
    reach = chips // 2
    rows, width = tokens.shape
    half = rows // 2
    ring = ring_of(chips)

    def hop(shift, cross):
        pairs = []
        for place in range(chips):
            for core, way in ((0, shift), (1, -shift)):
                to = ring[(place + way) % chips]
                pairs.append((2 * ring[place] + core, 2 * to + (core ^ cross)))
        return pairs

    on, to_other, back_to_other = hop(1, 0), hop(-1, 1), hop(1, 1)
    swap = [(i, i ^ 1) for i in range(devices)]

    def send(x, perm, name):
        with jax.named_scope(name):
            return lax.ppermute(x, "expert", perm)

    lane = jnp.arange(LANES, dtype=jnp.int32)
    pick = jnp.where(lane == expert, 256.0, jnp.where(lane == devices + expert, 1.0, 0.0))
    pick = pick.astype(jnp.float32)[None, :]
    core = (expert & 1).astype(jnp.int32)[None]
    gate_up_w, down_w = keep(gate_up_q[0], down_q[0])
    weights = (pick, gate_up_w, gate_up_scale, down_w, down_scale)

    kept, given = {}, {}

    def run(items, tie, hint=2):
        halves = [after(blocks[item], *tie) for item in items]
        others = [send(x, swap, f"swap_in_{item[0]}") for x, item in zip(halves, items)]
        outs = expert_part([*others, *halves], [x.shape[0] for x in halves] * 2, hint, *weights)
        for number, (distance, name) in enumerate(items):
            kept[distance, name] = outs[number]
            given[distance, name] = send(outs[len(items) + number], swap, f"swap_out_{distance}")
        return outs[:1]

    own, own_for_other = pack(core, tokens, routes, gate_num, devices)
    other = send(own, swap, "swap_in_0")
    kept[0], cut = expert_part([own, other], (rows, rows), 2, *weights)
    given[0] = send(cut, swap, "swap_out_0")
    same, cross = send(own, on, "gather_long_1"), send(own_for_other, to_other, "gather_long_1")
    long, short = join(after(same, kept[0]), cross)
    blocks = {(1, "long"): long, (1, "short"): short}
    last = run([(1, "long"), (1, "short")], [kept[0]])
    for distance in range(2, reach):
        tie = last if distance > 2 else []
        long = send(after(long, *tie), on, f"gather_long_{distance}")
        short = send(after(short, *tie), on, f"gather_short_{distance}")
        blocks[distance, "long"], blocks[distance, "short"] = long, short
    blocks[reach, "long"] = send(long, on, f"gather_long_{reach}")

    def step(distance, name, carried):
        terms = [(x, 0) for x in (kept[distance, name], given[distance, name], *carried)]
        total = step_sum((rows, terms))
        return [send(total, on, f"return_{name}_{distance}")], [total]

    def arrive(name, carried):
        terms = (kept[1, name], given[1, name], *carried)
        totals = split_sum(*terms)
        return [send(x, perm, f"return_{name}_1") for x, perm in zip(totals, (back_to_other, on))], totals

    for distance in range(2, reach - 1):
        last = run([(distance, "short")], last)
    run([(reach - 1, "short")], last, 2)
    second = run([(reach - 1, "long")], last, 2)
    short, totals = step(reach - 1, "short", ())
    run([(reach, "long")], [*totals, *second])
    given[reach, "long"] = after(given[reach, "long"], *short)
    long, totals = step(reach, "long", ())
    for distance in range(reach - 1, 0, -1):
        if 1 < distance < reach - 1:
            run([(distance, "long")], [])
        if distance > 2:
            short, totals = step(distance - 1, "short", [after(x, *totals) for x in short])
        elif distance == 2:
            short, totals = arrive("short", [after(x, *totals) for x in short])
        if distance > 1:
            long, totals = step(distance, "long", [after(x, *totals) for x in long])
        else:
            short_cross, short_same = short
            near = near_sum(kept[0], given[0], short_same, short_cross)
            long, totals = arrive("long", [after(x, near) for x in long])
    long_cross, long_same = long
    return last_sum(core, near, long_cross, long_same)


def solution(mesh):
    in_specs = (
        P(("groups", "expert"), None),
        P(("groups", "expert"), None),
        P(("groups", "expert"), None),
        P("expert", None, None),
        P("expert", None),
        P("expert", None, None),
        P("expert", None),
    )
    out_specs = P(("groups", "expert"), None)
    return jax.shard_map(body, mesh=mesh, in_specs=in_specs, out_specs=out_specs, check_vma=False)
```
